32 devices in a mesh: expert: 8 (over y, x, core), dp: 4 (over z).
Axes of the slice: x: 2, y: 2, z: 4, core: 2. Of those that a mesh axis runs over, the one named last changes fastest.
Arguments:
- attn_input: bfloat16 [3072, 4096], P('dp'), may hold values from -6 to 6
- query_grad: bfloat16 [3072, 8192], P('dp', 'expert'), may hold values from -6 to 6
- query_weight: float32 [8192, 4096], P(('expert', 'dp')), may hold values from -40 to 40
- moe_cotangent: bfloat16 [1024, 4096], P('expert', 'dp'), may hold values from -6 to 6
- expert_ids: int32 [1024, 8], P('expert'), may hold values from 0 to 15, all different within a row; in each aligned block of 128 rows (0 to 127, 128 to 255, ...) at most 80 rows name the same one
- route_weights: float32 [1024, 8], P('expert'), may hold values from 0.2 to 1
- gate_saved: bfloat16 [640, 16, 1536], P('dp', 'expert'), may hold values from -6 to 6
- up_saved: bfloat16 [640, 16, 1536], P('dp', 'expert'), may hold values from -6 to 6
- gate_weight: bfloat16 [16, 4096, 1536], P('expert', 'dp'), may hold values from -0.09375 to 0.09375
- up_weight: bfloat16 [16, 4096, 1536], P('expert', 'dp'), may hold values from -0.09375 to 0.09375
- down_weight: bfloat16 [16, 1536, 4096], P('expert', None, 'dp'), may hold values from -0.15625 to 0.15625
Outputs:
- query_weight_next: float32 [8192, 4096], P(('expert', 'dp'))
- moe_input_grad: float32 [1024, 4096], P('expert', 'dp')
The draws below stay inside these ranges and needn't reach their ends.
Inputs may be any that keep to these rules, and one draw needn't show every extreme that they name: `expert_ids`: in each aligned block of 128 rows no expert is named by more than 80 rows, and one expert by exactly 80 rows in some block; each row names 8 different experts.
All inputs are finite; a program needn't handle non-finite values.
Results may differ from the reference program's by a relative error of at most 0.022.
Values may be sent and summed in bfloat16 or wider, within the bound.
No kernel may reach another device: no remote copies, remote signals or barrier semaphores. Data moves between devices by JAX's collectives and lax.ppermute only.
A program may use at most 128 MiB of HBM per device.

```python
import math
import jax
import jax.numpy as jnp
import numpy as np
from jax import lax

D = 4096
FF = 1536
TOPK = 8
TOK_ATT = 768
TOK_MOE = 128
EXPERTS = 16
CAP = 80
SLOTS = 640
QCOLS = 8192
TOKENS_ATT = 3072
MOE_ROWS = 1024
N_EXPERT = 8
N_DP = 4


def draw_query_weight(key, part):
    first_key = jax.random.fold_in(key, 11)
    row_key = jax.random.fold_in(key, 12)
    column_key = jax.random.fold_in(key, 13)
    base = jnp.clip(jax.random.normal(first_key, (QCOLS, D), jnp.float32), -4.0, 4.0)
    row_scale = jnp.exp(jax.random.uniform(row_key, (QCOLS, 1), jnp.float32, 0.0, math.log(10.0)))
    column_scale = jnp.exp(jax.random.uniform(column_key, (1, D), jnp.float32, 0.0, math.log(10.0)))
    return base * row_scale * column_scale * 0.1


def strengthened(entries, stream_key, source, target, shards_of, factor):
    owner, partner = [(jnp.arange(entries.shape[dim]) // (entries.shape[dim] // shards_of)).reshape([-1 if axis == dim else 1 for axis in range(entries.ndim)]) for dim in (source, target)]
    chosen = jax.random.permutation(stream_key, shards_of)[partner]
    strong = (owner == chosen) | (owner == (partner + shards_of // 2) % shards_of)
    return jnp.where(strong, factor * entries, entries)


def level_of(key, dims, shards, low, top_value):
    def one(axis_at, parts):
        heights = jax.random.uniform(jax.random.fold_in(jax.random.fold_in(key, 6), axis_at), (parts,), jnp.float32, low / len(shards), top_value / len(shards))
        return jnp.repeat(jnp.exp(heights), dims[axis_at] // parts).reshape((-1,) + (1,) * (len(dims) - axis_at - 1))

    loudness = one(*shards[0])
    for cut in shards[1:]:
        loudness = loudness * one(*cut)
    return loudness


def routed_block(key, own, number, rows, count, top, limit, skew):
    ranking = jax.random.permutation(key, count)
    heavy_load, usual = portions_of(count, rows * top, limit, skew, True), portions_of(count, rows * top, limit, skew, False)
    places = jnp.arange(count)

    def named(sizes, rotation):
        used = int((sizes > 0).sum())
        fixed = max(1, used // 4)
        shifted = fixed + (places - fixed + rotation * (used - fixed)) % max(1, count - fixed)
        return jnp.zeros((count,), jnp.int32).at[ranking[jnp.where(places < fixed, places, shifted)]].set(jnp.asarray(sizes, jnp.int32))

    sizes = jnp.where(number % 4 == 0, named(heavy_load, number // 4), named(usual, number - number // 4 - 1))
    mixed = jax.random.permutation(jax.random.fold_in(own, 3), count)
    giver, taker = mixed[0:count // 2 * 2:2], mixed[1:count // 2 * 2:2]
    slack = jnp.minimum(sizes[giver] - 1, limit - sizes[taker]) // 2
    slack = jnp.where((giver == ranking[0]) | (taker == ranking[0]) | (sizes[taker] == 0), 0, jnp.maximum(slack, 0))
    shifted = jax.random.randint(jax.random.fold_in(own, 4), (count // 2,), 0, 1 << 20) % (slack + 1)
    sizes = sizes.at[giver].add(-shifted).at[taker].add(shifted)
    labels = jnp.searchsorted(jnp.cumsum(sizes), jnp.arange(rows * top), side="right").astype(jnp.int32)
    listing = labels.reshape(top, rows).T
    listing = listing[jax.random.permutation(jax.random.fold_in(own, 1), rows)]
    rotation = jax.random.randint(jax.random.fold_in(own, 2), (rows, 1), 0, top)
    return jnp.take_along_axis(listing, (jnp.arange(top)[None, :] + rotation) % top, axis=1)


def portions_of(count, total, reach, lean, full):
    loads = [(1 << 20) // math.isqrt(standing ** lean) + 1 for standing in range(1, count + 1)]
    largest = reach if full else min(reach, max(-(-total // count), total * loads[0] // sum(loads)))
    least = 1 if total - largest >= count - 1 else 0
    holding, rest = [largest] + [least] * (count - 1), total - largest - least * (count - 1)
    while rest > 0:
        movable = [i for i in range(1, count) if holding[i] < largest] or [i for i in range(1, count) if holding[i] < reach]
        pool, left = sum([loads[i] for i in movable]), rest
        for i in movable:
            addition = min(reach - holding[i], max(1, left * loads[i] // pool), rest)
            holding[i] = holding[i] + addition
            rest = rest - addition
    return np.array(holding)


def gaussian(key, extent, scale, bound, cuts=(), kind=jnp.bfloat16):
    level = level_of(key, extent, cuts, -0.22, 0.18) if cuts else 1.0
    entries = jax.random.normal(key, extent, jnp.float32) * scale * level
    return jnp.minimum(jnp.maximum(entries, -bound), bound).astype(kind)


def noise_with(own_key, dims, spread, bound, split, heavy, kind=jnp.bfloat16):
    array = spread * jax.random.normal(own_key, dims, jnp.float32)
    if split:
        array = array * level_of(own_key, dims, split, -0.22, 0.18)
    return jnp.clip(strengthened(array, jax.random.fold_in(own_key, 3), *heavy), -bound, bound).astype(kind)


def setup_inputs(seed: int = 0) -> dict:
    key_list = jax.random.split(jax.random.key(seed), 12)
    attn_input = gaussian(key_list[0], (TOKENS_ATT, D), 1.0, 6.0, ((0, 4),))
    query_grad = noise_with(key_list[1], (TOKENS_ATT, QCOLS), 1.0, 6.0, ((0, 4), (1, 8)), (0, 1, 8, 2.0))
    query_weight = draw_query_weight(jax.random.fold_in(key_list[11], 71), 0)
    moe_cotangent = gaussian(key_list[3], (MOE_ROWS, D), 1.0, 6.0, ((0, 8), (1, 4)))
    expert_ids_keys = jax.random.split(jax.random.fold_in(key_list[4], 1), MOE_ROWS // TOK_MOE)
    expert_ids_turns = jax.random.permutation(jax.random.fold_in(key_list[4], 3), MOE_ROWS // TOK_MOE)
    expert_ids = jax.vmap(lambda own, number: routed_block(jax.random.fold_in(key_list[4], 2), own, number, TOK_MOE, EXPERTS, TOPK, CAP, 1))(expert_ids_keys, expert_ids_turns).reshape((MOE_ROWS, TOPK))
    route_weights = jnp.clip(0.2 + 0.8 * jax.random.uniform(key_list[5], (MOE_ROWS, TOPK), jnp.float32) ** level_of(key_list[5], (MOE_ROWS, TOPK), ((0, 8),), -0.2, 0.2), 0.2, 1.0)
    gate_saved = gaussian(key_list[6], (SLOTS, EXPERTS, FF), 1.0, 6.0, ((0, 4), (1, 8)))
    up_saved = gaussian(key_list[7], (SLOTS, EXPERTS, FF), 1.0, 6.0, ((0, 4), (1, 8)))
    gate_weight = gaussian(key_list[8], (EXPERTS, D, FF), D ** -0.5, 0.09375, ((0, 8), (1, 4)))
    up_weight = gaussian(key_list[9], (EXPERTS, D, FF), D ** -0.5, 0.09375, ((0, 8), (1, 4)))
    down_weight = gaussian(key_list[10], (EXPERTS, FF, D), FF ** -0.5, 0.15625, ((0, 8), (2, 4)))
    return dict(attn_input=attn_input, query_grad=query_grad, query_weight=query_weight, moe_cotangent=moe_cotangent, expert_ids=expert_ids, route_weights=route_weights, gate_saved=gate_saved, up_saved=up_saved, gate_weight=gate_weight, up_weight=up_weight, down_weight=down_weight)


step_rate = 0.01
epsilon = 1e-06

def slot_tables(expert_ids, route_weights, experts, capacity):
    expert_iota = lax.broadcasted_iota(jnp.int32, (1, 1, experts), 2)
    chosen = (expert_ids[:, :, None] == expert_iota).astype(jnp.int32)
    counts = lax.optimization_barrier(jnp.sum(chosen, axis=1, dtype=jnp.int32))
    before = jnp.cumsum(counts, axis=0, dtype=jnp.int32) - counts
    position = lax.optimization_barrier(jnp.sum(chosen * before[:, None, :], axis=2, dtype=jnp.int32))
    slot_code = position * experts + expert_ids
    slot_iota = lax.broadcasted_iota(jnp.int32, (1, 1, capacity * experts), 2)
    matched = slot_code[:, :, None] == slot_iota
    select = lax.optimization_barrier(jnp.sum(matched.astype(route_weights.dtype), axis=1))
    scaled = lax.optimization_barrier(jnp.sum(jnp.where(matched, route_weights[:, :, None], 0.0), axis=1))
    return (select, scaled)

def activation_grads(hidden, gate_vals, up_vals):
    gate_float = gate_vals.astype(jnp.float32)
    up_float = up_vals.astype(jnp.float32)
    sigmoid_vals = jax.nn.sigmoid(gate_float)
    gate_grad = hidden * up_float * sigmoid_vals * (1.0 + gate_float * (1.0 - sigmoid_vals))
    up_grad = hidden * gate_float * sigmoid_vals
    return (gate_grad.astype(jnp.bfloat16), up_grad.astype(jnp.bfloat16))

def expert_backward(operands):
    slot_rows, gate_vals, up_vals, gate_w, up_w, down_w = operands
    width = slot_rows.shape[1]
    split_rows = slot_rows.reshape(SLOTS, N_DP, width // N_DP).astype(jnp.float32)
    split_down = down_w.reshape(FF, N_DP, width // N_DP).astype(jnp.float32)
    partial_sums = jnp.einsum('snc,hnc->nsh', split_rows, split_down)
    rounded = lax.optimization_barrier(partial_sums.astype(jnp.bfloat16))
    hidden = lax.optimization_barrier(jnp.sum(rounded.astype(jnp.float32), axis=0))
    gate_grad, up_grad = activation_grads(hidden, gate_vals, up_vals)
    total = jnp.dot(gate_grad, gate_w.T, preferred_element_type=jnp.float32)
    total = total + jnp.dot(up_grad, up_w.T, preferred_element_type=jnp.float32)
    return total.astype(jnp.bfloat16)

def reference(attn_input, query_grad, query_weight, moe_cotangent, expert_ids, route_weights, gate_saved, up_saved, gate_weight, up_weight, down_weight):
    batches = (attn_input.reshape(N_DP, TOK_ATT, D), query_grad.reshape(N_DP, TOK_ATT, QCOLS))

    def add_batch(total, pair):
        inputs, grads = pair
        term = lax.dot_general(grads, inputs, (((0,), (0,)), ((), ())), preferred_element_type=jnp.float32)
        rounded = lax.optimization_barrier(term.astype(jnp.bfloat16))
        return (total + rounded.astype(jnp.float32), None)
    gradient, unused = lax.scan(add_batch, jnp.zeros((QCOLS, D), jnp.float32), batches)
    radial = lax.optimization_barrier(jnp.mean(query_weight * gradient, axis=1, keepdims=True)) / (lax.optimization_barrier(jnp.mean(query_weight * query_weight, axis=1, keepdims=True)) + epsilon)
    stepped = query_weight - step_rate * (gradient - radial * query_weight)
    query_weight_next = stepped * lax.rsqrt(lax.optimization_barrier(jnp.mean(stepped * stepped, axis=1, keepdims=True)) + epsilon)
    block_ids = expert_ids.reshape(N_EXPERT, TOK_MOE, TOPK)
    block_weights = route_weights.reshape(N_EXPERT, TOK_MOE, TOPK)
    block_rows = moe_cotangent.reshape(N_EXPERT, TOK_MOE, D)

    def dispatch(operands):
        ids_block, weights_block, rows_block = operands
        select, scaled = slot_tables(ids_block, weights_block, EXPERTS, CAP)
        sent = jnp.dot(scaled.T, rows_block.astype(jnp.float32), precision=lax.Precision.HIGHEST, preferred_element_type=jnp.float32)
        return (sent.astype(jnp.bfloat16), select.astype(jnp.bfloat16))
    sent, selects = lax.map(dispatch, (block_ids, block_weights, block_rows))
    per_expert = jnp.transpose(sent.reshape(N_EXPERT, CAP, EXPERTS, D), (2, 0, 1, 3)).reshape(EXPERTS, SLOTS, D)
    slot_grads = lax.map(expert_backward, (per_expert, jnp.transpose(gate_saved, (1, 0, 2)), jnp.transpose(up_saved, (1, 0, 2)), gate_weight, up_weight, down_weight))
    by_source = jnp.transpose(slot_grads.reshape(EXPERTS, N_EXPERT, CAP, D), (1, 2, 0, 3)).reshape(N_EXPERT, CAP * EXPERTS, D)

    def combine(operands):
        select, flat_rows = operands
        return jnp.dot(select, flat_rows, preferred_element_type=jnp.float32)
    moe_input_grad = lax.map(combine, (selects, by_source)).reshape(N_EXPERT * TOK_MOE, D)
    return (query_weight_next, moe_input_grad)
```

```python
import jax
import jax.numpy as jnp
from jax import lax
from jax.sharding import PartitionSpec as P

step_rate = 0.01
epsilon = 1e-06


def shift(value, n, hops, first, last):
    return lax.ppermute(value, "dp", [(i, i + hops) for i in range(first, last + 1) if 0 <= i + hops < n])


def ordered(z, lefts, rights):
    near = jnp.where(z <= 1, rights[0], lefts[0])
    middle = jnp.where(z == 0, rights[1], jnp.where(z == 1, lefts[0], jnp.where(z == 2, rights[0], lefts[1])))
    far = jnp.where(z == 0, rights[2], jnp.where(z == 1, rights[1], jnp.where(z == 2, lefts[1], lefts[2])))
    return near, middle, far


def ordered_sources(z):
    near = jnp.where(z <= 1, z + 1, z - 1)
    middle = jnp.where(z == 0, 2, jnp.where(z == 1, 0, jnp.where(z == 2, 3, 1)))
    far = jnp.where(z <= 1, 3, 0)
    return near, middle, far


def line_gather(value, n):
    lefts, rights = [], []
    from_left, from_right = value, value
    for step in range(n - 1):
        from_left = shift(from_left, n, 1, step, n - 2)
        from_right = shift(from_right, n, -1, 1, n - 1 - step)
        lefts.append(from_left)
        rights.append(from_right)
    return lefts, rights


def line_reduce_scatter(parts, n, z):
    def block(index):
        return lax.dynamic_index_in_dim(parts, jnp.clip(index, 0, n - 1), 0, keepdims=False)

    from_left = from_right = None
    for step in range(1, n):
        up = block(z + n - step)
        down = block(z - n + step)
        if from_left is not None:
            up = up + from_left.astype(jnp.float32)
            down = down + from_right.astype(jnp.float32)
        from_left = shift(up.astype(jnp.bfloat16), n, 1, 0, step - 1)
        from_right = shift(down.astype(jnp.bfloat16), n, -1, n - step, n - 1)
    return block(z) + from_left.astype(jnp.float32) + from_right.astype(jnp.float32)


def activation_grads(hidden, gate_vals, up_vals):
    gate_float = gate_vals.astype(jnp.float32)
    up_float = up_vals.astype(jnp.float32)
    sigmoid_vals = jax.nn.sigmoid(gate_float)
    gate_grad = hidden * up_float * sigmoid_vals * (1.0 + gate_float * (1.0 - sigmoid_vals))
    up_grad = hidden * gate_float * sigmoid_vals
    return jnp.stack([gate_grad, up_grad], axis=0).astype(jnp.bfloat16)


def row_update(query_weight, gradient):
    radial = jnp.mean(query_weight * gradient, axis=1, keepdims=True) / (
        jnp.mean(query_weight * query_weight, axis=1, keepdims=True) + epsilon
    )
    stepped = query_weight - step_rate * (gradient - radial * query_weight)
    return stepped * lax.rsqrt(jnp.mean(stepped * stepped, axis=1, keepdims=True) + epsilon)


def token_product(grads, inputs):
    return lax.dot_general(grads, inputs, (((0,), (0,)), ((), ())), preferred_element_type=jnp.float32)


def weight_update_scattered(attn_input, query_grad, query_weight):
    gradient = lax.psum_scatter(
        token_product(query_grad, attn_input).astype(jnp.bfloat16), "dp", scatter_dimension=0, tiled=True
    ).astype(jnp.float32)
    return row_update(query_weight, gradient)


def weight_update_gathered(attn_input, query_grad, query_weight):
    n = lax.axis_size("dp")
    z = lax.axis_index("dp")
    group = lax.axis_index("expert")
    rows = query_weight.shape[0]
    share = attn_input.shape[0] // lax.axis_size("expert")

    own_slice = lax.dynamic_slice_in_dim(attn_input, group * share, share, 0)
    slices = ordered(z, *line_gather(own_slice, n))

    def columns(index):
        return lax.dynamic_slice_in_dim(query_grad, jnp.clip(index, 0, n - 1) * rows, rows, 1)

    lefts = [shift(columns(z + k), n, k, 0, n - 1 - k) for k in range(1, n)]
    rights = [shift(columns(z - k), n, -k, k, n - 1) for k in range(1, n)]
    grads = ordered(z, lefts, rights)

    gradient = token_product(columns(z), attn_input)
    for grad, part in zip(grads, slices):
        whole = lax.all_gather(part, "expert", axis=0, tiled=True)
        gradient = gradient + token_product(grad, whole)
    return row_update(query_weight, gradient)


def expert_update(
    moe_cotangent,
    expert_ids,
    route_weights,
    gate_saved,
    up_saved,
    gate_weight,
    up_weight,
    down_weight,
):
    groups = lax.axis_size("expert")
    n = lax.axis_size("dp")
    z = lax.axis_index("dp")
    local = gate_weight.shape[0]
    per_dp = gate_saved.shape[0]
    capacity = per_dp * n // groups
    tokens, width = moe_cotangent.shape
    hidden_units = down_weight.shape[1]
    blocks = groups // n

    rows = lax.all_gather(moe_cotangent, "expert", axis=0, tiled=False)
    routing = lax.all_gather(
        jnp.concatenate([expert_ids.astype(jnp.float32), route_weights], axis=1), "expert", axis=0, tiled=False
    )
    top = expert_ids.shape[1]
    ids = routing[:, :, :top].astype(jnp.int32)
    weights = routing[:, :, top:]

    mine = lax.axis_index("expert") * local + lax.broadcasted_iota(jnp.int32, (1, local, 1, 1), 1)
    hit = ids[:, None] == mine
    chosen = jnp.any(hit, axis=3)
    counts = chosen.astype(jnp.int32)
    token_weight = jnp.sum(jnp.where(hit, weights[:, None], 0.0), axis=3)
    position = jnp.cumsum(counts, axis=2, dtype=jnp.int32) - counts
    slot = jnp.where(chosen, position, -1)
    slot_iota = lax.broadcasted_iota(jnp.int32, (1, 1, capacity, 1), 2)
    matched = slot[:, :, None, :] == slot_iota
    select = matched.astype(jnp.bfloat16)
    slot_weight = jnp.sum(jnp.where(matched, token_weight[:, :, None, :], 0.0), axis=3)

    arrived = jnp.einsum("gect,gtd->gecd", select, rows, preferred_element_type=jnp.float32)
    arrived = (arrived * slot_weight[..., None]).astype(jnp.bfloat16)
    arrived = jnp.transpose(arrived, (1, 0, 2, 3)).reshape(local, groups * capacity, width)

    gathered = []
    for expert in range(local):
        parts = jnp.einsum(
            "sd,hd->sh", arrived[expert], down_weight[expert], preferred_element_type=jnp.float32
        )
        if n == 4:
            parts = parts.astype(jnp.bfloat16).reshape(n, per_dp, hidden_units).astype(jnp.float32)
            hidden = line_reduce_scatter(parts, n, z)
        else:
            hidden = lax.psum_scatter(
                parts.astype(jnp.bfloat16), "dp", scatter_dimension=0, tiled=True
            ).astype(jnp.float32)
        grads = activation_grads(hidden, gate_saved[:, expert], up_saved[:, expert])
        if n == 4:
            gathered.append((grads,) + ordered(z, *line_gather(grads, n)))
        else:
            gathered.append((lax.all_gather(grads, "dp", axis=1, tiled=True),))

    sources = (z,) + ordered_sources(z) if n == 4 else (0,)
    chunk = per_dp // capacity if n == 4 else groups
    returned = jnp.zeros((groups, tokens, width), jnp.bfloat16)
    for place, source in enumerate(sources):
        total = 0.0
        first = source * chunk
        chunk_select = lax.dynamic_slice_in_dim(select, first, chunk, 0)
        for expert in range(local):
            grads = gathered[expert][place]
            slot_input = jnp.einsum("sh,ch->sc", grads[0], gate_weight[expert], preferred_element_type=jnp.float32)
            slot_input = slot_input + jnp.einsum(
                "sh,ch->sc", grads[1], up_weight[expert], preferred_element_type=jnp.float32
            )
            slot_input = slot_input.astype(jnp.bfloat16).reshape(chunk, capacity, width)
            total = total + jnp.einsum(
                "gct,gcd->gtd", chunk_select[:, expert], slot_input, preferred_element_type=jnp.float32
            )
        returned = lax.dynamic_update_slice_in_dim(returned, total.astype(jnp.bfloat16), first, 0)
    return lax.psum_scatter(returned, "expert", scatter_dimension=0, tiled=False).astype(jnp.float32)


def shards(
    attn_input,
    query_grad,
    query_weight,
    moe_cotangent,
    expert_ids,
    route_weights,
    gate_saved,
    up_saved,
    gate_weight,
    up_weight,
    down_weight,
):
    moe_input_grad = expert_update(
        moe_cotangent,
        expert_ids,
        route_weights,
        gate_saved,
        up_saved,
        gate_weight,
        up_weight,
        down_weight,
    )
    update = weight_update_gathered if lax.axis_size("dp") == 4 else weight_update_scattered
    query_weight_next = update(attn_input, query_grad, query_weight)
    return (query_weight_next, moe_input_grad)


def solution(mesh):
    placed = (
        P("dp", None),
        P("dp", "expert"),
        P(("expert", "dp"), None),
        P("expert", "dp"),
        P("expert", None),
        P("expert", None),
        P("dp", "expert", None),
        P("dp", "expert", None),
        P("expert", "dp", None),
        P("expert", "dp", None),
        P("expert", None, "dp"),
    )
    return jax.shard_map(
        shards,
        mesh=mesh,
        in_specs=placed,
        out_specs=(P(("expert", "dp"), None), P("expert", "dp")),
        check_vma=False,
    )
```

```python
import jax
import jax.numpy as jnp
from jax import lax
from jax.sharding import PartitionSpec as P

step_rate = 0.01
epsilon = 1e-06

ends_in = [(0, 1), (3, 2)]
across = [(1, 2), (2, 1)]
ends_out = [(1, 0), (2, 3)]


def hop(value, pairs, name):
    with jax.named_scope(name):
        return lax.ppermute(value, "dp", pairs)


def swap(value, bits, name):
    with jax.named_scope(name):
        return lax.ppermute(value, "expert", [(i, i ^ bits) for i in range(8)])


def after(value, *others):
    return lax.optimization_barrier((value,) + others)[0]


def pick(stack, index):
    return lax.dynamic_index_in_dim(stack, index, 0, keepdims=False)


def line_places():
    low = lax.axis_index("dp") < 2
    return [jnp.where(low, a, b) for a, b in ((0, 3), (1, 2), (2, 1), (3, 0))]


def on_middle():
    z = lax.axis_index("dp")
    return (z == 1) | (z == 2)


def activation_grads(hidden, gate_vals, up_vals):
    gate_float = gate_vals.astype(jnp.float32)
    up_float = up_vals.astype(jnp.float32)
    sigmoid_vals = jax.nn.sigmoid(gate_float)
    gate_grad = hidden * up_float * sigmoid_vals * (1.0 + gate_float * (1.0 - sigmoid_vals))
    up_grad = hidden * gate_float * sigmoid_vals
    return jnp.stack([gate_grad, up_grad], axis=0).astype(jnp.bfloat16)


def row_update(query_weight, gradient):
    radial = jnp.mean(query_weight * gradient, axis=1, keepdims=True) / (
        jnp.mean(query_weight * query_weight, axis=1, keepdims=True) + epsilon
    )
    stepped = query_weight - step_rate * (gradient - radial * query_weight)
    return stepped * lax.rsqrt(jnp.mean(stepped * stepped, axis=1, keepdims=True) + epsilon)


def token_product(grads, inputs):
    return lax.dot_general(grads, inputs, (((0,), (0,)), ((), ())), preferred_element_type=jnp.float32)


def expert_tables(ids, weights, local, capacity):
    first = lax.axis_index("expert") * local
    experts = first + lax.broadcasted_iota(jnp.int32, (local, 1, 1), 0)
    hit = ids[..., None, :, :] == experts
    chosen = jnp.any(hit, axis=-2)
    counts = chosen.astype(jnp.int32)
    token_weight = jnp.sum(jnp.where(hit, weights[..., None, :, :], 0.0), axis=-2)
    position = jnp.cumsum(counts, axis=-1, dtype=jnp.int32) - counts
    slot = jnp.where(chosen, position, -1)
    matched = slot[..., None, :] == lax.broadcasted_iota(jnp.int32, (capacity, 1), 0)
    slot_weight = jnp.sum(jnp.where(matched, token_weight[..., None, :], 0.0), axis=-1)
    return matched.astype(jnp.bfloat16), slot_weight


def slot_product(grads, gate_weight, up_weight):
    total = jnp.einsum("sh,ch->sc", grads[0], gate_weight, preferred_element_type=jnp.float32)
    total = total + jnp.einsum("sh,ch->sc", grads[1], up_weight, preferred_element_type=jnp.float32)
    return total.astype(jnp.bfloat16)


def general_weight_update(attn_input, query_grad, query_weight):
    gradient = lax.psum_scatter(
        token_product(query_grad, attn_input).astype(jnp.bfloat16), "dp", scatter_dimension=0, tiled=True
    ).astype(jnp.float32)
    return row_update(query_weight, gradient)


def general_expert_update(
    moe_cotangent, expert_ids, route_weights, gate_saved, up_saved, gate_weight, up_weight, down_weight
):
    groups = lax.axis_size("expert")
    local = gate_weight.shape[0]
    capacity = gate_saved.shape[0] * lax.axis_size("dp") // groups
    tokens, width = moe_cotangent.shape
    rows = lax.all_gather(moe_cotangent, "expert", axis=0, tiled=False)
    routing = jnp.stack([expert_ids.T.astype(jnp.float32), route_weights.T])
    routing = lax.all_gather(routing, "expert", axis=0, tiled=False)
    select, slot_weight = expert_tables(routing[:, 0].astype(jnp.int32), routing[:, 1], local, capacity)
    arrived = jnp.einsum("gect,gtd->egcd", select, rows, preferred_element_type=jnp.float32)
    arrived = (arrived * jnp.swapaxes(slot_weight, 0, 1)[..., None]).astype(jnp.bfloat16)
    total = 0.0
    for expert in range(local):
        flat = arrived[expert].reshape(groups * capacity, width)
        parts = jnp.einsum("sd,hd->sh", flat, down_weight[expert], preferred_element_type=jnp.float32)
        hidden = lax.psum_scatter(
            parts.astype(jnp.bfloat16), "dp", scatter_dimension=0, tiled=True
        ).astype(jnp.float32)
        grads = activation_grads(hidden, gate_saved[:, expert], up_saved[:, expert])
        grads = lax.all_gather(grads, "dp", axis=1, tiled=True)
        slot_input = slot_product(grads, gate_weight[expert], up_weight[expert])
        total = total + jnp.einsum(
            "gct,gcd->gtd",
            select[:, expert],
            slot_input.reshape(groups, capacity, width),
            preferred_element_type=jnp.float32,
        )
    return lax.psum_scatter(
        total.astype(jnp.bfloat16), "expert", scatter_dimension=0, tiled=False
    ).astype(jnp.float32)


def general(
    attn_input, query_grad, query_weight, moe_cotangent, expert_ids, route_weights,
    gate_saved, up_saved, gate_weight, up_weight, down_weight,
):
    moe_input_grad = general_expert_update(
        moe_cotangent, expert_ids, route_weights, gate_saved, up_saved, gate_weight, up_weight, down_weight
    )
    return general_weight_update(attn_input, query_grad, query_weight), moe_input_grad


def reduce_over_line(parts, chip):
    own_end, own_middle, other_middle, other_end = line_places()

    def block(place):
        return pick(parts, place ^ chip).astype(jnp.float32)

    def plus(place, arrived):
        return (block(place) + arrived.astype(jnp.float32)).astype(jnp.bfloat16)

    far = hop(pick(parts, other_end ^ chip), ends_in, "sum_far_in")
    middle = hop(pick(parts, other_middle ^ chip), ends_in, "sum_middle_in")
    far = hop(plus(other_end, far), across, "sum_far_across")
    near = hop(pick(parts, own_middle ^ chip), ends_in, "sum_near_in")
    middle = hop(plus(other_middle, middle), across, "sum_middle_across")
    far = hop(plus(own_end, far), ends_out, "sum_far_out")
    total = block(lax.axis_index("dp")) + far.astype(jnp.float32)
    return total + middle.astype(jnp.float32) + near.astype(jnp.float32)


def gather_over_line(value):
    out_1 = hop(value, ends_out, "grads_out_1")
    cross_1 = hop(value, across, "grads_across_1")
    inward = hop(value, ends_in, "grads_in")
    out_2 = hop(cross_1, ends_out, "grads_out_2")
    cross_2 = hop(inward, across, "grads_across_2")
    out_3 = hop(cross_2, ends_out, "grads_out_3")
    middle = on_middle()
    return (
        jnp.where(middle, cross_1, out_1),
        jnp.where(middle, inward, out_2),
        jnp.where(middle, cross_2, out_3),
    )


def line_sources():
    own_end, own_middle, other_middle, other_end = line_places()
    middle = on_middle()
    return (
        jnp.where(middle, other_middle, own_middle),
        jnp.where(middle, own_end, other_middle),
        other_end,
    )


def shards(
    attn_input, query_grad, query_weight, moe_cotangent, expert_ids, route_weights,
    gate_saved, up_saved, gate_weight, up_weight, down_weight,
):
    if (lax.axis_size("expert"), lax.axis_size("dp")) != (8, 4):
        return general(
            attn_input, query_grad, query_weight, moe_cotangent, expert_ids, route_weights,
            gate_saved, up_saved, gate_weight, up_weight, down_weight,
        )
    z = lax.axis_index("dp")
    place = lax.axis_index("expert")
    chip, core = place // 2, place % 2
    own_end, own_middle, other_middle, other_end = line_places()
    middle = on_middle()
    local, width, hidden_units = gate_weight.shape
    tokens = moe_cotangent.shape[0]
    per_dp = gate_saved.shape[0]
    capacity = per_dp // 2
    rows = query_weight.shape[0]
    model = attn_input.shape[1]

    routing = jnp.stack([expert_ids.T.astype(jnp.float32), route_weights.T])
    tables = jnp.stack([routing] + [swap(routing, bits, "routing_plane") for bits in (2, 4, 6)])
    cotangents = jnp.stack([moe_cotangent] + [swap(moe_cotangent, bits, "tokens_plane") for bits in (2, 4, 6)])
    tables = jnp.stack([tables, swap(tables, 1, "routing_core")], axis=1)
    cotangents = (cotangents, swap(cotangents, 1, "tokens_core"))

    share = lax.dynamic_slice(
        attn_input, (chip * (attn_input.shape[0] // 4), core * (model // 2)), (attn_input.shape[0] // 4, model // 2)
    )

    def columns(index):
        return lax.dynamic_slice_in_dim(query_grad, index * rows, rows, 1)

    other_pair = lax.dynamic_slice_in_dim(query_grad, jnp.where(z < 2, 2, 0) * rows, 2 * rows, 1)

    def of_pair(pair, end):
        first = (z < 2) if end else (z >= 2)
        return jnp.where(first, pair[:, :rows], pair[:, rows:])

    in_share = hop(share, ends_in, "inputs_in")
    cross_share = hop(share, across, "inputs_across_1")
    out_share = hop(share, ends_out, "inputs_out_1")
    in_pair = hop(other_pair, ends_in, "columns_in_pair")
    cross_pair = hop(other_pair, across, "columns_across_1")
    out_own = hop(columns(own_end), ends_out, "columns_out_1")
    in_own = hop(columns(own_middle), ends_in, "columns_in_own")
    cross_share_2 = hop(in_share, across, "inputs_across_2")
    out_share_2 = hop(cross_share, ends_out, "inputs_out_2")
    cross_pair_2 = hop(in_pair, across, "columns_across_2")
    out_own_2 = hop(of_pair(cross_pair, True), ends_out, "columns_out_2")
    out_share_3 = hop(cross_share_2, ends_out, "inputs_out_3")
    out_own_3 = hop(of_pair(cross_pair_2, True), ends_out, "columns_out_3")

    select, slot_weight = expert_tables(tables[:, :, 0].astype(jnp.int32), tables[:, :, 1], local, capacity)
    parts = []
    for expert in range(local):
        arrived = jnp.stack(
            [
                jnp.einsum(
                    "gct,gtd->gcd", select[:, i, expert], cotangents[i], preferred_element_type=jnp.float32
                )
                * slot_weight[:, i, expert, :, None]
                for i in range(2)
            ],
            axis=1,
        ).astype(jnp.bfloat16)
        part = jnp.einsum(
            "sd,hd->sh",
            arrived.reshape(4 * per_dp, width),
            down_weight[expert],
            preferred_element_type=jnp.float32,
        )
        parts.append(part.astype(jnp.bfloat16).reshape(4, per_dp, hidden_units))

    parts[0] = after(parts[0], in_share, cross_share, cross_pair, out_share, out_own)

    def saved(array, expert):
        blocks = array[:, expert].reshape(2, capacity, hidden_units)
        return jnp.where(core == 0, blocks, blocks[::-1]).reshape(per_dp, hidden_units)

    gathered = []
    for expert in range(local):
        hidden = reduce_over_line(parts[expert], chip)
        if expert == 0:
            hidden = after(hidden, cross_share_2, cross_pair_2, out_share_2, out_own_2)
        grads = activation_grads(hidden, saved(gate_saved, expert), saved(up_saved, expert))
        gathered.append((grads,) + gather_over_line(grads))

    units = [(lax.dynamic_slice_in_dim(attn_input, core * (model // 2), model // 2, 1), columns(z))]
    same_core = [[0, 2, 4, 6], [1, 3, 5, 7]]
    for part, grad in (
        (jnp.where(middle, cross_share, out_share), jnp.where(middle, of_pair(cross_pair, False), out_own)),
        (jnp.where(middle, in_share, out_share_2), jnp.where(middle, in_own, out_own_2)),
        (jnp.where(middle, cross_share_2, out_share_3), jnp.where(middle, of_pair(cross_pair_2, False), out_own_3)),
    ):
        units.append((lax.all_gather(part, "expert", axis=0, tiled=True, axis_index_groups=same_core), grad))
    gradient = 0.0
    for inputs, grad in units:
        gradient = gradient + token_product(jnp.concatenate([grad, swap(grad, 1, "columns_core")], axis=1), inputs)
    mine = gradient[:rows].astype(jnp.bfloat16)
    received = swap(gradient[rows:].astype(jnp.bfloat16), 1, "gradient_core")
    gradient = jnp.where(
        core == 0, jnp.concatenate([mine, received], axis=1), jnp.concatenate([received, mine], axis=1)
    ).astype(jnp.float32)
    query_weight_next = row_update(query_weight, gradient)

    returned = jnp.zeros((4, tokens, width), jnp.bfloat16)
    for unit, source in enumerate((z,) + line_sources()):
        relative = source ^ chip
        chosen = pick(select, relative)
        total = 0.0
        for expert in range(local):
            slot_input = slot_product(gathered[expert][unit], gate_weight[expert], up_weight[expert])
            total = total + jnp.einsum(
                "gct,gcd->gtd",
                chosen[:, expert],
                slot_input.reshape(2, capacity, width),
                preferred_element_type=jnp.float32,
            )
        chip_total = total[0] + swap(total[1].astype(jnp.bfloat16), 1, "returned_core").astype(jnp.float32)
        returned = lax.dynamic_update_slice_in_dim(returned, chip_total.astype(jnp.bfloat16)[None], relative, 0)
    moe_input_grad = returned[0].astype(jnp.float32)
    for relative in (1, 2, 3):
        moe_input_grad = moe_input_grad + swap(returned[relative], 2 * relative, "returned_plane").astype(jnp.float32)
    return (query_weight_next, moe_input_grad)


def solution(mesh):
    placed = (
        P("dp", None),
        P("dp", "expert"),
        P(("expert", "dp"), None),
        P("expert", "dp"),
        P("expert", None),
        P("expert", None),
        P("dp", "expert", None),
        P("dp", "expert", None),
        P("expert", "dp", None),
        P("expert", "dp", None),
        P("expert", None, "dp"),
    )
    return jax.shard_map(
        shards,
        mesh=mesh,
        in_specs=placed,
        out_specs=(P(("expert", "dp"), None), P("expert", "dp")),
        check_vma=False,
    )
```

```python
import jax
import jax.numpy as jnp
from jax import lax
from jax.sharding import PartitionSpec as P

step_rate = 0.01
epsilon = 1e-06

ends_in = [(0, 1), (3, 2)]
across = [(1, 2), (2, 1)]
ends_out = [(1, 0), (2, 3)]


class Line:
    def __init__(self):
        self.started = {}

    def hop(self, value, pairs, name):
        history = self.started.setdefault(tuple(pairs), [])
        if len(history) > 1:
            value = after(value, history[-2])
        with jax.named_scope(name):
            history.append(lax.ppermute(value, "dp", pairs))
        return history[-1]


def swap(value, bits, name):
    with jax.named_scope(name):
        return lax.ppermute(value, "expert", [(i, i ^ bits) for i in range(8)])


def after(value, *others):
    return lax.optimization_barrier((value,) + others)[0]


def pick(stack, index):
    return lax.dynamic_index_in_dim(stack, index, 0, keepdims=False)


def line_places():
    low = lax.axis_index("dp") < 2
    return [jnp.where(low, a, b) for a, b in ((0, 3), (1, 2), (2, 1), (3, 0))]


def on_middle():
    z = lax.axis_index("dp")
    return (z == 1) | (z == 2)


def activation_grads(hidden, gate_vals, up_vals):
    gate_float = gate_vals.astype(jnp.float32)
    up_float = up_vals.astype(jnp.float32)
    sigmoid_vals = jax.nn.sigmoid(gate_float)
    gate_grad = hidden * up_float * sigmoid_vals * (1.0 + gate_float * (1.0 - sigmoid_vals))
    up_grad = hidden * gate_float * sigmoid_vals
    return jnp.stack([gate_grad, up_grad], axis=0).astype(jnp.bfloat16)


def row_update(query_weight, gradient):
    radial = jnp.mean(query_weight * gradient, axis=1, keepdims=True) / (
        jnp.mean(query_weight * query_weight, axis=1, keepdims=True) + epsilon
    )
    stepped = query_weight - step_rate * (gradient - radial * query_weight)
    return stepped * lax.rsqrt(jnp.mean(stepped * stepped, axis=1, keepdims=True) + epsilon)


def three_terms(value):
    first = lax.reduce_precision(value, 8, 7)
    second = lax.reduce_precision(value - first, 8, 7)
    return first, second, value - first - second


def token_product(grads, inputs):
    return lax.dot_general(grads, inputs, (((0,), (0,)), ((), ())), preferred_element_type=jnp.float32)


def expert_tables(ids, weights, local, capacity):
    first = lax.axis_index("expert") * local
    experts = first + lax.broadcasted_iota(jnp.int32, (local, 1, 1), 0)
    hit = ids[..., None, :, :] == experts
    chosen = jnp.any(hit, axis=-2)
    counts = chosen.astype(jnp.int32)
    token_weight = jnp.sum(jnp.where(hit, weights[..., None, :, :], 0.0), axis=-2)
    position = jnp.cumsum(counts, axis=-1, dtype=jnp.int32) - counts
    slot = jnp.where(chosen, position, -1)
    matched = slot[..., None, :] == lax.broadcasted_iota(jnp.int32, (capacity, 1), 0)
    slot_weight = jnp.sum(jnp.where(matched, token_weight[..., None, :], 0.0), axis=-1)
    return matched.astype(jnp.bfloat16), slot_weight


def slot_product(grads, gate_weight, up_weight):
    total = jnp.einsum("sh,ch->sc", grads[0], gate_weight, preferred_element_type=jnp.float32)
    total = total + jnp.einsum("sh,ch->sc", grads[1], up_weight, preferred_element_type=jnp.float32)
    return total.astype(jnp.bfloat16)


def general_weight_update(attn_input, query_grad, query_weight):
    gradient = lax.psum_scatter(
        token_product(query_grad, attn_input).astype(jnp.bfloat16), "dp", scatter_dimension=0, tiled=True
    ).astype(jnp.float32)
    return row_update(query_weight, gradient)


def general_expert_update(
    moe_cotangent, expert_ids, route_weights, gate_saved, up_saved, gate_weight, up_weight, down_weight
):
    groups = lax.axis_size("expert")
    local = gate_weight.shape[0]
    capacity = gate_saved.shape[0] * lax.axis_size("dp") // groups
    tokens, width = moe_cotangent.shape
    rows = lax.all_gather(moe_cotangent, "expert", axis=0, tiled=False)
    routing = jnp.stack([expert_ids.T.astype(jnp.float32), route_weights.T])
    routing = lax.all_gather(routing, "expert", axis=0, tiled=False)
    select, slot_weight = expert_tables(routing[:, 0].astype(jnp.int32), routing[:, 1], local, capacity)
    arrived = jnp.einsum("gect,gtd->egcd", select, rows, preferred_element_type=jnp.float32)
    arrived = (arrived * jnp.swapaxes(slot_weight, 0, 1)[..., None]).astype(jnp.bfloat16)
    total = 0.0
    for expert in range(local):
        flat = arrived[expert].reshape(groups * capacity, width)
        parts = jnp.einsum("sd,hd->sh", flat, down_weight[expert], preferred_element_type=jnp.float32)
        hidden = lax.psum_scatter(
            parts.astype(jnp.bfloat16), "dp", scatter_dimension=0, tiled=True
        ).astype(jnp.float32)
        grads = activation_grads(hidden, gate_saved[:, expert], up_saved[:, expert])
        grads = lax.all_gather(grads, "dp", axis=1, tiled=True)
        slot_input = slot_product(grads, gate_weight[expert], up_weight[expert])
        total = total + jnp.einsum(
            "gct,gcd->gtd",
            select[:, expert],
            slot_input.reshape(groups, capacity, width),
            preferred_element_type=jnp.float32,
        )
    return lax.psum_scatter(
        total.astype(jnp.bfloat16), "expert", scatter_dimension=0, tiled=False
    ).astype(jnp.float32)


def general(
    attn_input, query_grad, query_weight, moe_cotangent, expert_ids, route_weights,
    gate_saved, up_saved, gate_weight, up_weight, down_weight,
):
    moe_input_grad = general_expert_update(
        moe_cotangent, expert_ids, route_weights, gate_saved, up_saved, gate_weight, up_weight, down_weight
    )
    return general_weight_update(attn_input, query_grad, query_weight), moe_input_grad


def reduce_over_line(line, parts, chip):
    own_end, own_middle, other_middle, other_end = line_places()

    def block(place):
        return pick(parts, place ^ chip).astype(jnp.float32)

    def plus(place, arrived):
        return (block(place) + arrived.astype(jnp.float32)).astype(jnp.bfloat16)

    far = line.hop(pick(parts, other_end ^ chip), ends_in, "sum_far_in")
    middle = line.hop(pick(parts, other_middle ^ chip), ends_in, "sum_middle_in")
    near = line.hop(pick(parts, own_middle ^ chip), ends_in, "sum_near_in")
    far = line.hop(plus(other_end, far), across, "sum_far_across")
    middle = line.hop(plus(other_middle, middle), across, "sum_middle_across")
    far = line.hop(plus(own_end, far), ends_out, "sum_far_out")
    total = block(lax.axis_index("dp")) + far.astype(jnp.float32)
    return total + middle.astype(jnp.float32) + near.astype(jnp.float32)


def line_sources():
    own_end, own_middle, other_middle, other_end = line_places()
    middle = on_middle()
    return (
        jnp.where(middle, other_middle, own_middle),
        jnp.where(middle, own_end, other_middle),
        other_end,
    )


def shards(
    attn_input, query_grad, query_weight, moe_cotangent, expert_ids, route_weights,
    gate_saved, up_saved, gate_weight, up_weight, down_weight,
):
    if (lax.axis_size("expert"), lax.axis_size("dp")) != (8, 4):
        return general(
            attn_input, query_grad, query_weight, moe_cotangent, expert_ids, route_weights,
            gate_saved, up_saved, gate_weight, up_weight, down_weight,
        )
    z = lax.axis_index("dp")
    place = lax.axis_index("expert")
    chip, core = place // 2, place % 2
    own_end, own_middle, other_middle, other_end = line_places()
    middle = on_middle()
    local, width, hidden_units = gate_weight.shape
    tokens = moe_cotangent.shape[0]
    per_dp = gate_saved.shape[0]
    capacity = per_dp // 2
    rows = query_weight.shape[0]
    model = attn_input.shape[1]

    line = Line()

    top = expert_ids.shape[1]
    packed = [moe_cotangent, expert_ids.astype(jnp.bfloat16)] + [p.astype(jnp.bfloat16) for p in three_terms(route_weights)]
    packed.append(jnp.zeros((tokens, 128 - 4 * top), jnp.bfloat16))
    packed = jnp.concatenate(packed, axis=1)
    pieces = [packed] + [swap(packed, bits, "tokens_plane") for bits in (2, 4, 6)]

    def columns(index):
        return lax.dynamic_slice_in_dim(query_grad, index * rows, rows, 1)

    def of_pair(pair, end):
        first = (z < 2) if end else (z >= 2)
        return jnp.where(first, pair[:, :rows], pair[:, rows:])

    share = lax.dynamic_slice(
        attn_input, (chip * (attn_input.shape[0] // 4), core * (model // 2)), (attn_input.shape[0] // 4, model // 2)
    )
    other_pair = lax.dynamic_slice_in_dim(query_grad, jnp.where(z < 2, 2, 0) * rows, 2 * rows, 1)
    in_columns = jnp.concatenate([other_pair, columns(own_middle)], axis=1)
    cross_share = line.hop(share, across, "inputs_across_1")
    out_share = line.hop(share, ends_out, "inputs_out_1")
    in_share = line.hop(share, ends_in, "inputs_in")
    cross_pair = line.hop(other_pair, across, "columns_across_1")
    out_own = line.hop(columns(own_end), ends_out, "columns_out_1")
    in_columns = line.hop(in_columns, ends_in, "columns_in")

    tables = jnp.stack([p[:, width:] for p in pieces])
    cotangents = jnp.stack([p[:, :width] for p in pieces])
    tables = jnp.stack([tables, swap(tables, 1, "routing_core")], axis=1)
    cotangents = (cotangents, swap(cotangents, 1, "tokens_core"))
    tables = jnp.swapaxes(tables, 2, 3).astype(jnp.float32)
    weights = sum(tables[:, :, i * top : (i + 1) * top] for i in (1, 2, 3))
    select, slot_weight = expert_tables(tables[:, :, :top].astype(jnp.int32), weights, local, capacity)
    parts = []
    for expert in range(local):
        arrived = jnp.stack(
            [
                jnp.einsum(
                    "gct,gtd->gcd", select[:, i, expert], cotangents[i], preferred_element_type=jnp.float32
                )
                * slot_weight[:, i, expert, :, None]
                for i in range(2)
            ],
            axis=1,
        ).astype(jnp.bfloat16)
        part = jnp.einsum(
            "sd,hd->sh",
            arrived.reshape(4 * per_dp, width),
            down_weight[expert],
            preferred_element_type=jnp.float32,
        )
        parts.append(part.astype(jnp.bfloat16).reshape(4, per_dp, hidden_units))

    def saved(array, expert):
        blocks = array[:, expert].reshape(2, capacity, hidden_units)
        return jnp.where(core == 0, blocks, blocks[::-1]).reshape(per_dp, hidden_units)

    def grads_of(hidden, expert):
        return activation_grads(hidden, saved(gate_saved, expert), saved(up_saved, expert))

    in_share, cross_share, out_share, cross_pair = (after(v, parts[0]) for v in (in_share, cross_share, out_share, cross_pair))
    cross_share_2 = line.hop(in_share, across, "inputs_across_2")
    out_share_2 = line.hop(cross_share, ends_out, "inputs_out_2")
    out_own_2 = line.hop(of_pair(cross_pair, True), ends_out, "columns_out_2")
    cross_pair_2 = line.hop(in_columns[:, : 2 * rows], across, "columns_across_2")
    out_share_3 = line.hop(cross_share_2, ends_out, "inputs_out_3")
    grads = [grads_of(reduce_over_line(line, parts[0], chip), 0)]
    out_own_3 = line.hop(of_pair(cross_pair_2, True), ends_out, "columns_out_3")
    grads.append(grads_of(reduce_over_line(line, parts[1], chip), 1))

    inward = [line.hop(g, ends_in, "grads_in") for g in grads]
    cross_1, cross_2, out_1, out_2, out_3 = [], [], [], [], []
    for g, arrived in zip(grads, inward):
        cross_1.append(line.hop(g, across, "grads_across_1"))
        cross_2.append(line.hop(arrived, across, "grads_across_2"))
    out_1.append(line.hop(grads[0], ends_out, "grads_out_1"))
    out_2.append(line.hop(cross_1[0], ends_out, "grads_out_2"))
    out_1.append(line.hop(grads[1], ends_out, "grads_out_1"))
    out_3.append(line.hop(cross_2[0], ends_out, "grads_out_3"))
    out_2.append(line.hop(cross_1[1], ends_out, "grads_out_2"))
    out_3.append(line.hop(cross_2[1], ends_out, "grads_out_3"))

    own_columns = after(columns(z), grads[0])
    units = [(lax.dynamic_slice_in_dim(attn_input, core * (model // 2), model // 2, 1), own_columns)]
    same_core = [[0, 2, 4, 6], [1, 3, 5, 7]]
    for part, grad in (
        (jnp.where(middle, cross_share, out_share), jnp.where(middle, of_pair(cross_pair, False), out_own)),
        (jnp.where(middle, in_share, out_share_2), jnp.where(middle, in_columns[:, 2 * rows :], out_own_2)),
        (jnp.where(middle, cross_share_2, out_share_3), jnp.where(middle, of_pair(cross_pair_2, False), out_own_3)),
    ):
        units.append((lax.all_gather(part, "expert", axis=0, tiled=True, axis_index_groups=same_core), grad))
    siblings = swap(jnp.stack([grad for _, grad in units]), 1, "columns_core")
    gradient = 0.0
    for i, (inputs, grad) in enumerate(units):
        gradient = gradient + token_product(jnp.concatenate([grad, siblings[i]], axis=1), inputs)
    mine = gradient[:rows].astype(jnp.bfloat16)
    received = swap(gradient[rows:].astype(jnp.bfloat16), 1, "gradient_core")
    gradient = jnp.where(
        core == 0, jnp.concatenate([mine, received], axis=1), jnp.concatenate([received, mine], axis=1)
    ).astype(jnp.float32)
    query_weight_next = row_update(query_weight, gradient)

    out_3[1] = after(out_3[1], query_weight_next)
    sources = (z,) + line_sources()
    totals = []
    for unit, source in enumerate(sources):
        chosen = pick(select, source ^ chip)
        total = 0.0
        for expert in range(local):
            values = (
                grads[expert],
                jnp.where(middle, cross_1[expert], out_1[expert]),
                jnp.where(middle, inward[expert], out_2[expert]),
                jnp.where(middle, cross_2[expert], out_3[expert]),
            )[unit]
            slot_input = slot_product(values, gate_weight[expert], up_weight[expert])
            total = total + jnp.einsum(
                "gct,gcd->gtd",
                chosen[:, expert],
                slot_input.reshape(2, capacity, width),
                preferred_element_type=jnp.float32,
            )
        totals.append(total)
    early = swap(jnp.stack([t[1] for t in totals[:3]]).astype(jnp.bfloat16), 1, "returned_core")
    late = swap(totals[3][1].astype(jnp.bfloat16), 1, "returned_core_last")
    returned = jnp.zeros((4, tokens, width), jnp.bfloat16)
    for unit, arrived in enumerate((early[0], early[1], early[2], late)):
        chip_total = (totals[unit][0] + arrived.astype(jnp.float32)).astype(jnp.bfloat16)
        returned = lax.dynamic_update_slice_in_dim(returned, chip_total[None], sources[unit] ^ chip, 0)
    moe_input_grad = returned[0].astype(jnp.float32)
    for relative in (1, 2, 3):
        moe_input_grad = moe_input_grad + swap(returned[relative], 2 * relative, "returned_plane").astype(jnp.float32)
    return (query_weight_next, moe_input_grad)


def solution(mesh):
    placed = (
        P("dp", None),
        P("dp", "expert"),
        P(("expert", "dp"), None),
        P("expert", "dp"),
        P("expert", None),
        P("expert", None),
        P("dp", "expert", None),
        P("dp", "expert", None),
        P("expert", "dp", None),
        P("expert", "dp", None),
        P("expert", None, "dp"),
    )
    return jax.shard_map(
        shards,
        mesh=mesh,
        in_specs=placed,
        out_specs=(P(("expert", "dp"), None), P("expert", "dp")),
        check_vma=False,
    )
```

```python
import jax
import jax.numpy as jnp
from jax import lax
from jax.sharding import PartitionSpec as P

step_rate = 0.01
epsilon = 1e-06

ends_in = [(0, 1), (3, 2)]
across = [(1, 2), (2, 1)]
ends_out = [(1, 0), (2, 3)]


class Line:
    def __init__(self):
        self.started = {}

    def hop(self, value, pairs, name, flying=2):
        history = self.started.setdefault(tuple(pairs), [])
        if len(history) >= flying:
            value = after(value, history[-flying])
        with jax.named_scope(name):
            history.append(lax.ppermute(value, "dp", pairs))
        return history[-1]


def swap(value, bits, name):
    with jax.named_scope(name):
        return lax.ppermute(value, "expert", [(i, i ^ bits) for i in range(8)])


def after(value, *others):
    return lax.optimization_barrier((value,) + others)[0]


def pick(stack, index):
    return lax.dynamic_index_in_dim(stack, index, 0, keepdims=False)


def line_places():
    low = lax.axis_index("dp") < 2
    return [jnp.where(low, a, b) for a, b in ((0, 3), (1, 2), (2, 1), (3, 0))]


def on_middle():
    z = lax.axis_index("dp")
    return (z == 1) | (z == 2)


def activation_grads(hidden, gate_vals, up_vals):
    gate_float = gate_vals.astype(jnp.float32)
    up_float = up_vals.astype(jnp.float32)
    sigmoid_vals = jax.nn.sigmoid(gate_float)
    gate_grad = hidden * up_float * sigmoid_vals * (1.0 + gate_float * (1.0 - sigmoid_vals))
    up_grad = hidden * gate_float * sigmoid_vals
    return jnp.stack([gate_grad, up_grad], axis=0).astype(jnp.bfloat16)


def row_update(query_weight, gradient):
    radial = jnp.mean(query_weight * gradient, axis=1, keepdims=True) / (
        jnp.mean(query_weight * query_weight, axis=1, keepdims=True) + epsilon
    )
    stepped = query_weight - step_rate * (gradient - radial * query_weight)
    return stepped * lax.rsqrt(jnp.mean(stepped * stepped, axis=1, keepdims=True) + epsilon)


def three_terms(value):
    first = lax.reduce_precision(value, 8, 7)
    second = lax.reduce_precision(value - first, 8, 7)
    return first, second, value - first - second


def token_product(grads, inputs):
    return lax.dot_general(grads, inputs, (((0,), (0,)), ((), ())), preferred_element_type=jnp.float32)


def expert_tables(ids, weights, local, capacity):
    first = lax.axis_index("expert") * local
    experts = first + lax.broadcasted_iota(jnp.int32, (local, 1, 1), 0)
    hit = ids[..., None, :, :] == experts
    chosen = jnp.any(hit, axis=-2)
    counts = chosen.astype(jnp.int32)
    token_weight = jnp.sum(jnp.where(hit, weights[..., None, :, :], 0.0), axis=-2)
    position = jnp.cumsum(counts, axis=-1, dtype=jnp.int32) - counts
    slot = jnp.where(chosen, position, -1)
    matched = slot[..., None, :] == lax.broadcasted_iota(jnp.int32, (capacity, 1), 0)
    slot_weight = jnp.sum(jnp.where(matched, token_weight[..., None, :], 0.0), axis=-1)
    return matched.astype(jnp.bfloat16), slot_weight


def slot_product(grads, gate_weight, up_weight):
    total = jnp.einsum("sh,ch->sc", grads[0], gate_weight, preferred_element_type=jnp.float32)
    total = total + jnp.einsum("sh,ch->sc", grads[1], up_weight, preferred_element_type=jnp.float32)
    return total.astype(jnp.bfloat16)


def general_weight_update(attn_input, query_grad, query_weight):
    gradient = lax.psum_scatter(
        token_product(query_grad, attn_input).astype(jnp.bfloat16), "dp", scatter_dimension=0, tiled=True
    ).astype(jnp.float32)
    return row_update(query_weight, gradient)


def general_expert_update(
    moe_cotangent, expert_ids, route_weights, gate_saved, up_saved, gate_weight, up_weight, down_weight
):
    groups = lax.axis_size("expert")
    local = gate_weight.shape[0]
    capacity = gate_saved.shape[0] * lax.axis_size("dp") // groups
    tokens, width = moe_cotangent.shape
    rows = lax.all_gather(moe_cotangent, "expert", axis=0, tiled=False)
    routing = jnp.stack([expert_ids.T.astype(jnp.float32), route_weights.T])
    routing = lax.all_gather(routing, "expert", axis=0, tiled=False)
    select, slot_weight = expert_tables(routing[:, 0].astype(jnp.int32), routing[:, 1], local, capacity)
    arrived = jnp.einsum("gect,gtd->egcd", select, rows, preferred_element_type=jnp.float32)
    arrived = (arrived * jnp.swapaxes(slot_weight, 0, 1)[..., None]).astype(jnp.bfloat16)
    total = 0.0
    for expert in range(local):
        flat = arrived[expert].reshape(groups * capacity, width)
        parts = jnp.einsum("sd,hd->sh", flat, down_weight[expert], preferred_element_type=jnp.float32)
        hidden = lax.psum_scatter(
            parts.astype(jnp.bfloat16), "dp", scatter_dimension=0, tiled=True
        ).astype(jnp.float32)
        grads = activation_grads(hidden, gate_saved[:, expert], up_saved[:, expert])
        grads = lax.all_gather(grads, "dp", axis=1, tiled=True)
        slot_input = slot_product(grads, gate_weight[expert], up_weight[expert])
        total = total + jnp.einsum(
            "gct,gcd->gtd",
            select[:, expert],
            slot_input.reshape(groups, capacity, width),
            preferred_element_type=jnp.float32,
        )
    return lax.psum_scatter(
        total.astype(jnp.bfloat16), "expert", scatter_dimension=0, tiled=False
    ).astype(jnp.float32)


def general(
    attn_input, query_grad, query_weight, moe_cotangent, expert_ids, route_weights,
    gate_saved, up_saved, gate_weight, up_weight, down_weight,
):
    moe_input_grad = general_expert_update(
        moe_cotangent, expert_ids, route_weights, gate_saved, up_saved, gate_weight, up_weight, down_weight
    )
    return general_weight_update(attn_input, query_grad, query_weight), moe_input_grad


def reduce_over_line(line, parts, chip):
    own_end, own_middle, other_middle, other_end = line_places()

    def block(place):
        return jnp.stack([pick(part, place ^ chip) for part in parts])

    def plus(place, arrived):
        return (block(place).astype(jnp.float32) + arrived.astype(jnp.float32)).astype(jnp.bfloat16)

    far = line.hop(block(other_end), ends_in, "sum_far_in")
    middle = line.hop(block(other_middle), ends_in, "sum_middle_in")
    near = line.hop(block(own_middle), ends_in, "sum_near_in")
    far = line.hop(plus(other_end, far), across, "sum_far_across")
    middle = line.hop(plus(other_middle, middle), across, "sum_middle_across")
    far = line.hop(plus(own_end, far), ends_out, "sum_far_out")
    total = block(lax.axis_index("dp")).astype(jnp.float32) + far.astype(jnp.float32)
    return total + middle.astype(jnp.float32) + near.astype(jnp.float32)


def line_sources():
    own_end, own_middle, other_middle, other_end = line_places()
    middle = on_middle()
    return (
        jnp.where(middle, other_middle, own_middle),
        jnp.where(middle, own_end, other_middle),
        other_end,
    )


def shards(
    attn_input, query_grad, query_weight, moe_cotangent, expert_ids, route_weights,
    gate_saved, up_saved, gate_weight, up_weight, down_weight,
):
    if (lax.axis_size("expert"), lax.axis_size("dp")) != (8, 4):
        return general(
            attn_input, query_grad, query_weight, moe_cotangent, expert_ids, route_weights,
            gate_saved, up_saved, gate_weight, up_weight, down_weight,
        )
    z = lax.axis_index("dp")
    place = lax.axis_index("expert")
    chip, core = place // 2, place % 2
    own_end, own_middle, other_middle, other_end = line_places()
    middle = on_middle()
    local, width, hidden_units = gate_weight.shape
    tokens = moe_cotangent.shape[0]
    per_dp = gate_saved.shape[0]
    capacity = per_dp // 2
    rows = query_weight.shape[0]
    model = attn_input.shape[1]

    line = Line()

    top = expert_ids.shape[1]
    packed = [moe_cotangent, expert_ids.astype(jnp.bfloat16)] + [p.astype(jnp.bfloat16) for p in three_terms(route_weights)]
    packed.append(jnp.zeros((tokens, 128 - 4 * top), jnp.bfloat16))
    packed = jnp.concatenate(packed, axis=1)
    pieces = [packed] + [swap(packed, bits, "tokens_plane") for bits in (2, 4, 6)]

    quarter = model // 8

    def columns(index):
        return lax.dynamic_slice_in_dim(query_grad, index * rows, rows, 1)

    def of_pair(pair, end):
        first = (z < 2) if end else (z >= 2)
        return jnp.where(first, pair[:, :rows], pair[:, rows : 2 * rows])

    share = lax.dynamic_slice_in_dim(attn_input, (core * 4 + chip) * quarter, quarter, 1)
    other_pair = lax.dynamic_slice_in_dim(query_grad, jnp.where(z < 2, 2, 0) * rows, 2 * rows, 1)
    inputs_across = line.hop(jnp.concatenate([share, other_pair], axis=1), across, "inputs_across_1")
    inputs_out = line.hop(jnp.concatenate([share, columns(own_end)], axis=1), ends_out, "inputs_out_1")
    inputs_in = line.hop(jnp.concatenate([share, other_pair, columns(own_middle)], axis=1), ends_in, "inputs_in")

    tables = jnp.stack([p[:, width:] for p in pieces])
    cotangents = jnp.stack([p[:, :width] for p in pieces])
    tables = jnp.stack([tables, swap(tables, 1, "routing_core")], axis=1)
    cotangents = (cotangents, swap(cotangents, 1, "tokens_core"))
    tables = jnp.swapaxes(tables, 2, 3).astype(jnp.float32)
    weights = sum(tables[:, :, i * top : (i + 1) * top] for i in (1, 2, 3))
    select, slot_weight = expert_tables(tables[:, :, :top].astype(jnp.int32), weights, local, capacity)
    parts = []
    for expert in range(local):
        arrived = jnp.stack(
            [
                jnp.einsum(
                    "gct,gtd->gcd", select[:, i, expert], cotangents[i], preferred_element_type=jnp.float32
                )
                * slot_weight[:, i, expert, :, None]
                for i in range(2)
            ],
            axis=1,
        ).astype(jnp.bfloat16)
        part = jnp.einsum(
            "sd,hd->sh",
            arrived.reshape(4 * per_dp, width),
            down_weight[expert],
            preferred_element_type=jnp.float32,
        )
        parts.append(part.astype(jnp.bfloat16).reshape(4, per_dp, hidden_units))

    def saved(array):
        blocks = jnp.swapaxes(array, 0, 1).reshape(local, 2, capacity, hidden_units)
        return jnp.where(core == 0, blocks, blocks[:, ::-1]).reshape(local, per_dp, hidden_units)

    def for_end(inputs):
        return jnp.concatenate([inputs[:, :quarter], of_pair(inputs[:, quarter:], True)], axis=1)

    inputs_across, inputs_out, inputs_in = (after(v, *parts) for v in (inputs_across, inputs_out, inputs_in))
    inputs_out_2 = line.hop(for_end(inputs_across), ends_out, "inputs_out_2")
    inputs_across_2 = line.hop(inputs_in[:, : quarter + 2 * rows], across, "inputs_across_2")
    inputs_out_3 = line.hop(for_end(inputs_across_2), ends_out, "inputs_out_3")
    hidden = reduce_over_line(line, parts, chip)
    grads = activation_grads(hidden, saved(gate_saved), saved(up_saved))

    cross_1 = line.hop(grads, across, "grads_across_1")
    out_1 = line.hop(grads, ends_out, "grads_out_1")
    inward = line.hop(grads, ends_in, "grads_in")
    out_2 = line.hop(cross_1, ends_out, "grads_out_2", 1)
    cross_2 = line.hop(inward, across, "grads_across_2")
    out_3 = line.hop(cross_2, ends_out, "grads_out_3", 1)

    own = lax.dynamic_slice_in_dim(attn_input, core * (model // 2), model // 2, 1)
    own = [own[:, i * quarter : (i + 1) * quarter] for i in range(4)]
    units = [(own, after(columns(z), grads))]
    same_core = [[0, 2, 4, 6], [1, 3, 5, 7]]
    for at_middle, at_end, columns_at_middle in (
        (inputs_across, inputs_out, of_pair(inputs_across[:, quarter:], False)),
        (inputs_in, inputs_out_2, inputs_in[:, quarter + 2 * rows :]),
        (inputs_across_2, inputs_out_3, of_pair(inputs_across_2[:, quarter:], False)),
    ):
        part = jnp.where(middle, at_middle[:, :quarter], at_end[:, :quarter])
        grad = jnp.where(middle, columns_at_middle, at_end[:, quarter:])
        units.append((lax.all_gather(part, "expert", axis=0, axis_index_groups=same_core), grad))
    siblings = swap(jnp.stack([grad for _, grad in units]), 1, "columns_core")
    gradient = [0.0] * 4
    for i, (inputs, grad) in enumerate(units):
        both = jnp.concatenate([grad, siblings[i]], axis=1)
        gradient = [total + token_product(both, piece) for total, piece in zip(gradient, inputs)]
    gradient = jnp.concatenate(gradient, axis=1)
    mine = gradient[:rows].astype(jnp.bfloat16)
    received = swap(gradient[rows:].astype(jnp.bfloat16), 1, "gradient_core")
    gradient = jnp.where(
        core == 0, jnp.concatenate([mine, received], axis=1), jnp.concatenate([received, mine], axis=1)
    ).astype(jnp.float32)
    query_weight_next = row_update(query_weight, gradient)

    out_3 = after(out_3, query_weight_next)
    sources = (z,) + line_sources()
    values = (
        grads,
        jnp.where(middle, cross_1, out_1),
        jnp.where(middle, inward, out_2),
        jnp.where(middle, cross_2, out_3),
    )
    totals = []
    for unit, source in enumerate(sources):
        chosen = pick(select, source ^ chip)
        total = 0.0
        for expert in range(local):
            slot_input = slot_product(values[unit][:, expert], gate_weight[expert], up_weight[expert])
            total = total + jnp.einsum(
                "gct,gcd->gtd",
                chosen[:, expert],
                slot_input.reshape(2, capacity, width),
                preferred_element_type=jnp.float32,
            )
        totals.append(total)
    early = swap(jnp.stack([t[1] for t in totals[:3]]).astype(jnp.bfloat16), 1, "returned_core")
    late = swap(totals[3][1].astype(jnp.bfloat16), 1, "returned_core_last")
    returned = jnp.zeros((4, tokens, width), jnp.bfloat16)
    for unit, arrived in enumerate((early[0], early[1], early[2], late)):
        chip_total = (totals[unit][0] + arrived.astype(jnp.float32)).astype(jnp.bfloat16)
        returned = lax.dynamic_update_slice_in_dim(returned, chip_total[None], sources[unit] ^ chip, 0)
    moe_input_grad = returned[0].astype(jnp.float32)
    for relative in (1, 2, 3):
        moe_input_grad = moe_input_grad + swap(returned[relative], 2 * relative, "returned_plane").astype(jnp.float32)
    return (query_weight_next, moe_input_grad)


def solution(mesh):
    placed = (
        P("dp", None),
        P("dp", "expert"),
        P(("expert", "dp"), None),
        P("expert", "dp"),
        P("expert", None),
        P("expert", None),
        P("dp", "expert", None),
        P("dp", "expert", None),
        P("expert", "dp", None),
        P("expert", "dp", None),
        P("expert", None, "dp"),
    )
    return jax.shard_map(
        shards,
        mesh=mesh,
        in_specs=placed,
        out_specs=(P(("expert", "dp"), None), P("expert", "dp")),
        check_vma=False,
    )
```

```python
import jax
import jax.numpy as jnp
from jax import lax
from jax.sharding import PartitionSpec as P

step_rate = 0.01
epsilon = 1e-06

ends_in = [(0, 1), (3, 2)]
across = [(1, 2), (2, 1)]
ends_out = [(1, 0), (2, 3)]


class Line:
    def __init__(self):
        self.started = {}

    def hop(self, value, pairs, name, flying=2):
        history = self.started.setdefault(tuple(pairs), [])
        if len(history) >= flying:
            value = after(value, history[-flying])
        with jax.named_scope(name):
            history.append(lax.ppermute(value, "dp", pairs))
        return history[-1]


def swap(value, bits, name):
    with jax.named_scope(name):
        return lax.ppermute(value, "expert", [(i, i ^ bits) for i in range(8)])


def after(value, *others):
    return lax.optimization_barrier((value,) + others)[0]


def pick(stack, index):
    return lax.dynamic_index_in_dim(stack, index, 0, keepdims=False)


def line_places():
    low = lax.axis_index("dp") < 2
    return [jnp.where(low, a, b) for a, b in ((0, 3), (1, 2), (2, 1), (3, 0))]


def on_middle():
    z = lax.axis_index("dp")
    return (z == 1) | (z == 2)


def activation_grads(hidden, gate_vals, up_vals):
    gate_float = gate_vals.astype(jnp.float32)
    up_float = up_vals.astype(jnp.float32)
    sigmoid_vals = jax.nn.sigmoid(gate_float)
    gate_grad = hidden * up_float * sigmoid_vals * (1.0 + gate_float * (1.0 - sigmoid_vals))
    up_grad = hidden * gate_float * sigmoid_vals
    return jnp.stack([gate_grad, up_grad], axis=0).astype(jnp.bfloat16)


def row_update(query_weight, gradient):
    radial = jnp.mean(query_weight * gradient, axis=1, keepdims=True) / (
        jnp.mean(query_weight * query_weight, axis=1, keepdims=True) + epsilon
    )
    stepped = query_weight - step_rate * (gradient - radial * query_weight)
    return stepped * lax.rsqrt(jnp.mean(stepped * stepped, axis=1, keepdims=True) + epsilon)


def three_terms(value):
    first = lax.reduce_precision(value, 8, 7)
    second = lax.reduce_precision(value - first, 8, 7)
    return first, second, value - first - second


def token_product(grads, inputs):
    return lax.dot_general(grads, inputs, (((0,), (0,)), ((), ())), preferred_element_type=jnp.float32)


def expert_tables(ids, weights, local, capacity):
    first = lax.axis_index("expert") * local
    experts = first + lax.broadcasted_iota(jnp.int32, (local, 1, 1), 0)
    hit = ids[..., None, :, :] == experts
    chosen = jnp.any(hit, axis=-2)
    counts = chosen.astype(jnp.int32)
    token_weight = jnp.sum(jnp.where(hit, weights[..., None, :, :], 0.0), axis=-2)
    position = jnp.cumsum(counts, axis=-1, dtype=jnp.int32) - counts
    slot = jnp.where(chosen, position, -1)
    matched = slot[..., None, :] == lax.broadcasted_iota(jnp.int32, (capacity, 1), 0)
    slot_weight = jnp.sum(jnp.where(matched, token_weight[..., None, :], 0.0), axis=-1)
    return matched.astype(jnp.bfloat16), slot_weight


def slot_product(grads, gate_weight, up_weight):
    total = jnp.einsum("sh,ch->sc", grads[0], gate_weight, preferred_element_type=jnp.float32)
    total = total + jnp.einsum("sh,ch->sc", grads[1], up_weight, preferred_element_type=jnp.float32)
    return total.astype(jnp.bfloat16)


def general_weight_update(attn_input, query_grad, query_weight):
    gradient = lax.psum_scatter(
        token_product(query_grad, attn_input).astype(jnp.bfloat16), "dp", scatter_dimension=0, tiled=True
    ).astype(jnp.float32)
    return row_update(query_weight, gradient)


def general_expert_update(
    moe_cotangent, expert_ids, route_weights, gate_saved, up_saved, gate_weight, up_weight, down_weight
):
    groups = lax.axis_size("expert")
    local = gate_weight.shape[0]
    capacity = gate_saved.shape[0] * lax.axis_size("dp") // groups
    tokens, width = moe_cotangent.shape
    rows = lax.all_gather(moe_cotangent, "expert", axis=0, tiled=False)
    routing = jnp.stack([expert_ids.T.astype(jnp.float32), route_weights.T])
    routing = lax.all_gather(routing, "expert", axis=0, tiled=False)
    select, slot_weight = expert_tables(routing[:, 0].astype(jnp.int32), routing[:, 1], local, capacity)
    arrived = jnp.einsum("gect,gtd->egcd", select, rows, preferred_element_type=jnp.float32)
    arrived = (arrived * jnp.swapaxes(slot_weight, 0, 1)[..., None]).astype(jnp.bfloat16)
    total = 0.0
    for expert in range(local):
        flat = arrived[expert].reshape(groups * capacity, width)
        parts = jnp.einsum("sd,hd->sh", flat, down_weight[expert], preferred_element_type=jnp.float32)
        hidden = lax.psum_scatter(
            parts.astype(jnp.bfloat16), "dp", scatter_dimension=0, tiled=True
        ).astype(jnp.float32)
        grads = activation_grads(hidden, gate_saved[:, expert], up_saved[:, expert])
        grads = lax.all_gather(grads, "dp", axis=1, tiled=True)
        slot_input = slot_product(grads, gate_weight[expert], up_weight[expert])
        total = total + jnp.einsum(
            "gct,gcd->gtd",
            select[:, expert],
            slot_input.reshape(groups, capacity, width),
            preferred_element_type=jnp.float32,
        )
    return lax.psum_scatter(
        total.astype(jnp.bfloat16), "expert", scatter_dimension=0, tiled=False
    ).astype(jnp.float32)


def general(
    attn_input, query_grad, query_weight, moe_cotangent, expert_ids, route_weights,
    gate_saved, up_saved, gate_weight, up_weight, down_weight,
):
    moe_input_grad = general_expert_update(
        moe_cotangent, expert_ids, route_weights, gate_saved, up_saved, gate_weight, up_weight, down_weight
    )
    return general_weight_update(attn_input, query_grad, query_weight), moe_input_grad


def by_chip(pieces, chip):
    odd, high = chip % 2 == 1, chip >= 2
    pairs = [
        jnp.where(odd, pieces[i ^ 1], pieces[i]) for i in range(4)
    ]
    return [jnp.where(high, pairs[i ^ 2], pairs[i]) for i in range(4)]


def shards(
    attn_input, query_grad, query_weight, moe_cotangent, expert_ids, route_weights,
    gate_saved, up_saved, gate_weight, up_weight, down_weight,
):
    if (lax.axis_size("expert"), lax.axis_size("dp")) != (8, 4):
        return general(
            attn_input, query_grad, query_weight, moe_cotangent, expert_ids, route_weights,
            gate_saved, up_saved, gate_weight, up_weight, down_weight,
        )
    z = lax.axis_index("dp")
    place = lax.axis_index("expert")
    chip, core = place // 2, place % 2
    own_end, own_middle, other_middle, other_end = line_places()
    middle = on_middle()
    local, width, hidden_units = gate_weight.shape
    tokens, top = expert_ids.shape
    per_dp = gate_saved.shape[0]
    capacity = per_dp // 2
    rows = query_weight.shape[0]
    model = attn_input.shape[1]
    quarter = model // 8
    line = Line()

    routing = [expert_ids.astype(jnp.float32)] + list(three_terms(route_weights))
    routing = jnp.stack([value.T.reshape(tokens * top) for value in routing]).astype(jnp.bfloat16)
    routing = jnp.pad(routing.reshape(4 * tokens * top // width, width), ((0, 16 - 4 * tokens * top // width), (0, 0)))
    packed = jnp.concatenate([moe_cotangent, routing], axis=0)
    pieces = by_chip([packed] + [swap(packed, bits, "tokens_plane") for bits in (2, 4, 6)], chip)

    def columns(index):
        return lax.dynamic_slice_in_dim(query_grad, index * rows, rows, 1)

    def of_pair(pair, end):
        first = (z < 2) if end else (z >= 2)
        return jnp.where(first, pair[:, :rows], pair[:, rows : 2 * rows])

    def for_end(inputs):
        return jnp.concatenate([inputs[:, :quarter], of_pair(inputs[:, quarter:], True)], axis=1)

    share = lax.dynamic_slice_in_dim(attn_input, (core * 4 + chip) * quarter, quarter, 1)
    other_pair = lax.dynamic_slice_in_dim(query_grad, jnp.where(z < 2, 2, 0) * rows, 2 * rows, 1)
    inputs_across = line.hop(jnp.concatenate([share, other_pair], axis=1), across, "inputs_across_1")
    inputs_out = line.hop(jnp.concatenate([share, columns(own_end)], axis=1), ends_out, "inputs_out_1")
    inputs_in = line.hop(jnp.concatenate([share, other_pair, columns(own_middle)], axis=1), ends_in, "inputs_in")

    tables = jnp.stack([p[tokens:] for p in pieces])
    cotangents = jnp.stack([p[:tokens] for p in pieces])
    tables = jnp.stack([tables, swap(tables, 1, "routing_core")], axis=1).astype(jnp.float32)
    cotangents = (cotangents, swap(cotangents, 1, "tokens_core"))
    tables = tables[:, :, : 4 * tokens * top // width].reshape(4, 2, 4, top, tokens)
    weights = tables[:, :, 1] + tables[:, :, 2] + tables[:, :, 3]
    select, slot_weight = expert_tables(tables[:, :, 0].astype(jnp.int32), weights, local, capacity)

    def sums_of(expert, *first):
        arrived = jnp.stack(
            [
                jnp.einsum(
                    "gct,gtd->gcd", select[:, i, expert], cotangents[i], preferred_element_type=jnp.float32
                )
                * slot_weight[:, i, expert, :, None]
                for i in range(2)
            ],
            axis=1,
        ).astype(jnp.bfloat16)
        parts = jnp.einsum(
            "sd,hd->sh",
            after(arrived.reshape(4 * per_dp, width), *first),
            down_weight[expert],
            preferred_element_type=jnp.float32,
        )
        return parts.astype(jnp.bfloat16)

    parts = [sums_of(0, inputs_out), sums_of(1, inputs_across)]
    hidden = [lax.psum_scatter(part, "dp", scatter_dimension=0, tiled=True) for part in parts]

    inputs_across, inputs_out, inputs_in = (after(v, *parts) for v in (inputs_across, inputs_out, inputs_in))
    inputs_out_2 = line.hop(for_end(inputs_across), ends_out, "inputs_out_2")
    inputs_across_2 = line.hop(inputs_in[:, : quarter + 2 * rows], across, "inputs_across_2")
    inputs_out_3 = line.hop(for_end(inputs_across_2), ends_out, "inputs_out_3")
    hidden[0] = after(hidden[0], inputs_out_2, inputs_across_2)
    hidden[1] = after(hidden[1], inputs_out_3)

    def saved(array, expert):
        blocks = array[:, expert].reshape(2, capacity, hidden_units)
        return jnp.where(core == 0, blocks, blocks[::-1]).reshape(per_dp, hidden_units)

    grads = [
        activation_grads(hidden[e].astype(jnp.float32), saved(gate_saved, e), saved(up_saved, e)) for e in range(local)
    ]
    gathered = [lax.all_gather(g, "dp", axis=1, tiled=True) for g in grads]

    units = [
        (
            [lax.dynamic_slice_in_dim(attn_input, (core * 4 + (chip ^ r)) * quarter, quarter, 1) for r in range(4)],
            columns(z),
        )
    ]
    for at_middle, at_end, columns_at_middle in (
        (inputs_across, inputs_out, of_pair(inputs_across[:, quarter:], False)),
        (inputs_in, inputs_out_2, inputs_in[:, quarter + 2 * rows :]),
        (inputs_across_2, inputs_out_3, of_pair(inputs_across_2[:, quarter:], False)),
    ):
        part = after(jnp.where(middle, at_middle[:, :quarter], at_end[:, :quarter]), *grads)
        grad = jnp.where(middle, columns_at_middle, at_end[:, quarter:])
        units.append(([part] + [swap(part, bits, "inputs_plane") for bits in (2, 4, 6)], grad))
    siblings = swap(after(jnp.stack([grad for _, grad in units]), *grads), 1, "columns_core")
    gradient = [0.0] * 4
    for i, (inputs, grad) in enumerate(units):
        both = jnp.concatenate([grad, siblings[i]], axis=1)
        gradient = [total + token_product(both, piece) for total, piece in zip(gradient, inputs)]
    mine = [part[:rows].astype(jnp.bfloat16) for part in gradient]
    received = swap(jnp.stack([part[rows:] for part in gradient]).astype(jnp.bfloat16), 1, "gradient_core")
    mine, received = by_chip(mine, chip), by_chip(received, chip)
    low = [jnp.where(core == 0, a, b) for a, b in zip(mine, received)]
    high = [jnp.where(core == 0, b, a) for a, b in zip(mine, received)]
    query_weight_next = row_update(query_weight, jnp.concatenate(low + high, axis=1).astype(jnp.float32))

    gathered[1] = after(gathered[1], query_weight_next)
    total = 0.0
    for expert in range(local):
        slot_input = slot_product(gathered[expert], gate_weight[expert], up_weight[expert])
        total = total + jnp.einsum(
            "gict,gicd->gitd",
            select[:, :, expert],
            slot_input.reshape(4, 2, capacity, width),
            preferred_element_type=jnp.float32,
        )
    total = total[:, 0] + swap(total[:, 1].astype(jnp.bfloat16), 1, "returned_core").astype(jnp.float32)
    moe_input_grad = pick(total, chip)
    total = total.astype(jnp.bfloat16)
    for relative in (1, 2, 3):
        arrived = swap(pick(total, chip ^ relative), 2 * relative, "returned_plane")
        moe_input_grad = moe_input_grad + arrived.astype(jnp.float32)
    return (query_weight_next, moe_input_grad)


def solution(mesh):
    placed = (
        P("dp", None),
        P("dp", "expert"),
        P(("expert", "dp"), None),
        P("expert", "dp"),
        P("expert", None),
        P("expert", None),
        P("dp", "expert", None),
        P("dp", "expert", None),
        P("expert", "dp", None),
        P("expert", "dp", None),
        P("expert", None, "dp"),
    )
    return jax.shard_map(
        shards,
        mesh=mesh,
        in_specs=placed,
        out_specs=(P(("expert", "dp"), None), P("expert", "dp")),
        check_vma=False,
    )
```

```python
import jax
import jax.numpy as jnp
from jax import lax
from jax.sharding import PartitionSpec as P

step_rate = 0.01
epsilon = 1e-06

ends_in = [(0, 1), (3, 2)]
across = [(1, 2), (2, 1)]
ends_out = [(1, 0), (2, 3)]


class Line:
    def __init__(self):
        self.done = []

    def round(self, *sends):
        arrived = []
        for value, pairs, name in sends:
            value = after(value, *self.done) if self.done else value
            with jax.named_scope(name):
                arrived.append(lax.ppermute(value, "dp", pairs))
        self.done = list(arrived)
        return arrived

    def beside(self, *values):
        self.done += values


def swap(value, bits, name):
    with jax.named_scope(name):
        return lax.ppermute(value, "expert", [(i, i ^ bits) for i in range(8)])


def after(value, *others):
    return lax.optimization_barrier((value,) + others)[0]


def pick(stack, index):
    return lax.dynamic_index_in_dim(stack, index, 0, keepdims=False)


def line_places():
    low = lax.axis_index("dp") < 2
    return [jnp.where(low, a, b) for a, b in ((0, 3), (1, 2), (2, 1), (3, 0))]


def on_middle():
    z = lax.axis_index("dp")
    return (z == 1) | (z == 2)


def activation_grads(hidden, gate_vals, up_vals):
    gate_float = gate_vals.astype(jnp.float32)
    up_float = up_vals.astype(jnp.float32)
    sigmoid_vals = jax.nn.sigmoid(gate_float)
    gate_grad = hidden * up_float * sigmoid_vals * (1.0 + gate_float * (1.0 - sigmoid_vals))
    up_grad = hidden * gate_float * sigmoid_vals
    return jnp.stack([gate_grad, up_grad], axis=0).astype(jnp.bfloat16)


def row_update(query_weight, gradient):
    radial = jnp.mean(query_weight * gradient, axis=1, keepdims=True) / (
        jnp.mean(query_weight * query_weight, axis=1, keepdims=True) + epsilon
    )
    stepped = query_weight - step_rate * (gradient - radial * query_weight)
    return stepped * lax.rsqrt(jnp.mean(stepped * stepped, axis=1, keepdims=True) + epsilon)


def three_terms(value):
    first = lax.reduce_precision(value, 8, 7)
    second = lax.reduce_precision(value - first, 8, 7)
    return first, second, value - first - second


def token_product(grads, inputs):
    return lax.dot_general(grads, inputs, (((0,), (0,)), ((), ())), preferred_element_type=jnp.float32)


def expert_tables(ids, weights, local, capacity):
    first = lax.axis_index("expert") * local
    experts = first + lax.broadcasted_iota(jnp.int32, (local, 1, 1), 0)
    hit = ids[..., None, :, :] == experts
    chosen = jnp.any(hit, axis=-2)
    counts = chosen.astype(jnp.int32)
    token_weight = jnp.sum(jnp.where(hit, weights[..., None, :, :], 0.0), axis=-2)
    position = jnp.cumsum(counts, axis=-1, dtype=jnp.int32) - counts
    slot = jnp.where(chosen, position, -1)
    matched = slot[..., None, :] == lax.broadcasted_iota(jnp.int32, (capacity, 1), 0)
    slot_weight = jnp.sum(jnp.where(matched, token_weight[..., None, :], 0.0), axis=-1)
    return matched.astype(jnp.bfloat16), slot_weight


def slot_product(grads, gate_weight, up_weight):
    total = jnp.einsum("sh,ch->sc", grads[0], gate_weight, preferred_element_type=jnp.float32)
    total = total + jnp.einsum("sh,ch->sc", grads[1], up_weight, preferred_element_type=jnp.float32)
    return total.astype(jnp.bfloat16)


def general_weight_update(attn_input, query_grad, query_weight):
    gradient = lax.psum_scatter(
        token_product(query_grad, attn_input).astype(jnp.bfloat16), "dp", scatter_dimension=0, tiled=True
    ).astype(jnp.float32)
    return row_update(query_weight, gradient)


def general_expert_update(
    moe_cotangent, expert_ids, route_weights, gate_saved, up_saved, gate_weight, up_weight, down_weight
):
    groups = lax.axis_size("expert")
    local = gate_weight.shape[0]
    capacity = gate_saved.shape[0] * lax.axis_size("dp") // groups
    tokens, width = moe_cotangent.shape
    rows = lax.all_gather(moe_cotangent, "expert", axis=0, tiled=False)
    routing = jnp.stack([expert_ids.T.astype(jnp.float32), route_weights.T])
    routing = lax.all_gather(routing, "expert", axis=0, tiled=False)
    select, slot_weight = expert_tables(routing[:, 0].astype(jnp.int32), routing[:, 1], local, capacity)
    arrived = jnp.einsum("gect,gtd->egcd", select, rows, preferred_element_type=jnp.float32)
    arrived = (arrived * jnp.swapaxes(slot_weight, 0, 1)[..., None]).astype(jnp.bfloat16)
    total = 0.0
    for expert in range(local):
        flat = arrived[expert].reshape(groups * capacity, width)
        parts = jnp.einsum("sd,hd->sh", flat, down_weight[expert], preferred_element_type=jnp.float32)
        hidden = lax.psum_scatter(
            parts.astype(jnp.bfloat16), "dp", scatter_dimension=0, tiled=True
        ).astype(jnp.float32)
        grads = activation_grads(hidden, gate_saved[:, expert], up_saved[:, expert])
        grads = lax.all_gather(grads, "dp", axis=1, tiled=True)
        slot_input = slot_product(grads, gate_weight[expert], up_weight[expert])
        total = total + jnp.einsum(
            "gct,gcd->gtd",
            select[:, expert],
            slot_input.reshape(groups, capacity, width),
            preferred_element_type=jnp.float32,
        )
    return lax.psum_scatter(
        total.astype(jnp.bfloat16), "expert", scatter_dimension=0, tiled=False
    ).astype(jnp.float32)


def general(
    attn_input, query_grad, query_weight, moe_cotangent, expert_ids, route_weights,
    gate_saved, up_saved, gate_weight, up_weight, down_weight,
):
    moe_input_grad = general_expert_update(
        moe_cotangent, expert_ids, route_weights, gate_saved, up_saved, gate_weight, up_weight, down_weight
    )
    return general_weight_update(attn_input, query_grad, query_weight), moe_input_grad


def line_sources():
    own_end, own_middle, other_middle, other_end = line_places()
    middle = on_middle()
    return (
        jnp.where(middle, other_middle, own_middle),
        jnp.where(middle, own_end, other_middle),
        other_end,
    )


def shards(
    attn_input, query_grad, query_weight, moe_cotangent, expert_ids, route_weights,
    gate_saved, up_saved, gate_weight, up_weight, down_weight,
):
    if (lax.axis_size("expert"), lax.axis_size("dp")) != (8, 4):
        return general(
            attn_input, query_grad, query_weight, moe_cotangent, expert_ids, route_weights,
            gate_saved, up_saved, gate_weight, up_weight, down_weight,
        )
    z = lax.axis_index("dp")
    place = lax.axis_index("expert")
    chip, core = place // 2, place % 2
    own_end, own_middle, other_middle, other_end = line_places()
    middle = on_middle()
    local, width, hidden_units = gate_weight.shape
    tokens, top = expert_ids.shape
    per_dp = gate_saved.shape[0]
    capacity = per_dp // 2
    rows = query_weight.shape[0]
    half = rows // 2
    line = Line()

    routing = [expert_ids.astype(jnp.float32)] + list(three_terms(route_weights))
    routing = jnp.stack([value.T.reshape(tokens * top) for value in routing]).astype(jnp.bfloat16)
    routing = jnp.pad(routing.reshape(4 * tokens * top // width, width), ((0, 16 - 4 * tokens * top // width), (0, 0)))
    packed = jnp.concatenate([moe_cotangent, routing], axis=0)
    pieces = [packed] + [swap(packed, bits, "tokens_plane") for bits in (2, 4, 6)]

    def product(index, *first):
        grads = lax.dynamic_slice_in_dim(query_grad, index * rows, rows, 1)
        return token_product(after(grads, *first) if first else grads, attn_input).astype(jnp.bfloat16)

    def add(a, b):
        return (a.astype(jnp.float32) + b.astype(jnp.float32)).astype(jnp.bfloat16)

    to_far = product(other_end)
    (far_0,) = line.round((to_far[:half], ends_in, "rows_far_in_0"))

    tables = jnp.stack([p[tokens:] for p in pieces])
    cotangents = jnp.stack([p[:tokens] for p in pieces])
    tables = jnp.stack([tables, swap(tables, 1, "routing_core")], axis=1).astype(jnp.float32)
    cotangents = (cotangents, swap(cotangents, 1, "tokens_core"))
    tables = tables[:, :, : 4 * tokens * top // width].reshape(4, 2, 4, top, tokens)
    weights = tables[:, :, 1] + tables[:, :, 2] + tables[:, :, 3]
    select, slot_weight = expert_tables(tables[:, :, 0].astype(jnp.int32), weights, local, capacity)
    parts = []
    for expert in range(local):
        arrived = jnp.stack(
            [
                jnp.einsum(
                    "gct,gtd->gcd", select[:, i, expert], cotangents[i], preferred_element_type=jnp.float32
                )
                * slot_weight[:, i, expert, :, None]
                for i in range(2)
            ],
            axis=1,
        ).astype(jnp.bfloat16)
        part = jnp.einsum(
            "sd,hd->sh",
            arrived.reshape(4 * per_dp, width),
            down_weight[expert],
            preferred_element_type=jnp.float32,
        )
        parts.append(part.astype(jnp.bfloat16).reshape(4, per_dp, hidden_units))

    def block(index):
        return jnp.stack([pick(part, index ^ chip) for part in parts])

    def saved(array):
        blocks = jnp.swapaxes(array, 0, 1).reshape(local, 2, capacity, hidden_units)
        return jnp.where(core == 0, blocks, blocks[:, ::-1]).reshape(local, per_dp, hidden_units)

    to_end = product(own_end, far_0)
    sum_far, far_0 = line.round(
        (block(other_end), ends_in, "sum_far_in"), (add(to_far[:half], far_0), across, "rows_far_across_0")
    )
    to_middle = product(other_middle, sum_far)
    sum_middle, sum_far, far_0 = line.round(
        (block(other_middle), ends_in, "sum_middle_in"),
        (add(block(other_end), sum_far), across, "sum_far_across"),
        (add(to_end[:half], far_0), ends_out, "rows_far_out_0"),
    )
    to_near = product(own_middle, sum_far)
    sum_near, sum_middle, sum_far = line.round(
        (block(own_middle), ends_in, "sum_near_in"),
        (add(block(other_middle), sum_middle), across, "sum_middle_across"),
        (add(block(own_end), sum_far), ends_out, "sum_far_out"),
    )
    line.beside(to_middle, to_near)
    hidden = block(z).astype(jnp.float32) + sum_far.astype(jnp.float32)
    hidden = hidden + sum_middle.astype(jnp.float32) + sum_near.astype(jnp.float32)
    grads = activation_grads(hidden, saved(gate_saved), saved(up_saved))

    sources = (z,) + line_sources()
    relatives = [source ^ chip for source in sources]

    def unit(values, relative):
        chosen = pick(select, relative)
        total = 0.0
        for expert in range(local):
            slot_input = slot_product(values[:, expert], gate_weight[expert], up_weight[expert])
            total = total + jnp.einsum(
                "gct,gcd->gtd",
                chosen[:, expert],
                slot_input.reshape(2, capacity, width),
                preferred_element_type=jnp.float32,
            )
        return total

    inward, cross_1, out_1 = line.round(
        (grads, ends_in, "grads_in"), (grads, across, "grads_across_1"), (grads, ends_out, "grads_out_1")
    )
    totals = [unit(after(grads, sum_near), relatives[0])]
    line.beside(totals[0])
    far_1, middle_0, cross_2, out_2 = line.round(
        (to_far[half:], ends_in, "rows_far_in_1"),
        (to_middle[:half], ends_in, "rows_middle_in_0"),
        (inward, across, "grads_across_2"),
        (cross_1, ends_out, "grads_out_2"),
    )
    totals.append(unit(jnp.where(middle, cross_1, out_1), relatives[1]))
    line.beside(totals[1])
    middle_1, near_0, far_1, middle_0, out_3 = line.round(
        (to_middle[half:], ends_in, "rows_middle_in_1"),
        (to_near[:half], ends_in, "rows_near_in_0"),
        (add(to_far[half:], far_1), across, "rows_far_across_1"),
        (add(to_middle[:half], middle_0), across, "rows_middle_across_0"),
        (cross_2, ends_out, "grads_out_3"),
    )
    totals.append(unit(jnp.where(middle, inward, out_2), relatives[2]))
    early = swap(jnp.stack([t[1] for t in totals]).astype(jnp.bfloat16), 1, "returned_core")
    line.beside(early)
    near_1, middle_1, far_1 = line.round(
        (to_near[half:], ends_in, "rows_near_in_1"),
        (add(to_middle[half:], middle_1), across, "rows_middle_across_1"),
        (add(to_end[half:], far_1), ends_out, "rows_far_out_1"),
    )
    totals.append(unit(jnp.where(middle, cross_2, out_3), relatives[3]))
    late = swap(totals[3][1].astype(jnp.bfloat16), 1, "returned_core_last")

    returned = jnp.zeros((4, tokens, width), jnp.bfloat16)
    for total, arrived, relative in zip(totals, (early[0], early[1], early[2], late), relatives):
        returned = lax.dynamic_update_slice_in_dim(returned, add(total[0], arrived)[None], relative, 0)
    moe_input_grad = returned[0].astype(jnp.float32)
    for relative in (1, 2, 3):
        moe_input_grad = moe_input_grad + swap(returned[relative], 2 * relative, "returned_plane").astype(jnp.float32)

    gradient = [
        jnp.where(middle, to_near[cut], to_end[cut]).astype(jnp.float32) + sum(part.astype(jnp.float32) for part in arrived)
        for cut, arrived in ((slice(0, half), (far_0, middle_0, near_0)), (slice(half, rows), (far_1, middle_1, near_1)))
    ]
    query_weight_next = row_update(query_weight, jnp.concatenate(gradient, axis=0))
    return (query_weight_next, moe_input_grad)


def solution(mesh):
    placed = (
        P("dp", None),
        P("dp", "expert"),
        P(("expert", "dp"), None),
        P("expert", "dp"),
        P("expert", None),
        P("expert", None),
        P("dp", "expert", None),
        P("dp", "expert", None),
        P("expert", "dp", None),
        P("expert", "dp", None),
        P("expert", None, "dp"),
    )
    return jax.shard_map(
        shards,
        mesh=mesh,
        in_specs=placed,
        out_specs=(P(("expert", "dp"), None), P("expert", "dp")),
        check_vma=False,
    )
```

```python
import jax
import jax.numpy as jnp
from jax import lax
from jax.sharding import PartitionSpec as P

step_rate = 0.01
epsilon = 1e-06

ends_in = [(0, 1), (3, 2)]
across = [(1, 2), (2, 1)]
ends_out = [(1, 0), (2, 3)]


class Line:
    def __init__(self):
        self.done = []

    def round(self, *sends):
        arrived = []
        for value, pairs, name in sends:
            value = after(value, *self.done) if self.done else value
            with jax.named_scope(name):
                arrived.append(lax.ppermute(value, "dp", pairs))
        self.done = list(arrived)
        return arrived

    def beside(self, *values):
        self.done += values


def swap(value, bits, name):
    with jax.named_scope(name):
        return lax.ppermute(value, "expert", [(i, i ^ bits) for i in range(8)])


def after(value, *others):
    return lax.optimization_barrier((value,) + others)[0]


def pick(stack, index):
    return lax.dynamic_index_in_dim(stack, index, 0, keepdims=False)


def line_places():
    low = lax.axis_index("dp") < 2
    return [jnp.where(low, a, b) for a, b in ((0, 3), (1, 2), (2, 1), (3, 0))]


def on_middle():
    z = lax.axis_index("dp")
    return (z == 1) | (z == 2)


def activation_grads(hidden, gate_vals, up_vals):
    gate_float = gate_vals.astype(jnp.float32)
    up_float = up_vals.astype(jnp.float32)
    sigmoid_vals = jax.nn.sigmoid(gate_float)
    gate_grad = hidden * up_float * sigmoid_vals * (1.0 + gate_float * (1.0 - sigmoid_vals))
    up_grad = hidden * gate_float * sigmoid_vals
    return jnp.stack([gate_grad, up_grad], axis=0).astype(jnp.bfloat16)


def row_update(query_weight, gradient):
    radial = jnp.mean(query_weight * gradient, axis=1, keepdims=True) / (
        jnp.mean(query_weight * query_weight, axis=1, keepdims=True) + epsilon
    )
    stepped = query_weight - step_rate * (gradient - radial * query_weight)
    return stepped * lax.rsqrt(jnp.mean(stepped * stepped, axis=1, keepdims=True) + epsilon)


def three_terms(value):
    first = lax.reduce_precision(value, 8, 7)
    second = lax.reduce_precision(value - first, 8, 7)
    return first, second, value - first - second


def token_product(grads, inputs):
    return lax.dot_general(grads, inputs, (((0,), (0,)), ((), ())), preferred_element_type=jnp.float32)


def expert_tables(ids, weights, local, capacity):
    first = lax.axis_index("expert") * local
    experts = first + lax.broadcasted_iota(jnp.int32, (local, 1, 1), 0)
    hit = ids[..., None, :, :] == experts
    chosen = jnp.any(hit, axis=-2)
    token_weight = jnp.sum(jnp.where(hit, weights[..., None, :, :], 0.0), axis=-2)
    token = lax.broadcasted_iota(jnp.int32, (chosen.shape[-1],) * 2, 0)
    earlier = token < lax.broadcasted_iota(jnp.int32, token.shape, 1)
    position = jnp.dot(
        chosen.astype(jnp.bfloat16), earlier.astype(jnp.bfloat16), preferred_element_type=jnp.float32
    ).astype(jnp.int32)
    slot = jnp.where(chosen, position, -1)
    matched = slot[..., None, :] == lax.broadcasted_iota(jnp.int32, (capacity, 1), 0)
    slot_weight = jnp.sum(jnp.where(matched, token_weight[..., None, :], 0.0), axis=-1)
    return matched.astype(jnp.bfloat16), slot_weight


def slot_product(grads, gate_weight, up_weight):
    total = jnp.einsum("sh,ch->sc", grads[0], gate_weight, preferred_element_type=jnp.float32)
    total = total + jnp.einsum("sh,ch->sc", grads[1], up_weight, preferred_element_type=jnp.float32)
    return total.astype(jnp.bfloat16)


def general_weight_update(attn_input, query_grad, query_weight):
    gradient = lax.psum_scatter(
        token_product(query_grad, attn_input).astype(jnp.bfloat16), "dp", scatter_dimension=0, tiled=True
    ).astype(jnp.float32)
    return row_update(query_weight, gradient)


def general_expert_update(
    moe_cotangent, expert_ids, route_weights, gate_saved, up_saved, gate_weight, up_weight, down_weight
):
    groups = lax.axis_size("expert")
    local = gate_weight.shape[0]
    capacity = gate_saved.shape[0] * lax.axis_size("dp") // groups
    tokens, width = moe_cotangent.shape
    rows = lax.all_gather(moe_cotangent, "expert", axis=0, tiled=False)
    routing = jnp.stack([expert_ids.T.astype(jnp.float32), route_weights.T])
    routing = lax.all_gather(routing, "expert", axis=0, tiled=False)
    select, slot_weight = expert_tables(routing[:, 0].astype(jnp.int32), routing[:, 1], local, capacity)
    arrived = jnp.einsum("gect,gtd->egcd", select, rows, preferred_element_type=jnp.float32)
    arrived = (arrived * jnp.swapaxes(slot_weight, 0, 1)[..., None]).astype(jnp.bfloat16)
    total = 0.0
    for expert in range(local):
        flat = arrived[expert].reshape(groups * capacity, width)
        parts = jnp.einsum("sd,hd->sh", flat, down_weight[expert], preferred_element_type=jnp.float32)
        hidden = lax.psum_scatter(
            parts.astype(jnp.bfloat16), "dp", scatter_dimension=0, tiled=True
        ).astype(jnp.float32)
        grads = activation_grads(hidden, gate_saved[:, expert], up_saved[:, expert])
        grads = lax.all_gather(grads, "dp", axis=1, tiled=True)
        slot_input = slot_product(grads, gate_weight[expert], up_weight[expert])
        total = total + jnp.einsum(
            "gct,gcd->gtd",
            select[:, expert],
            slot_input.reshape(groups, capacity, width),
            preferred_element_type=jnp.float32,
        )
    return lax.psum_scatter(
        total.astype(jnp.bfloat16), "expert", scatter_dimension=0, tiled=False
    ).astype(jnp.float32)


def general(
    attn_input, query_grad, query_weight, moe_cotangent, expert_ids, route_weights,
    gate_saved, up_saved, gate_weight, up_weight, down_weight,
):
    moe_input_grad = general_expert_update(
        moe_cotangent, expert_ids, route_weights, gate_saved, up_saved, gate_weight, up_weight, down_weight
    )
    return general_weight_update(attn_input, query_grad, query_weight), moe_input_grad


def line_sources():
    own_end, own_middle, other_middle, other_end = line_places()
    middle = on_middle()
    return (
        jnp.where(middle, other_middle, own_middle),
        jnp.where(middle, own_end, other_middle),
        other_end,
    )


def shards(
    attn_input, query_grad, query_weight, moe_cotangent, expert_ids, route_weights,
    gate_saved, up_saved, gate_weight, up_weight, down_weight,
):
    if (lax.axis_size("expert"), lax.axis_size("dp")) != (8, 4):
        return general(
            attn_input, query_grad, query_weight, moe_cotangent, expert_ids, route_weights,
            gate_saved, up_saved, gate_weight, up_weight, down_weight,
        )
    z = lax.axis_index("dp")
    place = lax.axis_index("expert")
    chip, core = place // 2, place % 2
    own_end, own_middle, other_middle, other_end = line_places()
    middle = on_middle()
    local, width, hidden_units = gate_weight.shape
    tokens, top = expert_ids.shape
    per_dp = gate_saved.shape[0]
    capacity = per_dp // 2
    rows = query_weight.shape[0]
    half = rows // 2
    line = Line()

    pieces = jnp.stack([moe_cotangent] + [swap(moe_cotangent, bits, "tokens_plane") for bits in (2, 4, 6)])
    routing = [expert_ids.astype(jnp.float32)] + list(three_terms(route_weights))
    tables = jnp.stack([value.T for value in routing]).astype(jnp.bfloat16)
    tables = jnp.stack([tables, swap(tables, 2, "routing_x")])
    tables = jnp.concatenate([tables, swap(tables, 4, "routing_y")])
    tables = jnp.stack([tables, swap(tables, 1, "routing_core")], axis=1).astype(jnp.float32)

    def product(places, *first):
        grads = [lax.dynamic_slice_in_dim(query_grad, index * rows + at * half, half, 1) for index, at in places]
        grads = jnp.concatenate(grads, axis=1)
        return token_product(after(grads, *first) if first else grads, attn_input).astype(jnp.bfloat16)

    def add(a, b):
        return (a.astype(jnp.float32) + b.astype(jnp.float32)).astype(jnp.bfloat16)

    to_far_0 = product([(other_end, 0)])
    (far_0,) = line.round((to_far_0, ends_in, "rows_far_in_0"))

    cotangents = (pieces, swap(pieces, 1, "tokens_core"))
    weights = tables[:, :, 1] + tables[:, :, 2] + tables[:, :, 3]
    select, slot_weight = expert_tables(tables[:, :, 0].astype(jnp.int32), weights, local, capacity)
    parts = []
    for expert in range(local):
        arrived = jnp.stack(
            [
                jnp.einsum(
                    "gct,gtd->gcd", select[:, i, expert], cotangents[i], preferred_element_type=jnp.float32
                )
                * slot_weight[:, i, expert, :, None]
                for i in range(2)
            ],
            axis=1,
        ).astype(jnp.bfloat16)
        part = jnp.einsum(
            "sd,hd->sh",
            arrived.reshape(4 * per_dp, width),
            down_weight[expert],
            preferred_element_type=jnp.float32,
        )
        parts.append(part.astype(jnp.bfloat16).reshape(4, per_dp, hidden_units))

    def block(index):
        return jnp.stack([pick(part, index ^ chip) for part in parts])

    def saved(array):
        blocks = jnp.swapaxes(array, 0, 1).reshape(local, 2, capacity, hidden_units)
        return jnp.where(core == 0, blocks, blocks[:, ::-1]).reshape(local, per_dp, hidden_units)

    to_end = product([(own_end, 0), (own_end, 1)], far_0)
    sum_far, far_0 = line.round(
        (block(other_end), ends_in, "sum_far_in"), (add(to_far_0, far_0), across, "rows_far_across_0")
    )
    to_far_1_middle_0 = product([(other_end, 1), (other_middle, 0)], sum_far)
    sum_middle, sum_far, far_0 = line.round(
        (block(other_middle), ends_in, "sum_middle_in"),
        (add(block(other_end), sum_far), across, "sum_far_across"),
        (add(to_end[:half], far_0), ends_out, "rows_far_out_0"),
    )
    to_middle_1_near_0 = product([(other_middle, 1), (own_middle, 0)], sum_far)
    sum_near, sum_middle, sum_far = line.round(
        (block(own_middle), ends_in, "sum_near_in"),
        (add(block(other_middle), sum_middle), across, "sum_middle_across"),
        (add(block(own_end), sum_far), ends_out, "sum_far_out"),
    )
    to_near_1 = product([(own_middle, 1)], sum_middle)
    line.beside(to_far_1_middle_0, to_middle_1_near_0, to_near_1)
    hidden = block(z).astype(jnp.float32) + sum_far.astype(jnp.float32)
    hidden = hidden + sum_middle.astype(jnp.float32) + sum_near.astype(jnp.float32)
    grads = activation_grads(hidden, saved(gate_saved), saved(up_saved))

    sources = (z,) + line_sources()
    relatives = [source ^ chip for source in sources]

    def units(values, places):
        values = jnp.concatenate(values, axis=2)
        chosen = jnp.stack([pick(select, index) for index in places])
        total = 0.0
        for expert in range(local):
            slot_input = slot_product(values[:, expert], gate_weight[expert], up_weight[expert])
            total = total + jnp.einsum(
                "ugct,ugcd->ugtd",
                chosen[:, :, expert],
                slot_input.reshape(2, 2, capacity, width),
                preferred_element_type=jnp.float32,
            )
        return total

    inward, cross_1, out_1 = line.round(
        (grads, ends_in, "grads_in"), (grads, across, "grads_across_1"), (grads, ends_out, "grads_out_1")
    )
    far_1_middle_0_in, cross_2, out_2 = line.round(
        (to_far_1_middle_0, ends_in, "rows_far_1_middle_0_in"),
        (inward, across, "grads_across_2"),
        (cross_1, ends_out, "grads_out_2"),
    )
    early = units((grads, jnp.where(middle, cross_1, out_1)), relatives[:2])
    line.beside(early)
    middle_1_near_0, far_1_middle_0, out_3 = line.round(
        (to_middle_1_near_0, ends_in, "rows_middle_1_near_0_in"),
        (add(to_far_1_middle_0, far_1_middle_0_in), across, "rows_far_1_middle_0_across"),
        (cross_2, ends_out, "grads_out_3"),
    )
    near_1, middle_1, far_1 = line.round(
        (to_near_1, ends_in, "rows_near_in_1"),
        (add(to_middle_1_near_0[:half], middle_1_near_0[:half]), across, "rows_middle_across_1"),
        (add(to_end[half:], far_1_middle_0[:half]), ends_out, "rows_far_out_1"),
    )
    late = units((jnp.where(middle, inward, out_2), jnp.where(middle, cross_2, out_3)), relatives[2:])
    totals = jnp.concatenate([early[:, 0], late[:, 0]])
    early = swap(after(early[:, 1].astype(jnp.bfloat16), out_3), 1, "returned_core_early")
    late = swap(late[:, 1].astype(jnp.bfloat16), 1, "returned_core_late")

    returned = jnp.zeros((4, tokens, width), jnp.bfloat16)
    for i, arrived in enumerate((early[0], early[1], late[0], late[1])):
        returned = lax.dynamic_update_slice_in_dim(returned, add(totals[i], arrived)[None], relatives[i], 0)
    moe_input_grad = returned[0].astype(jnp.float32)
    for relative in (1, 2, 3):
        moe_input_grad = moe_input_grad + swap(returned[relative], 2 * relative, "returned_plane").astype(jnp.float32)

    gradient = [
        jnp.where(middle, at_middle, at_end).astype(jnp.float32) + sum(part.astype(jnp.float32) for part in arrived)
        for at_middle, at_end, arrived in (
            (to_middle_1_near_0[half:], to_end[:half], (far_0, far_1_middle_0[half:], middle_1_near_0[half:])),
            (to_near_1, to_end[half:], (far_1, middle_1, near_1)),
        )
    ]
    query_weight_next = row_update(query_weight, jnp.concatenate(gradient, axis=0))
    return (query_weight_next, moe_input_grad)


def solution(mesh):
    placed = (
        P("dp", None),
        P("dp", "expert"),
        P(("expert", "dp"), None),
        P("expert", "dp"),
        P("expert", None),
        P("expert", None),
        P("dp", "expert", None),
        P("dp", "expert", None),
        P("expert", "dp", None),
        P("expert", "dp", None),
        P("expert", None, "dp"),
    )
    return jax.shard_map(
        shards,
        mesh=mesh,
        in_specs=placed,
        out_specs=(P(("expert", "dp"), None), P("expert", "dp")),
        check_vma=False,
    )
```

```python
import jax
import jax.numpy as jnp
from jax import lax
from jax.sharding import PartitionSpec as P

step_rate = 0.01
epsilon = 1e-06

ends_in = [(0, 1), (3, 2)]
across = [(1, 2), (2, 1)]
ends_out = [(1, 0), (2, 3)]


class Line:
    def __init__(self):
        self.last = {}

    def hop(self, value, pairs, name, *first):
        key = tuple(pairs)
        first += (self.last[key],) if key in self.last else ()
        value = after(value, *first) if first else value
        with jax.named_scope(name):
            self.last[key] = lax.ppermute(value, "dp", pairs)
        return self.last[key]


def swap(value, bits, name):
    with jax.named_scope(name):
        return lax.ppermute(value, "expert", [(i, i ^ bits) for i in range(8)])


def after(value, *others):
    return lax.optimization_barrier((value,) + others)[0]


def pick(stack, index):
    return lax.dynamic_index_in_dim(stack, index, 0, keepdims=False)


def line_places():
    low = lax.axis_index("dp") < 2
    return [jnp.where(low, a, b) for a, b in ((0, 3), (1, 2), (2, 1), (3, 0))]


def on_middle():
    z = lax.axis_index("dp")
    return (z == 1) | (z == 2)


def activation_grads(hidden, gate_vals, up_vals):
    gate_float = gate_vals.astype(jnp.float32)
    up_float = up_vals.astype(jnp.float32)
    sigmoid_vals = jax.nn.sigmoid(gate_float)
    gate_grad = hidden * up_float * sigmoid_vals * (1.0 + gate_float * (1.0 - sigmoid_vals))
    up_grad = hidden * gate_float * sigmoid_vals
    return jnp.stack([gate_grad, up_grad], axis=0).astype(jnp.bfloat16)


def row_update(query_weight, gradient):
    radial = jnp.mean(query_weight * gradient, axis=1, keepdims=True) / (
        jnp.mean(query_weight * query_weight, axis=1, keepdims=True) + epsilon
    )
    stepped = query_weight - step_rate * (gradient - radial * query_weight)
    return stepped * lax.rsqrt(jnp.mean(stepped * stepped, axis=1, keepdims=True) + epsilon)


def three_terms(value):
    first = lax.reduce_precision(value, 8, 7)
    second = lax.reduce_precision(value - first, 8, 7)
    return first, second, value - first - second


def token_product(grads, inputs):
    return lax.dot_general(grads, inputs, (((0,), (0,)), ((), ())), preferred_element_type=jnp.float32)


def expert_tables(ids, weights, local, capacity):
    first = lax.axis_index("expert") * local
    experts = first + lax.broadcasted_iota(jnp.int32, (local, 1, 1), 0)
    hit = ids[..., None, :, :] == experts
    chosen = jnp.any(hit, axis=-2)
    token_weight = jnp.sum(jnp.where(hit, weights[..., None, :, :], 0.0), axis=-2)
    token = lax.broadcasted_iota(jnp.int32, (chosen.shape[-1],) * 2, 0)
    earlier = token < lax.broadcasted_iota(jnp.int32, token.shape, 1)
    position = jnp.dot(
        chosen.astype(jnp.bfloat16), earlier.astype(jnp.bfloat16), preferred_element_type=jnp.float32
    ).astype(jnp.int32)
    slot = jnp.where(chosen, position, -1)
    matched = slot[..., None, :] == lax.broadcasted_iota(jnp.int32, (capacity, 1), 0)
    slot_weight = jnp.sum(jnp.where(matched, token_weight[..., None, :], 0.0), axis=-1)
    return matched.astype(jnp.bfloat16), slot_weight


def slot_product(grads, gate_weight, up_weight):
    total = jnp.einsum("sh,ch->sc", grads[0], gate_weight, preferred_element_type=jnp.float32)
    total = total + jnp.einsum("sh,ch->sc", grads[1], up_weight, preferred_element_type=jnp.float32)
    return total.astype(jnp.bfloat16)


def general_weight_update(attn_input, query_grad, query_weight):
    gradient = lax.psum_scatter(
        token_product(query_grad, attn_input).astype(jnp.bfloat16), "dp", scatter_dimension=0, tiled=True
    ).astype(jnp.float32)
    return row_update(query_weight, gradient)


def general_expert_update(
    moe_cotangent, expert_ids, route_weights, gate_saved, up_saved, gate_weight, up_weight, down_weight
):
    groups = lax.axis_size("expert")
    local = gate_weight.shape[0]
    capacity = gate_saved.shape[0] * lax.axis_size("dp") // groups
    tokens, width = moe_cotangent.shape
    rows = lax.all_gather(moe_cotangent, "expert", axis=0, tiled=False)
    routing = jnp.stack([expert_ids.T.astype(jnp.float32), route_weights.T])
    routing = lax.all_gather(routing, "expert", axis=0, tiled=False)
    select, slot_weight = expert_tables(routing[:, 0].astype(jnp.int32), routing[:, 1], local, capacity)
    arrived = jnp.einsum("gect,gtd->egcd", select, rows, preferred_element_type=jnp.float32)
    arrived = (arrived * jnp.swapaxes(slot_weight, 0, 1)[..., None]).astype(jnp.bfloat16)
    total = 0.0
    for expert in range(local):
        flat = arrived[expert].reshape(groups * capacity, width)
        parts = jnp.einsum("sd,hd->sh", flat, down_weight[expert], preferred_element_type=jnp.float32)
        hidden = lax.psum_scatter(
            parts.astype(jnp.bfloat16), "dp", scatter_dimension=0, tiled=True
        ).astype(jnp.float32)
        grads = activation_grads(hidden, gate_saved[:, expert], up_saved[:, expert])
        grads = lax.all_gather(grads, "dp", axis=1, tiled=True)
        slot_input = slot_product(grads, gate_weight[expert], up_weight[expert])
        total = total + jnp.einsum(
            "gct,gcd->gtd",
            select[:, expert],
            slot_input.reshape(groups, capacity, width),
            preferred_element_type=jnp.float32,
        )
    return lax.psum_scatter(
        total.astype(jnp.bfloat16), "expert", scatter_dimension=0, tiled=False
    ).astype(jnp.float32)


def general(
    attn_input, query_grad, query_weight, moe_cotangent, expert_ids, route_weights,
    gate_saved, up_saved, gate_weight, up_weight, down_weight,
):
    moe_input_grad = general_expert_update(
        moe_cotangent, expert_ids, route_weights, gate_saved, up_saved, gate_weight, up_weight, down_weight
    )
    return general_weight_update(attn_input, query_grad, query_weight), moe_input_grad


def line_sources():
    own_end, own_middle, other_middle, other_end = line_places()
    middle = on_middle()
    return (
        jnp.where(middle, other_middle, own_middle),
        jnp.where(middle, own_end, other_middle),
        other_end,
    )


def shards(
    attn_input, query_grad, query_weight, moe_cotangent, expert_ids, route_weights,
    gate_saved, up_saved, gate_weight, up_weight, down_weight,
):
    if (lax.axis_size("expert"), lax.axis_size("dp")) != (8, 4):
        return general(
            attn_input, query_grad, query_weight, moe_cotangent, expert_ids, route_weights,
            gate_saved, up_saved, gate_weight, up_weight, down_weight,
        )
    z = lax.axis_index("dp")
    place = lax.axis_index("expert")
    chip, core = place // 2, place % 2
    own_end, own_middle, other_middle, other_end = line_places()
    middle = on_middle()
    local, width, hidden_units = gate_weight.shape
    tokens, top = expert_ids.shape
    per_dp = gate_saved.shape[0]
    capacity = per_dp // 2
    rows = query_weight.shape[0]
    half = rows // 2
    line = Line()

    pieces = jnp.stack([moe_cotangent] + [swap(moe_cotangent, bits, "tokens_plane") for bits in (2, 4, 6)])
    routing = [expert_ids.astype(jnp.float32)] + list(three_terms(route_weights))
    tables = jnp.stack([value.T for value in routing]).astype(jnp.bfloat16)
    tables = jnp.stack([tables, swap(tables, 2, "routing_x")])
    routed = tables
    tables = jnp.concatenate([tables, swap(tables, 4, "routing_y")])
    tables = jnp.stack([tables, swap(tables, 1, "routing_core")], axis=1).astype(jnp.float32)

    def product(places, *first):
        grads = [lax.dynamic_slice_in_dim(query_grad, index * rows + at * half, half, 1) for index, at in places]
        grads = jnp.concatenate(grads, axis=1)
        return token_product(after(grads, *first) if first else grads, attn_input).astype(jnp.bfloat16)

    def add(a, b):
        return (a.astype(jnp.float32) + b.astype(jnp.float32)).astype(jnp.bfloat16)

    to_far_0 = product([(other_end, 0)], routed)
    far_0 = line.hop(to_far_0, ends_in, "rows_far_in_0")

    cotangents = (pieces, swap(pieces, 1, "tokens_core"))
    weights = tables[:, :, 1] + tables[:, :, 2] + tables[:, :, 3]
    select, slot_weight = expert_tables(tables[:, :, 0].astype(jnp.int32), weights, local, capacity)
    parts = []
    for expert in range(local):
        arrived = jnp.stack(
            [
                jnp.einsum(
                    "gct,gtd->gcd", select[:, i, expert], cotangents[i], preferred_element_type=jnp.float32
                )
                * slot_weight[:, i, expert, :, None]
                for i in range(2)
            ],
            axis=1,
        ).astype(jnp.bfloat16)
        part = jnp.einsum(
            "sd,hd->sh",
            arrived.reshape(4 * per_dp, width),
            down_weight[expert],
            preferred_element_type=jnp.float32,
        )
        parts.append(part.astype(jnp.bfloat16).reshape(4, per_dp, hidden_units))

    def block(index):
        return jnp.stack([pick(part, index ^ chip) for part in parts])

    def saved(array):
        blocks = jnp.swapaxes(array, 0, 1).reshape(local, 2, capacity, hidden_units)
        return jnp.where(core == 0, blocks, blocks[:, ::-1]).reshape(local, per_dp, hidden_units)

    to_end = product([(own_end, 0), (own_end, 1)], far_0)
    sum_far = line.hop(block(other_end), ends_in, "sum_far_in")
    far_0 = line.hop(add(to_far_0, far_0), across, "rows_far_across_0")
    saved_pair = [saved(after(array, far_0)) for array in (gate_saved, up_saved)]
    to_far_1_middle_0 = product([(other_end, 1), (other_middle, 0)], sum_far)
    sum_middle = line.hop(block(other_middle), ends_in, "sum_middle_in")
    sum_far = line.hop(add(block(other_end), sum_far), across, "sum_far_across")
    far_0 = line.hop(add(to_end[:half], far_0), ends_out, "rows_far_out_0")
    to_middle_1_near_0 = product([(other_middle, 1), (own_middle, 0)], sum_far)
    sum_near = line.hop(block(own_middle), ends_in, "sum_near_in")
    sum_middle = line.hop(add(block(other_middle), sum_middle), across, "sum_middle_across")
    sum_far = line.hop(add(block(own_end), sum_far), ends_out, "sum_far_out")
    to_near_1 = product([(own_middle, 1)], sum_near)
    hidden = block(z).astype(jnp.float32) + sum_far.astype(jnp.float32)
    hidden = hidden + sum_middle.astype(jnp.float32) + sum_near.astype(jnp.float32)
    grads = activation_grads(hidden, *saved_pair)

    sources = (z,) + line_sources()
    relatives = [source ^ chip for source in sources]

    def units(values, places):
        values = jnp.concatenate(values, axis=2)
        chosen = jnp.stack([pick(select, index) for index in places])
        total = 0.0
        for expert in range(local):
            slot_input = slot_product(values[:, expert], gate_weight[expert], up_weight[expert])
            total = total + jnp.einsum(
                "ugct,ugcd->ugtd",
                chosen[:, :, expert],
                slot_input.reshape(2, 2, capacity, width),
                preferred_element_type=jnp.float32,
            )
        return total

    out_1 = line.hop(grads, ends_out, "grads_out_1", to_far_1_middle_0, to_middle_1_near_0)
    cross_1 = line.hop(grads, across, "grads_across_1")
    inward = line.hop(grads, ends_in, "grads_in")
    out_2 = line.hop(cross_1, ends_out, "grads_out_2")
    cross_2 = line.hop(inward, across, "grads_across_2")
    far_1_middle_0_in = line.hop(to_far_1_middle_0, ends_in, "rows_far_1_middle_0_in")
    early = units((grads, jnp.where(middle, cross_1, out_1)), relatives[:2])
    out_3 = line.hop(cross_2, ends_out, "grads_out_3", early)
    far_1_middle_0 = line.hop(
        add(to_far_1_middle_0, far_1_middle_0_in), across, "rows_far_1_middle_0_across"
    )
    middle_1_near_0 = line.hop(to_middle_1_near_0, ends_in, "rows_middle_1_near_0_in")
    far_1 = line.hop(add(to_end[half:], far_1_middle_0[:half]), ends_out, "rows_far_out_1")
    middle_1 = line.hop(
        add(to_middle_1_near_0[:half], middle_1_near_0[:half]), across, "rows_middle_across_1"
    )
    near_1 = line.hop(to_near_1, ends_in, "rows_near_in_1")
    late = units((jnp.where(middle, inward, out_2), jnp.where(middle, cross_2, out_3)), relatives[2:])
    totals = jnp.concatenate([early[:, 0], late[:, 0]])
    early = swap(after(early[:, 1].astype(jnp.bfloat16), out_3), 1, "returned_core_early")
    late = swap(late[:, 1].astype(jnp.bfloat16), 1, "returned_core_late")

    returned = jnp.zeros((4, tokens, width), jnp.bfloat16)
    for i, arrived in enumerate((early[0], early[1], late[0], late[1])):
        returned = lax.dynamic_update_slice_in_dim(returned, add(totals[i], arrived)[None], relatives[i], 0)
    moe_input_grad = returned[0].astype(jnp.float32)
    for relative in (1, 2, 3):
        moe_input_grad = moe_input_grad + swap(returned[relative], 2 * relative, "returned_plane").astype(jnp.float32)

    gradient = [
        jnp.where(middle, at_middle, at_end).astype(jnp.float32) + sum(part.astype(jnp.float32) for part in arrived)
        for at_middle, at_end, arrived in (
            (to_middle_1_near_0[half:], to_end[:half], (far_0, far_1_middle_0[half:], middle_1_near_0[half:])),
            (to_near_1, to_end[half:], (far_1, middle_1, near_1)),
        )
    ]
    query_weight_next = row_update(query_weight, jnp.concatenate(gradient, axis=0))
    return (query_weight_next, moe_input_grad)


def solution(mesh):
    placed = (
        P("dp", None),
        P("dp", "expert"),
        P(("expert", "dp"), None),
        P("expert", "dp"),
        P("expert", None),
        P("expert", None),
        P("dp", "expert", None),
        P("dp", "expert", None),
        P("expert", "dp", None),
        P("expert", "dp", None),
        P("expert", None, "dp"),
    )
    return jax.shard_map(
        shards,
        mesh=mesh,
        in_specs=placed,
        out_specs=(P(("expert", "dp"), None), P("expert", "dp")),
        check_vma=False,
    )
```

```python
import jax
import jax.numpy as jnp
from jax import lax
from jax.sharding import PartitionSpec as P

step_rate = 0.01
epsilon = 1e-06

ends_in = [(0, 1), (3, 2)]
across = [(1, 2), (2, 1)]
ends_out = [(1, 0), (2, 3)]


class Line:
    def __init__(self):
        self.last = {}

    def hop(self, value, pairs, name, *first):
        key = tuple(pairs)
        first += (self.last[key],) if key in self.last else ()
        value = after(value, *first) if first else value
        with jax.named_scope(name):
            self.last[key] = lax.ppermute(value, "dp", pairs)
        return self.last[key]


def swap(value, bits, name):
    with jax.named_scope(name):
        return lax.ppermute(value, "expert", [(i, i ^ bits) for i in range(8)])


def after(value, *others):
    return lax.optimization_barrier((value,) + others)[0]


def pick(stack, index):
    return lax.dynamic_index_in_dim(stack, index, 0, keepdims=False)


def line_places():
    low = lax.axis_index("dp") < 2
    return [jnp.where(low, a, b) for a, b in ((0, 3), (1, 2), (2, 1), (3, 0))]


def on_middle():
    z = lax.axis_index("dp")
    return (z == 1) | (z == 2)


def activation_grads(hidden, gate_vals, up_vals):
    gate_float = gate_vals.astype(jnp.float32)
    up_float = up_vals.astype(jnp.float32)
    sigmoid_vals = jax.nn.sigmoid(gate_float)
    gate_grad = hidden * up_float * sigmoid_vals * (1.0 + gate_float * (1.0 - sigmoid_vals))
    up_grad = hidden * gate_float * sigmoid_vals
    return jnp.stack([gate_grad, up_grad], axis=0).astype(jnp.bfloat16)


def row_update(query_weight, gradient):
    radial = jnp.mean(query_weight * gradient, axis=1, keepdims=True) / (
        jnp.mean(query_weight * query_weight, axis=1, keepdims=True) + epsilon
    )
    stepped = query_weight - step_rate * (gradient - radial * query_weight)
    return stepped * lax.rsqrt(jnp.mean(stepped * stepped, axis=1, keepdims=True) + epsilon)


def three_terms(value):
    first = lax.reduce_precision(value, 8, 7)
    second = lax.reduce_precision(value - first, 8, 7)
    return first, second, value - first - second


def token_product(grads, inputs):
    return lax.dot_general(grads, inputs, (((0,), (0,)), ((), ())), preferred_element_type=jnp.float32)


def expert_tables(ids, weights, local, capacity):
    first = lax.axis_index("expert") * local
    experts = first + lax.broadcasted_iota(jnp.int32, (local, 1, 1), 0)
    hit = ids[..., None, :, :] == experts
    chosen = jnp.any(hit, axis=-2)
    token_weight = jnp.sum(jnp.where(hit, weights[..., None, :, :], 0.0), axis=-2)
    token = lax.broadcasted_iota(jnp.int32, (chosen.shape[-1],) * 2, 0)
    earlier = token < lax.broadcasted_iota(jnp.int32, token.shape, 1)
    position = jnp.dot(
        chosen.astype(jnp.bfloat16), earlier.astype(jnp.bfloat16), preferred_element_type=jnp.float32
    ).astype(jnp.int32)
    slot = jnp.where(chosen, position, -1)
    matched = slot[..., None, :] == lax.broadcasted_iota(jnp.int32, (capacity, 1), 0)
    slot_weight = jnp.sum(jnp.where(matched, token_weight[..., None, :], 0.0), axis=-1)
    return matched.astype(jnp.bfloat16), slot_weight


def slot_product(grads, gate_weight, up_weight):
    total = jnp.einsum("sh,ch->sc", grads[0], gate_weight, preferred_element_type=jnp.float32)
    total = total + jnp.einsum("sh,ch->sc", grads[1], up_weight, preferred_element_type=jnp.float32)
    return total.astype(jnp.bfloat16)


def general_weight_update(attn_input, query_grad, query_weight):
    gradient = lax.psum_scatter(
        token_product(query_grad, attn_input).astype(jnp.bfloat16), "dp", scatter_dimension=0, tiled=True
    ).astype(jnp.float32)
    return row_update(query_weight, gradient)


def general_expert_update(
    moe_cotangent, expert_ids, route_weights, gate_saved, up_saved, gate_weight, up_weight, down_weight
):
    groups = lax.axis_size("expert")
    local = gate_weight.shape[0]
    capacity = gate_saved.shape[0] * lax.axis_size("dp") // groups
    tokens, width = moe_cotangent.shape
    rows = lax.all_gather(moe_cotangent, "expert", axis=0, tiled=False)
    routing = jnp.stack([expert_ids.T.astype(jnp.float32), route_weights.T])
    routing = lax.all_gather(routing, "expert", axis=0, tiled=False)
    select, slot_weight = expert_tables(routing[:, 0].astype(jnp.int32), routing[:, 1], local, capacity)
    arrived = jnp.einsum("gect,gtd->egcd", select, rows, preferred_element_type=jnp.float32)
    arrived = (arrived * jnp.swapaxes(slot_weight, 0, 1)[..., None]).astype(jnp.bfloat16)
    total = 0.0
    for expert in range(local):
        flat = arrived[expert].reshape(groups * capacity, width)
        parts = jnp.einsum("sd,hd->sh", flat, down_weight[expert], preferred_element_type=jnp.float32)
        hidden = lax.psum_scatter(
            parts.astype(jnp.bfloat16), "dp", scatter_dimension=0, tiled=True
        ).astype(jnp.float32)
        grads = activation_grads(hidden, gate_saved[:, expert], up_saved[:, expert])
        grads = lax.all_gather(grads, "dp", axis=1, tiled=True)
        slot_input = slot_product(grads, gate_weight[expert], up_weight[expert])
        total = total + jnp.einsum(
            "gct,gcd->gtd",
            select[:, expert],
            slot_input.reshape(groups, capacity, width),
            preferred_element_type=jnp.float32,
        )
    return lax.psum_scatter(
        total.astype(jnp.bfloat16), "expert", scatter_dimension=0, tiled=False
    ).astype(jnp.float32)


def general(
    attn_input, query_grad, query_weight, moe_cotangent, expert_ids, route_weights,
    gate_saved, up_saved, gate_weight, up_weight, down_weight,
):
    moe_input_grad = general_expert_update(
        moe_cotangent, expert_ids, route_weights, gate_saved, up_saved, gate_weight, up_weight, down_weight
    )
    return general_weight_update(attn_input, query_grad, query_weight), moe_input_grad


def line_sources():
    own_end, own_middle, other_middle, other_end = line_places()
    middle = on_middle()
    return (
        jnp.where(middle, other_middle, own_middle),
        jnp.where(middle, own_end, other_middle),
        other_end,
    )


def shards(
    attn_input, query_grad, query_weight, moe_cotangent, expert_ids, route_weights,
    gate_saved, up_saved, gate_weight, up_weight, down_weight,
):
    if (lax.axis_size("expert"), lax.axis_size("dp")) != (8, 4):
        return general(
            attn_input, query_grad, query_weight, moe_cotangent, expert_ids, route_weights,
            gate_saved, up_saved, gate_weight, up_weight, down_weight,
        )
    z = lax.axis_index("dp")
    place = lax.axis_index("expert")
    chip, core = place // 2, place % 2
    own_end, own_middle, other_middle, other_end = line_places()
    middle = on_middle()
    local, width, hidden_units = gate_weight.shape
    tokens, top = expert_ids.shape
    per_dp = gate_saved.shape[0]
    capacity = per_dp // 2
    rows = query_weight.shape[0]
    half = rows // 2
    line = Line()

    routing = [expert_ids.astype(jnp.float32)] + list(three_terms(route_weights))
    tables = jnp.stack([value.T for value in routing]).astype(jnp.bfloat16)
    tables = jnp.stack([tables, swap(tables, 2, "routing_x")])
    own_tokens = after(moe_cotangent, tables)
    pieces = jnp.stack([own_tokens] + [swap(own_tokens, bits, "tokens_plane") for bits in (2, 4, 6)])
    tables = jnp.concatenate([tables, swap(tables, 4, "routing_y")])
    routed = tables
    tables = jnp.stack([tables, swap(tables, 1, "routing_core")], axis=1).astype(jnp.float32)

    def product(places, *first):
        grads = [lax.dynamic_slice_in_dim(query_grad, index * rows + at * half, half, 1) for index, at in places]
        grads = jnp.concatenate(grads, axis=1)
        return token_product(after(grads, *first) if first else grads, attn_input).astype(jnp.bfloat16)

    def add(a, b):
        return (a.astype(jnp.float32) + b.astype(jnp.float32)).astype(jnp.bfloat16)

    to_far_0 = product([(other_end, 0)], routed)
    far_0 = line.hop(to_far_0, ends_in, "rows_far_in_0")

    cotangents = (pieces, swap(pieces, 1, "tokens_core"))
    weights = tables[:, :, 1] + tables[:, :, 2] + tables[:, :, 3]
    select, slot_weight = expert_tables(tables[:, :, 0].astype(jnp.int32), weights, local, capacity)
    parts = []
    for expert in range(local):
        arrived = jnp.stack(
            [
                jnp.einsum(
                    "gct,gtd->gcd", select[:, i, expert], cotangents[i], preferred_element_type=jnp.float32
                )
                * slot_weight[:, i, expert, :, None]
                for i in range(2)
            ],
            axis=1,
        ).astype(jnp.bfloat16)
        part = jnp.einsum(
            "sd,hd->sh",
            arrived.reshape(4 * per_dp, width),
            down_weight[expert],
            preferred_element_type=jnp.float32,
        )
        parts.append(part.astype(jnp.bfloat16).reshape(4, per_dp, hidden_units))

    def block(index):
        return jnp.stack([pick(part, index ^ chip) for part in parts])

    def saved(array):
        blocks = jnp.swapaxes(array, 0, 1).reshape(local, 2, capacity, hidden_units)
        return jnp.where(core == 0, blocks, blocks[:, ::-1]).reshape(local, per_dp, hidden_units)

    far_0 = line.last[tuple(ends_in)] = after(far_0, *parts)
    to_end = product([(own_end, 0), (own_end, 1)], far_0)
    sum_far = line.hop(block(other_end), ends_in, "sum_far_in")
    far_0 = line.hop(add(to_far_0, far_0), across, "rows_far_across_0")
    saved_pair = [saved(after(array, far_0)) for array in (gate_saved, up_saved)]
    to_far_1_middle_0 = product([(other_end, 1), (other_middle, 0)], sum_far)
    sum_middle = line.hop(block(other_middle), ends_in, "sum_middle_in")
    sum_far = line.hop(add(block(other_end), sum_far), across, "sum_far_across")
    far_0 = line.hop(add(to_end[:half], far_0), ends_out, "rows_far_out_0")
    to_middle_1 = product([(other_middle, 1)], sum_far)
    sum_near = line.hop(block(own_middle), ends_in, "sum_near_in")
    sum_middle = line.hop(add(block(other_middle), sum_middle), across, "sum_middle_across")
    sum_far = line.hop(add(block(own_end), sum_far), ends_out, "sum_far_out")
    hidden = block(z).astype(jnp.float32) + sum_far.astype(jnp.float32)
    hidden = hidden + sum_middle.astype(jnp.float32) + sum_near.astype(jnp.float32)
    grads = activation_grads(hidden, *saved_pair)

    sources = (z,) + line_sources()
    relatives = [source ^ chip for source in sources]

    def units(values, places):
        values = jnp.concatenate(values, axis=2)
        chosen = jnp.stack([pick(select, index) for index in places])
        total = 0.0
        for expert in range(local):
            slot_input = slot_product(values[:, expert], gate_weight[expert], up_weight[expert])
            total = total + jnp.einsum(
                "ugct,ugcd->ugtd",
                chosen[:, :, expert],
                slot_input.reshape(2, 2, capacity, width),
                preferred_element_type=jnp.float32,
            )
        return total

    out_1 = line.hop(grads, ends_out, "grads_out_1", to_far_1_middle_0, to_middle_1)
    cross_1 = line.hop(grads, across, "grads_across_1")
    inward = line.hop(grads, ends_in, "grads_in")
    to_near = product([(own_middle, 0), (own_middle, 1)], grads)
    out_2 = line.hop(cross_1, ends_out, "grads_out_2")
    cross_2 = line.hop(inward, across, "grads_across_2")
    far_1_middle_0_in = line.hop(to_far_1_middle_0, ends_in, "rows_far_1_middle_0_in")
    early = units((grads, jnp.where(middle, cross_1, out_1)), relatives[:2])
    out_3 = line.hop(cross_2, ends_out, "grads_out_3", early, to_near)
    far_1_middle_0 = line.hop(
        add(to_far_1_middle_0, far_1_middle_0_in), across, "rows_far_1_middle_0_across"
    )
    middle_1 = line.hop(to_middle_1, ends_in, "rows_middle_in_1")
    near = line.hop(to_near, ends_in, "rows_near_in")
    far_1 = line.hop(add(to_end[half:], far_1_middle_0[:half]), ends_out, "rows_far_out_1")
    middle_1 = line.hop(add(to_middle_1, middle_1), across, "rows_middle_across_1")
    late = units((jnp.where(middle, inward, out_2), jnp.where(middle, cross_2, out_3)), relatives[2:])
    totals = jnp.concatenate([early[:, 0], late[:, 0]])
    early = swap(after(early[:, 1].astype(jnp.bfloat16), out_3), 1, "returned_core_early")
    late = swap(late[:, 1].astype(jnp.bfloat16), 1, "returned_core_late")

    returned = jnp.zeros((4, tokens, width), jnp.bfloat16)
    for i, arrived in enumerate((early[0], early[1], late[0], late[1])):
        returned = lax.dynamic_update_slice_in_dim(returned, add(totals[i], arrived)[None], relatives[i], 0)
    moe_input_grad = returned[0].astype(jnp.float32)
    for relative in (1, 2, 3):
        moe_input_grad = moe_input_grad + swap(returned[relative], 2 * relative, "returned_plane").astype(jnp.float32)

    gradient = [
        jnp.where(middle, at_middle, at_end).astype(jnp.float32) + sum(part.astype(jnp.float32) for part in arrived)
        for at_middle, at_end, arrived in (
            (to_near[:half], to_end[:half], (far_0, far_1_middle_0[half:], near[:half])),
            (to_near[half:], to_end[half:], (far_1, middle_1, near[half:])),
        )
    ]
    query_weight_next = row_update(query_weight, jnp.concatenate(gradient, axis=0))
    return (query_weight_next, moe_input_grad)


def solution(mesh):
    placed = (
        P("dp", None),
        P("dp", "expert"),
        P(("expert", "dp"), None),
        P("expert", "dp"),
        P("expert", None),
        P("expert", None),
        P("dp", "expert", None),
        P("dp", "expert", None),
        P("expert", "dp", None),
        P("expert", "dp", None),
        P("expert", None, "dp"),
    )
    return jax.shard_map(
        shards,
        mesh=mesh,
        in_specs=placed,
        out_specs=(P(("expert", "dp"), None), P("expert", "dp")),
        check_vma=False,
    )
```

```python
import jax
import jax.numpy as jnp
from jax import lax
from jax.sharding import PartitionSpec as P

step_rate = 0.01
epsilon = 1e-06

ends_in = [(0, 1), (3, 2)]
across = [(1, 2), (2, 1)]
ends_out = [(1, 0), (2, 3)]


class Line:
    def __init__(self):
        self.last = {}

    def hop(self, value, pairs, name, *first):
        key = tuple(pairs)
        first += (self.last[key],) if key in self.last else ()
        value = after(value, *first) if first else value
        with jax.named_scope(name):
            self.last[key] = lax.ppermute(value, "dp", pairs)
        return self.last[key]


def swap(value, bits, name):
    with jax.named_scope(name):
        return lax.ppermute(value, "expert", [(i, i ^ bits) for i in range(8)])


def after(value, *others):
    return lax.optimization_barrier((value,) + others)[0]


def pick(stack, index):
    return lax.dynamic_index_in_dim(stack, index, 0, keepdims=False)


def line_places():
    low = lax.axis_index("dp") < 2
    return [jnp.where(low, a, b) for a, b in ((0, 3), (1, 2), (2, 1), (3, 0))]


def on_middle():
    z = lax.axis_index("dp")
    return (z == 1) | (z == 2)


def activation_grads(hidden, gate_vals, up_vals):
    gate_float = gate_vals.astype(jnp.float32)
    up_float = up_vals.astype(jnp.float32)
    sigmoid_vals = jax.nn.sigmoid(gate_float)
    gate_grad = hidden * up_float * sigmoid_vals * (1.0 + gate_float * (1.0 - sigmoid_vals))
    up_grad = hidden * gate_float * sigmoid_vals
    return jnp.stack([gate_grad, up_grad], axis=0).astype(jnp.bfloat16)


def row_update(query_weight, gradient):
    radial = jnp.mean(query_weight * gradient, axis=1, keepdims=True) / (
        jnp.mean(query_weight * query_weight, axis=1, keepdims=True) + epsilon
    )
    stepped = query_weight - step_rate * (gradient - radial * query_weight)
    return stepped * lax.rsqrt(jnp.mean(stepped * stepped, axis=1, keepdims=True) + epsilon)


def three_terms(value):
    first = lax.reduce_precision(value, 8, 7)
    second = lax.reduce_precision(value - first, 8, 7)
    return first, second, value - first - second


def token_product(grads, inputs):
    return lax.dot_general(grads, inputs, (((0,), (0,)), ((), ())), preferred_element_type=jnp.float32)


def expert_tables(ids, weights, local, capacity):
    first = lax.axis_index("expert") * local
    experts = first + lax.broadcasted_iota(jnp.int32, (local, 1, 1), 0)
    hit = ids[..., None, :, :] == experts
    chosen = jnp.any(hit, axis=-2)
    token_weight = jnp.sum(jnp.where(hit, weights[..., None, :, :], 0.0), axis=-2)
    token = lax.broadcasted_iota(jnp.int32, (chosen.shape[-1],) * 2, 0)
    earlier = token < lax.broadcasted_iota(jnp.int32, token.shape, 1)
    position = jnp.dot(
        chosen.astype(jnp.bfloat16), earlier.astype(jnp.bfloat16), preferred_element_type=jnp.float32
    ).astype(jnp.int32)
    slot = jnp.where(chosen, position, -1)
    matched = slot[..., None, :] == lax.broadcasted_iota(jnp.int32, (capacity, 1), 0)
    slot_weight = jnp.sum(jnp.where(matched, token_weight[..., None, :], 0.0), axis=-1)
    return matched.astype(jnp.bfloat16), slot_weight


def slot_product(grads, gate_weight, up_weight):
    total = jnp.einsum("sh,ch->sc", grads[0], gate_weight, preferred_element_type=jnp.float32)
    total = total + jnp.einsum("sh,ch->sc", grads[1], up_weight, preferred_element_type=jnp.float32)
    return total.astype(jnp.bfloat16)


def general_weight_update(attn_input, query_grad, query_weight):
    gradient = lax.psum_scatter(
        token_product(query_grad, attn_input).astype(jnp.bfloat16), "dp", scatter_dimension=0, tiled=True
    ).astype(jnp.float32)
    return row_update(query_weight, gradient)


def general_expert_update(
    moe_cotangent, expert_ids, route_weights, gate_saved, up_saved, gate_weight, up_weight, down_weight
):
    groups = lax.axis_size("expert")
    local = gate_weight.shape[0]
    capacity = gate_saved.shape[0] * lax.axis_size("dp") // groups
    tokens, width = moe_cotangent.shape
    rows = lax.all_gather(moe_cotangent, "expert", axis=0, tiled=False)
    routing = jnp.stack([expert_ids.T.astype(jnp.float32), route_weights.T])
    routing = lax.all_gather(routing, "expert", axis=0, tiled=False)
    select, slot_weight = expert_tables(routing[:, 0].astype(jnp.int32), routing[:, 1], local, capacity)
    arrived = jnp.einsum("gect,gtd->egcd", select, rows, preferred_element_type=jnp.float32)
    arrived = (arrived * jnp.swapaxes(slot_weight, 0, 1)[..., None]).astype(jnp.bfloat16)
    total = 0.0
    for expert in range(local):
        flat = arrived[expert].reshape(groups * capacity, width)
        parts = jnp.einsum("sd,hd->sh", flat, down_weight[expert], preferred_element_type=jnp.float32)
        hidden = lax.psum_scatter(
            parts.astype(jnp.bfloat16), "dp", scatter_dimension=0, tiled=True
        ).astype(jnp.float32)
        grads = activation_grads(hidden, gate_saved[:, expert], up_saved[:, expert])
        grads = lax.all_gather(grads, "dp", axis=1, tiled=True)
        slot_input = slot_product(grads, gate_weight[expert], up_weight[expert])
        total = total + jnp.einsum(
            "gct,gcd->gtd",
            select[:, expert],
            slot_input.reshape(groups, capacity, width),
            preferred_element_type=jnp.float32,
        )
    return lax.psum_scatter(
        total.astype(jnp.bfloat16), "expert", scatter_dimension=0, tiled=False
    ).astype(jnp.float32)


def general(
    attn_input, query_grad, query_weight, moe_cotangent, expert_ids, route_weights,
    gate_saved, up_saved, gate_weight, up_weight, down_weight,
):
    moe_input_grad = general_expert_update(
        moe_cotangent, expert_ids, route_weights, gate_saved, up_saved, gate_weight, up_weight, down_weight
    )
    return general_weight_update(attn_input, query_grad, query_weight), moe_input_grad


def line_sources():
    own_end, own_middle, other_middle, other_end = line_places()
    middle = on_middle()
    return (
        jnp.where(middle, other_middle, own_middle),
        jnp.where(middle, own_end, other_middle),
        other_end,
    )


def shards(
    attn_input, query_grad, query_weight, moe_cotangent, expert_ids, route_weights,
    gate_saved, up_saved, gate_weight, up_weight, down_weight,
):
    if (lax.axis_size("expert"), lax.axis_size("dp")) != (8, 4):
        return general(
            attn_input, query_grad, query_weight, moe_cotangent, expert_ids, route_weights,
            gate_saved, up_saved, gate_weight, up_weight, down_weight,
        )
    z = lax.axis_index("dp")
    place = lax.axis_index("expert")
    chip, core = place // 2, place % 2
    own_end, own_middle, other_middle, other_end = line_places()
    middle = on_middle()
    local, width, hidden_units = gate_weight.shape
    tokens, top = expert_ids.shape
    per_dp = gate_saved.shape[0]
    capacity = per_dp // 2
    rows = query_weight.shape[0]
    cut = rows * 5 // 8
    line = Line()

    def product(index, start, stop, *first):
        grads = lax.dynamic_slice_in_dim(query_grad, index * rows + start, stop - start, 1)
        return token_product(after(grads, *first) if first else grads, attn_input).astype(jnp.bfloat16)

    def add(a, b):
        return (a.astype(jnp.float32) + b.astype(jnp.float32)).astype(jnp.bfloat16)

    to_far_0 = product(other_end, 0, cut)

    routing = [expert_ids.astype(jnp.float32)] + list(three_terms(route_weights))
    tables = jnp.stack([value.T for value in routing]).astype(jnp.bfloat16)
    tables = after(jnp.stack([tables, swap(tables, 2, "routing_x")]), to_far_0)
    own_tokens = after(moe_cotangent, tables)
    pieces = jnp.stack([own_tokens] + [swap(own_tokens, bits, "tokens_plane") for bits in (2, 4, 6)])
    tables = jnp.concatenate([tables, swap(tables, 4, "routing_y")])
    tables = jnp.stack([tables, swap(tables, 1, "routing_core")], axis=1).astype(jnp.float32)

    far_0 = line.hop(to_far_0, ends_in, "rows_far_in_0")

    cotangents = (pieces, swap(pieces, 1, "tokens_core"))
    weights = tables[:, :, 1] + tables[:, :, 2] + tables[:, :, 3]
    select, slot_weight = expert_tables(tables[:, :, 0].astype(jnp.int32), weights, local, capacity)
    parts = []
    for expert in range(local):
        arrived = jnp.stack(
            [
                jnp.einsum(
                    "gct,gtd->gcd", select[:, i, expert], cotangents[i], preferred_element_type=jnp.float32
                )
                * slot_weight[:, i, expert, :, None]
                for i in range(2)
            ],
            axis=1,
        ).astype(jnp.bfloat16)
        part = jnp.einsum(
            "sd,hd->sh",
            arrived.reshape(4 * per_dp, width),
            down_weight[expert],
            preferred_element_type=jnp.float32,
        )
        parts.append(part.astype(jnp.bfloat16).reshape(4, per_dp, hidden_units))

    def block(index):
        return jnp.stack([pick(part, index ^ chip) for part in parts])

    def saved(array):
        blocks = jnp.swapaxes(array, 0, 1).reshape(local, 2, capacity, hidden_units)
        return jnp.where(core == 0, blocks, blocks[:, ::-1]).reshape(local, per_dp, hidden_units)

    far_0 = line.last[tuple(ends_in)] = after(far_0, *parts)
    to_end = product(own_end, 0, rows, far_0)
    sum_far = line.hop(block(other_end), ends_in, "sum_far_in")
    far_0 = line.hop(add(to_far_0, far_0), across, "rows_far_across_0")
    saved_pair = [saved(after(array, far_0)) for array in (gate_saved, up_saved)]
    to_far_1 = product(other_end, cut, rows, sum_far)
    sum_middle = line.hop(block(other_middle), ends_in, "sum_middle_in")
    sum_far = line.hop(add(block(other_end), sum_far), across, "sum_far_across")
    far_0 = line.hop(add(to_end[:cut], far_0), ends_out, "rows_far_out_0")
    to_middle = product(other_middle, 0, rows, sum_far)
    sum_near = line.hop(block(own_middle), ends_in, "sum_near_in")
    sum_middle = line.hop(add(block(other_middle), sum_middle), across, "sum_middle_across")
    sum_far = line.hop(add(block(own_end), sum_far), ends_out, "sum_far_out")
    far_1 = line.hop(to_far_1, ends_in, "rows_far_in_1")
    hidden = block(z).astype(jnp.float32) + sum_far.astype(jnp.float32)
    hidden = hidden + sum_middle.astype(jnp.float32) + sum_near.astype(jnp.float32)
    grads = activation_grads(hidden, *saved_pair)

    sources = (z,) + line_sources()
    relatives = [source ^ chip for source in sources]

    def units(values, places):
        values = jnp.concatenate(values, axis=2)
        chosen = jnp.stack([pick(select, index) for index in places])
        total = 0.0
        for expert in range(local):
            slot_input = slot_product(values[:, expert], gate_weight[expert], up_weight[expert])
            total = total + jnp.einsum(
                "ugct,ugcd->ugtd",
                chosen[:, :, expert],
                slot_input.reshape(2, 2, capacity, width),
                preferred_element_type=jnp.float32,
            )
        return total

    out_1 = line.hop(grads, ends_out, "grads_out_1", to_middle)
    cross_1 = line.hop(grads, across, "grads_across_1")
    inward = line.hop(grads, ends_in, "grads_in")
    to_near = product(own_middle, 0, rows, grads)
    out_2 = line.hop(cross_1, ends_out, "grads_out_2")
    cross_2 = line.hop(inward, across, "grads_across_2")
    middle_in = line.hop(to_middle, ends_in, "rows_middle_in")
    early = (grads, jnp.where(middle, cross_1, out_1))
    early = units([after(value, out_2, cross_2) for value in early], relatives[:2])
    out_3 = line.hop(cross_2, ends_out, "grads_out_3", to_near)
    both = jnp.concatenate([add(to_far_1, far_1), add(to_middle[:cut], middle_in[:cut])])
    both = line.hop(both, across, "rows_far_1_middle_0_across")
    far_1, middle_0 = both[: rows - cut], both[rows - cut :]
    near = line.hop(to_near, ends_in, "rows_near_in")
    middle_1 = line.hop(add(to_middle[cut:], middle_in[cut:]), across, "rows_middle_across_1")
    far_1 = line.hop(add(to_end[cut:], far_1), ends_out, "rows_far_out_1")
    late = units((jnp.where(middle, inward, out_2), jnp.where(middle, cross_2, out_3)), relatives[2:])
    totals = jnp.concatenate([early[:, 0], late[:, 0]])
    early = swap(after(early[:, 1].astype(jnp.bfloat16), out_3), 1, "returned_core_early")
    late = swap(late[:, 1].astype(jnp.bfloat16), 1, "returned_core_late")
    late = after(late, both)

    returned = jnp.zeros((4, tokens, width), jnp.bfloat16)
    for i, arrived in enumerate((early[0], early[1], late[0], late[1])):
        returned = lax.dynamic_update_slice_in_dim(returned, add(totals[i], arrived)[None], relatives[i], 0)
    moe_input_grad = returned[0].astype(jnp.float32)
    for relative in (1, 2, 3):
        moe_input_grad = moe_input_grad + swap(returned[relative], 2 * relative, "returned_plane").astype(jnp.float32)

    gradient = jnp.where(middle, to_near, to_end).astype(jnp.float32) + jnp.concatenate([far_0, far_1]).astype(jnp.float32)
    gradient = gradient + jnp.concatenate([middle_0, middle_1]).astype(jnp.float32) + near.astype(jnp.float32)
    query_weight_next = row_update(query_weight, gradient)
    return (query_weight_next, moe_input_grad)


def solution(mesh):
    placed = (
        P("dp", None),
        P("dp", "expert"),
        P(("expert", "dp"), None),
        P("expert", "dp"),
        P("expert", None),
        P("expert", None),
        P("dp", "expert", None),
        P("dp", "expert", None),
        P("expert", "dp", None),
        P("expert", "dp", None),
        P("expert", None, "dp"),
    )
    return jax.shard_map(
        shards,
        mesh=mesh,
        in_specs=placed,
        out_specs=(P(("expert", "dp"), None), P("expert", "dp")),
        check_vma=False,
    )
```

```python
import jax
import jax.numpy as jnp
from jax import lax
from jax.sharding import PartitionSpec as P

step_rate = 0.01
epsilon = 1e-06

ends_in = [(0, 1), (3, 2)]
across = [(1, 2), (2, 1)]
ends_out = [(1, 0), (2, 3)]


class Line:
    def __init__(self):
        self.last = {}

    def hop(self, value, pairs, name, *first):
        key = tuple(pairs)
        first += (self.last[key],) if key in self.last else ()
        value = after(value, *first) if first else value
        with jax.named_scope(name):
            self.last[key] = lax.ppermute(value, "dp", pairs)
        return self.last[key]


def swap(value, bits, name):
    with jax.named_scope(name):
        return lax.ppermute(value, "expert", [(i, i ^ bits) for i in range(8)])


def after(value, *others):
    return lax.optimization_barrier((value,) + others)[0]


def pick(stack, index):
    return lax.dynamic_index_in_dim(stack, index, 0, keepdims=False)


def line_places():
    low = lax.axis_index("dp") < 2
    return [jnp.where(low, a, b) for a, b in ((0, 3), (1, 2), (2, 1), (3, 0))]


def on_middle():
    z = lax.axis_index("dp")
    return (z == 1) | (z == 2)


def activation_grads(hidden, gate_vals, up_vals):
    gate_float = gate_vals.astype(jnp.float32)
    up_float = up_vals.astype(jnp.float32)
    sigmoid_vals = jax.nn.sigmoid(gate_float)
    gate_grad = hidden * up_float * sigmoid_vals * (1.0 + gate_float * (1.0 - sigmoid_vals))
    up_grad = hidden * gate_float * sigmoid_vals
    return jnp.stack([gate_grad, up_grad], axis=0).astype(jnp.bfloat16)


def row_update(query_weight, gradient):
    radial = jnp.mean(query_weight * gradient, axis=1, keepdims=True) / (
        jnp.mean(query_weight * query_weight, axis=1, keepdims=True) + epsilon
    )
    stepped = query_weight - step_rate * (gradient - radial * query_weight)
    return stepped * lax.rsqrt(jnp.mean(stepped * stepped, axis=1, keepdims=True) + epsilon)


def three_terms(value):
    first = lax.reduce_precision(value, 8, 7)
    second = lax.reduce_precision(value - first, 8, 7)
    return first, second, value - first - second


def token_product(grads, inputs):
    return lax.dot_general(grads, inputs, (((0,), (0,)), ((), ())), preferred_element_type=jnp.float32)


def expert_tables(ids, weights, local, capacity):
    first = lax.axis_index("expert") * local
    experts = first + lax.broadcasted_iota(jnp.int32, (local, 1, 1), 0)
    hit = ids[..., None, :, :] == experts
    chosen = jnp.any(hit, axis=-2)
    token_weight = jnp.sum(jnp.where(hit, weights[..., None, :, :], 0.0), axis=-2)
    token = lax.broadcasted_iota(jnp.int32, (chosen.shape[-1],) * 2, 0)
    earlier = token < lax.broadcasted_iota(jnp.int32, token.shape, 1)
    position = jnp.dot(
        chosen.astype(jnp.bfloat16), earlier.astype(jnp.bfloat16), preferred_element_type=jnp.float32
    ).astype(jnp.int32)
    slot = jnp.where(chosen, position, -1)
    matched = slot[..., None, :] == lax.broadcasted_iota(jnp.int32, (capacity, 1), 0)
    slot_weight = jnp.sum(jnp.where(matched, token_weight[..., None, :], 0.0), axis=-1)
    return matched.astype(jnp.bfloat16), slot_weight


def slot_product(grads, gate_weight, up_weight):
    total = jnp.einsum("sh,ch->sc", grads[0], gate_weight, preferred_element_type=jnp.float32)
    total = total + jnp.einsum("sh,ch->sc", grads[1], up_weight, preferred_element_type=jnp.float32)
    return total.astype(jnp.bfloat16)


def general_weight_update(attn_input, query_grad, query_weight):
    gradient = lax.psum_scatter(
        token_product(query_grad, attn_input).astype(jnp.bfloat16), "dp", scatter_dimension=0, tiled=True
    ).astype(jnp.float32)
    return row_update(query_weight, gradient)


def general_expert_update(
    moe_cotangent, expert_ids, route_weights, gate_saved, up_saved, gate_weight, up_weight, down_weight
):
    groups = lax.axis_size("expert")
    local = gate_weight.shape[0]
    capacity = gate_saved.shape[0] * lax.axis_size("dp") // groups
    tokens, width = moe_cotangent.shape
    rows = lax.all_gather(moe_cotangent, "expert", axis=0, tiled=False)
    routing = jnp.stack([expert_ids.T.astype(jnp.float32), route_weights.T])
    routing = lax.all_gather(routing, "expert", axis=0, tiled=False)
    select, slot_weight = expert_tables(routing[:, 0].astype(jnp.int32), routing[:, 1], local, capacity)
    arrived = jnp.einsum("gect,gtd->egcd", select, rows, preferred_element_type=jnp.float32)
    arrived = (arrived * jnp.swapaxes(slot_weight, 0, 1)[..., None]).astype(jnp.bfloat16)
    total = 0.0
    for expert in range(local):
        flat = arrived[expert].reshape(groups * capacity, width)
        parts = jnp.einsum("sd,hd->sh", flat, down_weight[expert], preferred_element_type=jnp.float32)
        hidden = lax.psum_scatter(
            parts.astype(jnp.bfloat16), "dp", scatter_dimension=0, tiled=True
        ).astype(jnp.float32)
        grads = activation_grads(hidden, gate_saved[:, expert], up_saved[:, expert])
        grads = lax.all_gather(grads, "dp", axis=1, tiled=True)
        slot_input = slot_product(grads, gate_weight[expert], up_weight[expert])
        total = total + jnp.einsum(
            "gct,gcd->gtd",
            select[:, expert],
            slot_input.reshape(groups, capacity, width),
            preferred_element_type=jnp.float32,
        )
    return lax.psum_scatter(
        total.astype(jnp.bfloat16), "expert", scatter_dimension=0, tiled=False
    ).astype(jnp.float32)


def general(
    attn_input, query_grad, query_weight, moe_cotangent, expert_ids, route_weights,
    gate_saved, up_saved, gate_weight, up_weight, down_weight,
):
    moe_input_grad = general_expert_update(
        moe_cotangent, expert_ids, route_weights, gate_saved, up_saved, gate_weight, up_weight, down_weight
    )
    return general_weight_update(attn_input, query_grad, query_weight), moe_input_grad


def line_sources():
    own_end, own_middle, other_middle, other_end = line_places()
    middle = on_middle()
    return (
        jnp.where(middle, other_middle, own_middle),
        jnp.where(middle, own_end, other_middle),
        other_end,
    )


def shards(
    attn_input, query_grad, query_weight, moe_cotangent, expert_ids, route_weights,
    gate_saved, up_saved, gate_weight, up_weight, down_weight,
):
    if (lax.axis_size("expert"), lax.axis_size("dp")) != (8, 4):
        return general(
            attn_input, query_grad, query_weight, moe_cotangent, expert_ids, route_weights,
            gate_saved, up_saved, gate_weight, up_weight, down_weight,
        )
    z = lax.axis_index("dp")
    place = lax.axis_index("expert")
    chip, core = place // 2, place % 2
    own_end, own_middle, other_middle, other_end = line_places()
    middle = on_middle()
    local, width, hidden_units = gate_weight.shape
    tokens, top = expert_ids.shape
    per_dp = gate_saved.shape[0]
    capacity = per_dp // 2
    rows = query_weight.shape[0]
    half = rows // 2
    cut = rows * 3 // 4
    line = Line()

    routing = [expert_ids.astype(jnp.float32)] + list(three_terms(route_weights))
    tables = jnp.stack([value.T for value in routing]).astype(jnp.bfloat16)
    tables = jnp.stack([tables, swap(tables, 2, "routing_x")])
    own_tokens = after(moe_cotangent, tables)
    pieces = jnp.stack([own_tokens] + [swap(own_tokens, bits, "tokens_plane") for bits in (2, 4, 6)])
    tables = jnp.concatenate([tables, swap(tables, 4, "routing_y")])
    routed = tables
    tables = jnp.stack([tables, swap(tables, 1, "routing_core")], axis=1).astype(jnp.float32)

    def product(places, *first):
        grads = [
            lax.dynamic_slice_in_dim(query_grad, index * rows + start, stop - start, 1) for index, start, stop in places
        ]
        grads = jnp.concatenate(grads, axis=1)
        return token_product(after(grads, *first) if first else grads, attn_input).astype(jnp.bfloat16)

    def add(a, b):
        return (a.astype(jnp.float32) + b.astype(jnp.float32)).astype(jnp.bfloat16)

    to_far_0 = product([(other_end, 0, half)], routed)
    far_0 = line.hop(to_far_0, ends_in, "rows_far_in_0")

    cotangents = (pieces, swap(pieces, 1, "tokens_core"))
    weights = tables[:, :, 1] + tables[:, :, 2] + tables[:, :, 3]
    select, slot_weight = expert_tables(tables[:, :, 0].astype(jnp.int32), weights, local, capacity)
    parts = []
    for expert in range(local):
        arrived = jnp.stack(
            [
                jnp.einsum(
                    "gct,gtd->gcd", select[:, i, expert], cotangents[i], preferred_element_type=jnp.float32
                )
                * slot_weight[:, i, expert, :, None]
                for i in range(2)
            ],
            axis=1,
        ).astype(jnp.bfloat16)
        part = jnp.einsum(
            "sd,hd->sh",
            arrived.reshape(4 * per_dp, width),
            down_weight[expert],
            preferred_element_type=jnp.float32,
        )
        parts.append(part.astype(jnp.bfloat16).reshape(4, per_dp, hidden_units))

    def block(index):
        return jnp.stack([pick(part, index ^ chip) for part in parts])

    def saved(array):
        blocks = jnp.swapaxes(array, 0, 1).reshape(local, 2, capacity, hidden_units)
        return jnp.where(core == 0, blocks, blocks[:, ::-1]).reshape(local, per_dp, hidden_units)

    far_0 = line.last[tuple(ends_in)] = after(far_0, *parts)
    to_end = product([(own_end, 0, rows)], far_0)
    sum_far = line.hop(block(other_end), ends_in, "sum_far_in")
    far_0 = line.hop(add(to_far_0, far_0), across, "rows_far_across_0")
    saved_pair = [saved(after(array, far_0)) for array in (gate_saved, up_saved)]
    to_far_1 = product([(other_end, half, cut)], sum_far)
    to_far_2_middle_0 = product([(other_end, cut, rows), (other_middle, 0, half)], sum_far)
    sum_middle = line.hop(block(other_middle), ends_in, "sum_middle_in")
    sum_far = line.hop(add(block(other_end), sum_far), across, "sum_far_across")
    far_0 = line.hop(add(to_end[:half], far_0), ends_out, "rows_far_out_0")
    to_middle_1 = product([(other_middle, half, rows)], sum_far)
    sum_near = line.hop(block(own_middle), ends_in, "sum_near_in", to_far_1)
    sum_middle = line.hop(add(block(other_middle), sum_middle), across, "sum_middle_across")
    sum_far = line.hop(add(block(own_end), sum_far), ends_out, "sum_far_out")
    far_1 = line.hop(to_far_1, ends_in, "rows_far_in_1")
    hidden = block(z).astype(jnp.float32) + sum_far.astype(jnp.float32)
    hidden = hidden + sum_middle.astype(jnp.float32) + sum_near.astype(jnp.float32)
    grads = activation_grads(hidden, *saved_pair)

    sources = (z,) + line_sources()
    relatives = [source ^ chip for source in sources]

    def units(values, places):
        values = jnp.concatenate(values, axis=2)
        chosen = jnp.stack([pick(select, index) for index in places])
        total = 0.0
        for expert in range(local):
            slot_input = slot_product(values[:, expert], gate_weight[expert], up_weight[expert])
            total = total + jnp.einsum(
                "ugct,ugcd->ugtd",
                chosen[:, :, expert],
                slot_input.reshape(2, 2, capacity, width),
                preferred_element_type=jnp.float32,
            )
        return total

    out_1 = line.hop(grads, ends_out, "grads_out_1", to_far_2_middle_0, to_middle_1)
    cross_1 = line.hop(grads, across, "grads_across_1")
    inward = line.hop(grads, ends_in, "grads_in")
    to_near = product([(own_middle, 0, rows)], grads)
    out_2 = line.hop(cross_1, ends_out, "grads_out_2")
    cross_2 = line.hop(inward, across, "grads_across_2")
    far_2_middle_0 = line.hop(to_far_2_middle_0, ends_in, "rows_far_2_middle_0_in")
    early = units((grads, jnp.where(middle, cross_1, out_1)), relatives[:2])
    out_3 = line.hop(cross_2, ends_out, "grads_out_3", early, to_near)
    far_1_middle_0 = jnp.concatenate([add(to_far_1, far_1), add(to_far_2_middle_0, far_2_middle_0)])
    far_1_middle_0 = line.hop(far_1_middle_0, across, "rows_far_1_middle_0_across")
    middle_1 = line.hop(to_middle_1, ends_in, "rows_middle_in_1")
    near = line.hop(to_near, ends_in, "rows_near_in")
    far_1 = line.hop(add(to_end[half:], far_1_middle_0[:half]), ends_out, "rows_far_out_1")
    middle_1 = line.hop(add(to_middle_1, middle_1), across, "rows_middle_across_1")
    late = units((jnp.where(middle, inward, out_2), jnp.where(middle, cross_2, out_3)), relatives[2:])
    totals = jnp.concatenate([early[:, 0], late[:, 0]])
    early = swap(after(early[:, 1].astype(jnp.bfloat16), out_3), 1, "returned_core_early")
    late = swap(late[:, 1].astype(jnp.bfloat16), 1, "returned_core_late")

    returned = jnp.zeros((4, tokens, width), jnp.bfloat16)
    for i, arrived in enumerate((early[0], early[1], late[0], late[1])):
        returned = lax.dynamic_update_slice_in_dim(returned, add(totals[i], arrived)[None], relatives[i], 0)
    moe_input_grad = returned[0].astype(jnp.float32)
    for relative in (1, 2, 3):
        moe_input_grad = moe_input_grad + swap(returned[relative], 2 * relative, "returned_plane").astype(jnp.float32)

    gradient = [
        jnp.where(middle, at_middle, at_end).astype(jnp.float32) + sum(part.astype(jnp.float32) for part in arrived)
        for at_middle, at_end, arrived in (
            (to_near[:half], to_end[:half], (far_0, far_1_middle_0[half:], near[:half])),
            (to_near[half:], to_end[half:], (far_1, middle_1, near[half:])),
        )
    ]
    query_weight_next = row_update(query_weight, jnp.concatenate(gradient, axis=0))
    return (query_weight_next, moe_input_grad)


def solution(mesh):
    placed = (
        P("dp", None),
        P("dp", "expert"),
        P(("expert", "dp"), None),
        P("expert", "dp"),
        P("expert", None),
        P("expert", None),
        P("dp", "expert", None),
        P("dp", "expert", None),
        P("expert", "dp", None),
        P("expert", "dp", None),
        P("expert", None, "dp"),
    )
    return jax.shard_map(
        shards,
        mesh=mesh,
        in_specs=placed,
        out_specs=(P(("expert", "dp"), None), P("expert", "dp")),
        check_vma=False,
    )
```

```python
import jax
import jax.numpy as jnp
from jax import lax
from jax.sharding import PartitionSpec as P

step_rate = 0.01
epsilon = 1e-06

ends_in = [(0, 1), (3, 2)]
across = [(1, 2), (2, 1)]
ends_out = [(1, 0), (2, 3)]


class Line:
    def __init__(self):
        self.last = {}

    def hop(self, value, pairs, name, *first):
        key = tuple(pairs)
        first += (self.last[key],) if key in self.last else ()
        value = after(value, *first) if first else value
        with jax.named_scope(name):
            self.last[key] = lax.ppermute(value, "dp", pairs)
        return self.last[key]


def swap(value, bits, name):
    with jax.named_scope(name):
        return lax.ppermute(value, "expert", [(i, i ^ bits) for i in range(8)])


def after(value, *others):
    return lax.optimization_barrier((value,) + others)[0]


def pick(stack, index):
    return lax.dynamic_index_in_dim(stack, index, 0, keepdims=False)


def line_places():
    low = lax.axis_index("dp") < 2
    return [jnp.where(low, a, b) for a, b in ((0, 3), (1, 2), (2, 1), (3, 0))]


def on_middle():
    z = lax.axis_index("dp")
    return (z == 1) | (z == 2)


def activation_grads(hidden, gate_vals, up_vals):
    gate_float = gate_vals.astype(jnp.float32)
    up_float = up_vals.astype(jnp.float32)
    sigmoid_vals = jax.nn.sigmoid(gate_float)
    gate_grad = hidden * up_float * sigmoid_vals * (1.0 + gate_float * (1.0 - sigmoid_vals))
    up_grad = hidden * gate_float * sigmoid_vals
    return jnp.stack([gate_grad, up_grad], axis=0).astype(jnp.bfloat16)


def row_update(query_weight, gradient):
    radial = jnp.mean(query_weight * gradient, axis=1, keepdims=True) / (
        jnp.mean(query_weight * query_weight, axis=1, keepdims=True) + epsilon
    )
    stepped = query_weight - step_rate * (gradient - radial * query_weight)
    return stepped * lax.rsqrt(jnp.mean(stepped * stepped, axis=1, keepdims=True) + epsilon)


def three_terms(value):
    first = lax.reduce_precision(value, 8, 7)
    second = lax.reduce_precision(value - first, 8, 7)
    return first, second, value - first - second


def token_product(grads, inputs):
    return lax.dot_general(grads, inputs, (((0,), (0,)), ((), ())), preferred_element_type=jnp.float32)


def expert_tables(ids, weights, local, capacity):
    first = lax.axis_index("expert") * local
    experts = first + lax.broadcasted_iota(jnp.int32, (local, 1, 1), 0)
    hit = ids[..., None, :, :] == experts
    chosen = jnp.any(hit, axis=-2)
    token_weight = jnp.sum(jnp.where(hit, weights[..., None, :, :], 0.0), axis=-2)
    token = lax.broadcasted_iota(jnp.int32, (chosen.shape[-1],) * 2, 0)
    earlier = token < lax.broadcasted_iota(jnp.int32, token.shape, 1)
    position = jnp.dot(
        chosen.astype(jnp.bfloat16), earlier.astype(jnp.bfloat16), preferred_element_type=jnp.float32
    ).astype(jnp.int32)
    slot = jnp.where(chosen, position, -1)
    matched = slot[..., None, :] == lax.broadcasted_iota(jnp.int32, (capacity, 1), 0)
    slot_weight = jnp.sum(jnp.where(matched, token_weight[..., None, :], 0.0), axis=-1)
    return matched.astype(jnp.bfloat16), slot_weight


def slot_product(grads, gate_weight, up_weight):
    total = jnp.einsum("sh,ch->sc", grads[0], gate_weight, preferred_element_type=jnp.float32)
    total = total + jnp.einsum("sh,ch->sc", grads[1], up_weight, preferred_element_type=jnp.float32)
    return total.astype(jnp.bfloat16)


def general_weight_update(attn_input, query_grad, query_weight):
    gradient = lax.psum_scatter(
        token_product(query_grad, attn_input).astype(jnp.bfloat16), "dp", scatter_dimension=0, tiled=True
    ).astype(jnp.float32)
    return row_update(query_weight, gradient)


def general_expert_update(
    moe_cotangent, expert_ids, route_weights, gate_saved, up_saved, gate_weight, up_weight, down_weight
):
    groups = lax.axis_size("expert")
    local = gate_weight.shape[0]
    capacity = gate_saved.shape[0] * lax.axis_size("dp") // groups
    tokens, width = moe_cotangent.shape
    rows = lax.all_gather(moe_cotangent, "expert", axis=0, tiled=False)
    routing = jnp.stack([expert_ids.T.astype(jnp.float32), route_weights.T])
    routing = lax.all_gather(routing, "expert", axis=0, tiled=False)
    select, slot_weight = expert_tables(routing[:, 0].astype(jnp.int32), routing[:, 1], local, capacity)
    arrived = jnp.einsum("gect,gtd->egcd", select, rows, preferred_element_type=jnp.float32)
    arrived = (arrived * jnp.swapaxes(slot_weight, 0, 1)[..., None]).astype(jnp.bfloat16)
    total = 0.0
    for expert in range(local):
        flat = arrived[expert].reshape(groups * capacity, width)
        parts = jnp.einsum("sd,hd->sh", flat, down_weight[expert], preferred_element_type=jnp.float32)
        hidden = lax.psum_scatter(
            parts.astype(jnp.bfloat16), "dp", scatter_dimension=0, tiled=True
        ).astype(jnp.float32)
        grads = activation_grads(hidden, gate_saved[:, expert], up_saved[:, expert])
        grads = lax.all_gather(grads, "dp", axis=1, tiled=True)
        slot_input = slot_product(grads, gate_weight[expert], up_weight[expert])
        total = total + jnp.einsum(
            "gct,gcd->gtd",
            select[:, expert],
            slot_input.reshape(groups, capacity, width),
            preferred_element_type=jnp.float32,
        )
    return lax.psum_scatter(
        total.astype(jnp.bfloat16), "expert", scatter_dimension=0, tiled=False
    ).astype(jnp.float32)


def general(
    attn_input, query_grad, query_weight, moe_cotangent, expert_ids, route_weights,
    gate_saved, up_saved, gate_weight, up_weight, down_weight,
):
    moe_input_grad = general_expert_update(
        moe_cotangent, expert_ids, route_weights, gate_saved, up_saved, gate_weight, up_weight, down_weight
    )
    return general_weight_update(attn_input, query_grad, query_weight), moe_input_grad


def line_sources():
    own_end, own_middle, other_middle, other_end = line_places()
    middle = on_middle()
    return (
        jnp.where(middle, other_middle, own_middle),
        jnp.where(middle, own_end, other_middle),
        other_end,
    )


def shards(
    attn_input, query_grad, query_weight, moe_cotangent, expert_ids, route_weights,
    gate_saved, up_saved, gate_weight, up_weight, down_weight,
):
    if (lax.axis_size("expert"), lax.axis_size("dp")) != (8, 4):
        return general(
            attn_input, query_grad, query_weight, moe_cotangent, expert_ids, route_weights,
            gate_saved, up_saved, gate_weight, up_weight, down_weight,
        )
    z = lax.axis_index("dp")
    place = lax.axis_index("expert")
    chip, core = place // 2, place % 2
    own_end, own_middle, other_middle, other_end = line_places()
    middle = on_middle()
    local, width, hidden_units = gate_weight.shape
    tokens, top = expert_ids.shape
    per_dp = gate_saved.shape[0]
    capacity = per_dp // 2
    rows = query_weight.shape[0]
    model = attn_input.shape[1]
    line = Line()

    routing = [expert_ids.astype(jnp.float32)] + list(three_terms(route_weights))
    tables = jnp.stack([value.T for value in routing]).astype(jnp.bfloat16)
    tables = jnp.stack([tables, swap(tables, 2, "routing_x")])
    own_tokens = after(moe_cotangent, tables)
    pieces = jnp.stack([own_tokens] + [swap(own_tokens, bits, "tokens_plane") for bits in (2, 4, 6)])
    tables = jnp.concatenate([tables, swap(tables, 4, "routing_y")])
    routed = tables
    tables = jnp.stack([tables, swap(tables, 1, "routing_core")], axis=1).astype(jnp.float32)

    quarter = model // 8

    def columns(index, count=1):
        return lax.dynamic_slice_in_dim(query_grad, index * rows, count * rows, 1)

    def of_pair(pair, end):
        first = (z < 2) if end else (z >= 2)
        return jnp.where(first, pair[:, :rows], pair[:, rows:])

    def add(a, b):
        return (a.astype(jnp.float32) + b.astype(jnp.float32)).astype(jnp.bfloat16)

    other_pair = columns(jnp.where(z < 2, 2, 0), 2)
    share = lax.dynamic_slice_in_dim(attn_input, (core * 4 + chip) * quarter, quarter, 1)
    share_in = line.hop(share, ends_in, "inputs_in")
    across_1 = line.hop(jnp.concatenate([share, other_pair], axis=1), across, "inputs_across_1")
    to_end = jnp.concatenate([share, columns(own_end)], axis=1)

    cotangents = (pieces, swap(pieces, 1, "tokens_core"))
    weights = tables[:, :, 1] + tables[:, :, 2] + tables[:, :, 3]
    select, slot_weight = expert_tables(tables[:, :, 0].astype(jnp.int32), weights, local, capacity)
    parts = []
    for expert in range(local):
        arrived = jnp.stack(
            [
                jnp.einsum(
                    "gct,gtd->gcd", select[:, i, expert], cotangents[i], preferred_element_type=jnp.float32
                )
                * slot_weight[:, i, expert, :, None]
                for i in range(2)
            ],
            axis=1,
        ).astype(jnp.bfloat16)
        part = jnp.einsum(
            "sd,hd->sh",
            arrived.reshape(4 * per_dp, width),
            down_weight[expert],
            preferred_element_type=jnp.float32,
        )
        parts.append(part.astype(jnp.bfloat16).reshape(4, per_dp, hidden_units))

    def block(index):
        return jnp.stack([pick(part, index ^ chip) for part in parts])

    def saved(array):
        blocks = jnp.swapaxes(array, 0, 1).reshape(local, 2, capacity, hidden_units)
        return jnp.where(core == 0, blocks, blocks[:, ::-1]).reshape(local, per_dp, hidden_units)

    share_in, across_1 = (after(value, *parts) for value in (share_in, across_1))
    line.last[tuple(ends_in)], line.last[tuple(across)] = share_in, across_1
    sum_far = line.hop(block(other_end), ends_in, "sum_far_in")
    out_share_1 = line.hop(after(to_end, *parts), ends_out, "inputs_out_1")
    share_across_2 = line.hop(share_in, across, "inputs_across_2")
    own_half = lax.dynamic_slice_in_dim(attn_input, core * (model // 2), model // 2, 1)
    own_columns = after(columns(z), share_across_2)
    own_columns = jnp.concatenate([own_columns, swap(own_columns, 1, "columns_core_own")], axis=1)
    gradient = token_product(own_columns, own_half)
    to_end = jnp.concatenate([across_1[:, :quarter], of_pair(across_1[:, quarter:], True)], axis=1)
    out_share_2 = line.hop(to_end, ends_out, "inputs_out_2")
    sum_middle = line.hop(block(other_middle), ends_in, "sum_middle_in")
    sum_far = line.hop(add(block(other_end), sum_far), across, "sum_far_across")
    out_share_3 = line.hop(share_across_2, ends_out, "inputs_out_3")
    saved_pair = [saved(after(array, sum_middle)) for array in (gate_saved, up_saved)]
    sum_near = line.hop(block(own_middle), ends_in, "sum_near_in", gradient)
    sum_middle = line.hop(add(block(other_middle), sum_middle), across, "sum_middle_across")
    sum_far = line.hop(add(block(own_end), sum_far), ends_out, "sum_far_out")

    def over_plane(at_middle, at_end):
        part = jnp.where(middle, at_middle, at_end)
        return lax.all_gather(part, "expert", axis=1, tiled=True, axis_index_groups=[[0, 2, 4, 6], [1, 3, 5, 7]])

    plane_1 = over_plane(across_1[:, :quarter], out_share_1[:, :quarter])
    plane_2 = over_plane(share_in, out_share_2[:, :quarter])
    plane_3 = over_plane(share_across_2, out_share_3)

    def step(gradient, grad, inputs, name):
        both = jnp.concatenate([grad, swap(grad, 1, name)], axis=1)
        return gradient + token_product(both, inputs)

    hidden = block(z).astype(jnp.float32) + sum_far.astype(jnp.float32)
    hidden = hidden + sum_middle.astype(jnp.float32) + sum_near.astype(jnp.float32)
    grads = activation_grads(hidden, *saved_pair)

    sources = (z,) + line_sources()
    relatives = [source ^ chip for source in sources]

    def units(values, places):
        values = jnp.concatenate(values, axis=2)
        chosen = jnp.stack([pick(select, index) for index in places])
        total = 0.0
        for expert in range(local):
            slot_input = slot_product(values[:, expert], gate_weight[expert], up_weight[expert])
            total = total + jnp.einsum(
                "ugct,ugcd->ugtd",
                chosen[:, :, expert],
                slot_input.reshape(2, 2, capacity, width),
                preferred_element_type=jnp.float32,
            )
        return total

    out_1 = line.hop(grads, ends_out, "grads_out_1")
    cross_1 = line.hop(grads, across, "grads_across_1")
    inward = line.hop(grads, ends_in, "grads_in")
    grad = jnp.where(middle, of_pair(across_1[:, quarter:], False), out_share_1[:, quarter:])
    gradient = step(gradient, after(grad, grads), plane_1, "columns_core_1")
    out_2 = line.hop(cross_1, ends_out, "grads_out_2", gradient)
    cross_2 = line.hop(inward, across, "grads_across_2")
    in_columns = jnp.concatenate([other_pair, columns(own_middle)], axis=1)
    in_columns = line.hop(in_columns, ends_in, "columns_in")
    early = units((grads, jnp.where(middle, cross_1, out_1)), relatives[:2])
    out_3 = line.hop(cross_2, ends_out, "grads_out_3", early)
    pair_across = line.hop(in_columns[:, : 2 * rows], across, "columns_across_2")
    grad = jnp.where(middle, in_columns[:, 2 * rows :], out_share_2[:, quarter:])
    gradient = step(gradient, after(grad, out_2, cross_2), plane_2, "columns_core_2")
    columns_out = line.hop(of_pair(pair_across, True), ends_out, "columns_out_3", gradient)
    late = units((jnp.where(middle, inward, out_2), jnp.where(middle, cross_2, out_3)), relatives[2:])
    totals = jnp.concatenate([early[:, 0], late[:, 0]])
    early = swap(after(early[:, 1].astype(jnp.bfloat16), out_3), 1, "returned_core_early")
    late = swap(late[:, 1].astype(jnp.bfloat16), 1, "returned_core_late")

    returned = jnp.zeros((4, tokens, width), jnp.bfloat16)
    for i, arrived in enumerate((early[0], early[1], late[0], late[1])):
        returned = lax.dynamic_update_slice_in_dim(returned, add(totals[i], arrived)[None], relatives[i], 0)
    moe_input_grad = returned[0].astype(jnp.float32)
    for relative in (1, 2, 3):
        moe_input_grad = moe_input_grad + swap(returned[relative], 2 * relative, "returned_plane").astype(jnp.float32)

    grad = jnp.where(middle, of_pair(pair_across, False), columns_out)
    gradient = step(gradient, grad, plane_3, "columns_core_3").astype(jnp.bfloat16)
    mine, received = gradient[:rows], swap(gradient[rows:], 1, "gradient_core")
    gradient = jnp.where(
        core == 0, jnp.concatenate([mine, received], axis=1), jnp.concatenate([received, mine], axis=1)
    )
    query_weight_next = row_update(query_weight, gradient.astype(jnp.float32))
    return (query_weight_next, moe_input_grad)


def solution(mesh):
    placed = (
        P("dp", None),
        P("dp", "expert"),
        P(("expert", "dp"), None),
        P("expert", "dp"),
        P("expert", None),
        P("expert", None),
        P("dp", "expert", None),
        P("dp", "expert", None),
        P("expert", "dp", None),
        P("expert", "dp", None),
        P("expert", None, "dp"),
    )
    return jax.shard_map(
        shards,
        mesh=mesh,
        in_specs=placed,
        out_specs=(P(("expert", "dp"), None), P("expert", "dp")),
        check_vma=False,
    )
```

```python
import jax
import jax.numpy as jnp
from jax import lax
from jax.sharding import PartitionSpec as P

step_rate = 0.01
epsilon = 1e-06

ends_in = [(0, 1), (3, 2)]
across = [(1, 2), (2, 1)]
ends_out = [(1, 0), (2, 3)]


class Line:
    def __init__(self):
        self.last = {}

    def hop(self, value, pairs, name, *first):
        key = tuple(pairs)
        first += (self.last[key],) if key in self.last else ()
        value = after(value, *first) if first else value
        with jax.named_scope(name):
            self.last[key] = lax.ppermute(value, "dp", pairs)
        return self.last[key]


def swap(value, bits, name):
    with jax.named_scope(name):
        return lax.ppermute(value, "expert", [(i, i ^ bits) for i in range(8)])


def after(value, *others):
    return lax.optimization_barrier((value,) + others)[0]


def pick(stack, index):
    return lax.dynamic_index_in_dim(stack, index, 0, keepdims=False)


def line_places():
    low = lax.axis_index("dp") < 2
    return [jnp.where(low, a, b) for a, b in ((0, 3), (1, 2), (2, 1), (3, 0))]


def on_middle():
    z = lax.axis_index("dp")
    return (z == 1) | (z == 2)


def activation_grads(hidden, gate_vals, up_vals):
    gate_float = gate_vals.astype(jnp.float32)
    up_float = up_vals.astype(jnp.float32)
    sigmoid_vals = jax.nn.sigmoid(gate_float)
    gate_grad = hidden * up_float * sigmoid_vals * (1.0 + gate_float * (1.0 - sigmoid_vals))
    up_grad = hidden * gate_float * sigmoid_vals
    return jnp.stack([gate_grad, up_grad], axis=0).astype(jnp.bfloat16)


def row_update(query_weight, gradient):
    radial = jnp.mean(query_weight * gradient, axis=1, keepdims=True) / (
        jnp.mean(query_weight * query_weight, axis=1, keepdims=True) + epsilon
    )
    stepped = query_weight - step_rate * (gradient - radial * query_weight)
    return stepped * lax.rsqrt(jnp.mean(stepped * stepped, axis=1, keepdims=True) + epsilon)


def three_terms(value):
    first = lax.reduce_precision(value, 8, 7)
    second = lax.reduce_precision(value - first, 8, 7)
    return first, second, value - first - second


def token_product(grads, inputs):
    return lax.dot_general(grads, inputs, (((0,), (0,)), ((), ())), preferred_element_type=jnp.float32)


def expert_tables(ids, weights, local, capacity):
    first = lax.axis_index("expert") * local
    experts = first + lax.broadcasted_iota(jnp.int32, (local, 1, 1), 0)
    hit = ids[..., None, :, :] == experts
    chosen = jnp.any(hit, axis=-2)
    token_weight = jnp.sum(jnp.where(hit, weights[..., None, :, :], 0.0), axis=-2)
    token = lax.broadcasted_iota(jnp.int32, (chosen.shape[-1],) * 2, 0)
    earlier = token < lax.broadcasted_iota(jnp.int32, token.shape, 1)
    position = jnp.dot(
        chosen.astype(jnp.bfloat16), earlier.astype(jnp.bfloat16), preferred_element_type=jnp.float32
    ).astype(jnp.int32)
    slot = jnp.where(chosen, position, -1)
    matched = slot[..., None, :] == lax.broadcasted_iota(jnp.int32, (capacity, 1), 0)
    slot_weight = jnp.sum(jnp.where(matched, token_weight[..., None, :], 0.0), axis=-1)
    return matched.astype(jnp.bfloat16), slot_weight


def slot_product(grads, gate_weight, up_weight):
    total = jnp.einsum("sh,ch->sc", grads[0], gate_weight, preferred_element_type=jnp.float32)
    total = total + jnp.einsum("sh,ch->sc", grads[1], up_weight, preferred_element_type=jnp.float32)
    return total.astype(jnp.bfloat16)


def general_weight_update(attn_input, query_grad, query_weight):
    gradient = lax.psum_scatter(
        token_product(query_grad, attn_input).astype(jnp.bfloat16), "dp", scatter_dimension=0, tiled=True
    ).astype(jnp.float32)
    return row_update(query_weight, gradient)


def general_expert_update(
    moe_cotangent, expert_ids, route_weights, gate_saved, up_saved, gate_weight, up_weight, down_weight
):
    groups = lax.axis_size("expert")
    local = gate_weight.shape[0]
    capacity = gate_saved.shape[0] * lax.axis_size("dp") // groups
    tokens, width = moe_cotangent.shape
    rows = lax.all_gather(moe_cotangent, "expert", axis=0, tiled=False)
    routing = jnp.stack([expert_ids.T.astype(jnp.float32), route_weights.T])
    routing = lax.all_gather(routing, "expert", axis=0, tiled=False)
    select, slot_weight = expert_tables(routing[:, 0].astype(jnp.int32), routing[:, 1], local, capacity)
    arrived = jnp.einsum("gect,gtd->egcd", select, rows, preferred_element_type=jnp.float32)
    arrived = (arrived * jnp.swapaxes(slot_weight, 0, 1)[..., None]).astype(jnp.bfloat16)
    total = 0.0
    for expert in range(local):
        flat = arrived[expert].reshape(groups * capacity, width)
        parts = jnp.einsum("sd,hd->sh", flat, down_weight[expert], preferred_element_type=jnp.float32)
        hidden = lax.psum_scatter(
            parts.astype(jnp.bfloat16), "dp", scatter_dimension=0, tiled=True
        ).astype(jnp.float32)
        grads = activation_grads(hidden, gate_saved[:, expert], up_saved[:, expert])
        grads = lax.all_gather(grads, "dp", axis=1, tiled=True)
        slot_input = slot_product(grads, gate_weight[expert], up_weight[expert])
        total = total + jnp.einsum(
            "gct,gcd->gtd",
            select[:, expert],
            slot_input.reshape(groups, capacity, width),
            preferred_element_type=jnp.float32,
        )
    return lax.psum_scatter(
        total.astype(jnp.bfloat16), "expert", scatter_dimension=0, tiled=False
    ).astype(jnp.float32)


def general(
    attn_input, query_grad, query_weight, moe_cotangent, expert_ids, route_weights,
    gate_saved, up_saved, gate_weight, up_weight, down_weight,
):
    moe_input_grad = general_expert_update(
        moe_cotangent, expert_ids, route_weights, gate_saved, up_saved, gate_weight, up_weight, down_weight
    )
    return general_weight_update(attn_input, query_grad, query_weight), moe_input_grad


def line_sources():
    own_end, own_middle, other_middle, other_end = line_places()
    middle = on_middle()
    return (
        jnp.where(middle, other_middle, own_middle),
        jnp.where(middle, own_end, other_middle),
        other_end,
    )


def shards(
    attn_input, query_grad, query_weight, moe_cotangent, expert_ids, route_weights,
    gate_saved, up_saved, gate_weight, up_weight, down_weight,
):
    if (lax.axis_size("expert"), lax.axis_size("dp")) != (8, 4):
        return general(
            attn_input, query_grad, query_weight, moe_cotangent, expert_ids, route_weights,
            gate_saved, up_saved, gate_weight, up_weight, down_weight,
        )
    z = lax.axis_index("dp")
    place = lax.axis_index("expert")
    chip, core = place // 2, place % 2
    own_end, own_middle, other_middle, other_end = line_places()
    middle = on_middle()
    local, width, hidden_units = gate_weight.shape
    tokens, top = expert_ids.shape
    per_dp = gate_saved.shape[0]
    capacity = per_dp // 2
    rows = query_weight.shape[0]
    half = rows // 2
    line = Line()

    routing = [expert_ids.astype(jnp.float32)] + list(three_terms(route_weights))
    tables = jnp.stack([value.T for value in routing]).astype(jnp.bfloat16)
    tables = jnp.stack([tables, swap(tables, 2, "routing_x")])
    own_tokens = after(moe_cotangent, tables)
    pieces = jnp.stack([own_tokens] + [swap(own_tokens, bits, "tokens_plane") for bits in (2, 4, 6)])
    tables = jnp.concatenate([tables, swap(tables, 4, "routing_y")])
    routed = tables
    tables = jnp.stack([tables, swap(tables, 1, "routing_core")], axis=1).astype(jnp.float32)

    def product(places, *first):
        grads = [lax.dynamic_slice_in_dim(query_grad, index * rows + at * half, half, 1) for index, at in places]
        grads = jnp.concatenate(grads, axis=1)
        return token_product(after(grads, *first) if first else grads, attn_input).astype(jnp.bfloat16)

    def add(a, b):
        return (a.astype(jnp.float32) + b.astype(jnp.float32)).astype(jnp.bfloat16)

    to_far_0 = product([(other_end, 0)], routed)
    far_0 = line.hop(to_far_0, ends_in, "rows_far_in_0")

    cotangents = (pieces, swap(pieces, 1, "tokens_core"))
    weights = tables[:, :, 1] + tables[:, :, 2] + tables[:, :, 3]
    select, slot_weight = expert_tables(tables[:, :, 0].astype(jnp.int32), weights, local, capacity)
    parts = []
    for expert in range(local):
        arrived = jnp.stack(
            [
                jnp.einsum(
                    "gct,gtd->gcd", select[:, i, expert], cotangents[i], preferred_element_type=jnp.float32
                )
                * slot_weight[:, i, expert, :, None]
                for i in range(2)
            ],
            axis=1,
        ).astype(jnp.bfloat16)
        part = jnp.einsum(
            "sd,hd->sh",
            arrived.reshape(4 * per_dp, width),
            down_weight[expert],
            preferred_element_type=jnp.float32,
        )
        parts.append(part.astype(jnp.bfloat16).reshape(4, per_dp, hidden_units))

    def block(index):
        return jnp.stack([pick(part, index ^ chip) for part in parts])

    def saved(array):
        blocks = jnp.swapaxes(array, 0, 1).reshape(local, 2, capacity, hidden_units)
        return jnp.where(core == 0, blocks, blocks[:, ::-1]).reshape(local, per_dp, hidden_units)

    far_0 = line.last[tuple(ends_in)] = after(far_0, *parts)
    to_end = product([(own_end, 0), (own_end, 1)], far_0)
    sum_far = line.hop(block(other_end), ends_in, "sum_far_in")
    far_0 = line.hop(add(to_far_0, far_0), across, "rows_far_across_0")
    saved_pair = [saved(after(array, far_0)) for array in (gate_saved, up_saved)]
    to_far_1 = product([(other_end, 1)], sum_far)
    sum_middle = line.hop(block(other_middle), ends_in, "sum_middle_in")
    sum_far = line.hop(add(block(other_end), sum_far), across, "sum_far_across")
    far_0 = line.hop(add(to_end[:half], far_0), ends_out, "rows_far_out_0")
    to_middle = product([(other_middle, 0), (other_middle, 1)], sum_far)
    sum_near = line.hop(block(own_middle), ends_in, "sum_near_in")
    sum_middle = line.hop(add(block(other_middle), sum_middle), across, "sum_middle_across")
    sum_far = line.hop(add(block(own_end), sum_far), ends_out, "sum_far_out")
    sum_far = after(sum_far, to_far_1, to_middle)
    hidden = block(z).astype(jnp.float32) + sum_far.astype(jnp.float32)
    hidden = hidden + sum_middle.astype(jnp.float32) + sum_near.astype(jnp.float32)
    grads = activation_grads(hidden, *saved_pair)

    sources = (z,) + line_sources()
    relatives = [source ^ chip for source in sources]

    def units(values, places):
        values = jnp.concatenate(values, axis=2)
        chosen = jnp.stack([pick(select, index) for index in places])
        total = 0.0
        for expert in range(local):
            slot_input = slot_product(values[:, expert], gate_weight[expert], up_weight[expert])
            total = total + jnp.einsum(
                "ugct,ugcd->ugtd",
                chosen[:, :, expert],
                slot_input.reshape(2, 2, capacity, width),
                preferred_element_type=jnp.float32,
            )
        return total

    out_1 = line.hop(grads, ends_out, "grads_out_1")
    cross_1 = line.hop(grads, across, "grads_across_1")
    inward = line.hop(grads, ends_in, "grads_in")
    to_near = product([(own_middle, 0), (own_middle, 1)], grads)
    out_2 = line.hop(cross_1, ends_out, "grads_out_2")
    cross_2 = line.hop(inward, across, "grads_across_2")
    far_1 = line.hop(to_far_1, ends_in, "rows_far_in_1")
    early = units((grads, jnp.where(middle, cross_1, out_1)), relatives[:2])
    out_3 = line.hop(cross_2, ends_out, "grads_out_3", early, to_near)
    far_1 = line.hop(add(to_far_1, far_1), across, "rows_far_across_1")
    middle_sum = line.hop(to_middle, ends_in, "rows_middle_in")
    near = line.hop(to_near, ends_in, "rows_near_in")
    far_1 = line.hop(add(to_end[half:], far_1), ends_out, "rows_far_out_1")
    middle_sum = line.hop(add(to_middle, middle_sum), across, "rows_middle_across")
    late = units((jnp.where(middle, inward, out_2), jnp.where(middle, cross_2, out_3)), relatives[2:])
    totals = jnp.concatenate([early[:, 0], late[:, 0]])
    early = swap(after(early[:, 1].astype(jnp.bfloat16), out_3), 1, "returned_core_early")
    late = swap(late[:, 1].astype(jnp.bfloat16), 1, "returned_core_late")

    blocks = [add(totals[i], arrived) for i, arrived in enumerate((early[0], early[1], late[0], late[1]))]

    def returned(relative):
        value = blocks[3]
        for i in range(3):
            value = jnp.where(relatives[i] == relative, blocks[i], value)
        return value

    moe_input_grad = returned(0).astype(jnp.float32)
    for relative in (1, 2, 3):
        moe_input_grad = moe_input_grad + swap(returned(relative), 2 * relative, "returned_plane").astype(jnp.float32)

    gradient = jnp.where(middle, to_near, to_end).astype(jnp.float32) + jnp.concatenate([far_0, far_1]).astype(jnp.float32)
    gradient = gradient + middle_sum.astype(jnp.float32) + near.astype(jnp.float32)
    query_weight_next = row_update(query_weight, gradient)
    return (query_weight_next, moe_input_grad)


def solution(mesh):
    placed = (
        P("dp", None),
        P("dp", "expert"),
        P(("expert", "dp"), None),
        P("expert", "dp"),
        P("expert", None),
        P("expert", None),
        P("dp", "expert", None),
        P("dp", "expert", None),
        P("expert", "dp", None),
        P("expert", "dp", None),
        P("expert", None, "dp"),
    )
    return jax.shard_map(
        shards,
        mesh=mesh,
        in_specs=placed,
        out_specs=(P(("expert", "dp"), None), P("expert", "dp")),
        check_vma=False,
    )
```

```python
import jax
import jax.numpy as jnp
from jax import lax
from jax.sharding import PartitionSpec as P

step_rate = 0.01
epsilon = 1e-06

ends_in = [(0, 1), (3, 2)]
across = [(1, 2), (2, 1)]
ends_out = [(1, 0), (2, 3)]


class Line:
    def __init__(self):
        self.last = {}

    def hop(self, value, pairs, name, *first):
        key = tuple(pairs)
        first += (self.last[key],) if key in self.last else ()
        value = after(value, *first) if first else value
        with jax.named_scope(name):
            self.last[key] = lax.ppermute(value, "dp", pairs)
        return self.last[key]


def swap(value, bits, name):
    with jax.named_scope(name):
        return lax.ppermute(value, "expert", [(i, i ^ bits) for i in range(8)])


def after(value, *others):
    return lax.optimization_barrier((value,) + others)[0]


def pick(stack, index):
    return lax.dynamic_index_in_dim(stack, index, 0, keepdims=False)


def line_places():
    low = lax.axis_index("dp") < 2
    return [jnp.where(low, a, b) for a, b in ((0, 3), (1, 2), (2, 1), (3, 0))]


def on_middle():
    z = lax.axis_index("dp")
    return (z == 1) | (z == 2)


def activation_grads(hidden, gate_vals, up_vals):
    gate_float = gate_vals.astype(jnp.float32)
    up_float = up_vals.astype(jnp.float32)
    sigmoid_vals = jax.nn.sigmoid(gate_float)
    gate_grad = hidden * up_float * sigmoid_vals * (1.0 + gate_float * (1.0 - sigmoid_vals))
    up_grad = hidden * gate_float * sigmoid_vals
    return jnp.stack([gate_grad, up_grad], axis=0).astype(jnp.bfloat16)


def row_update(query_weight, gradient):
    radial = jnp.mean(query_weight * gradient, axis=1, keepdims=True) / (
        jnp.mean(query_weight * query_weight, axis=1, keepdims=True) + epsilon
    )
    stepped = query_weight - step_rate * (gradient - radial * query_weight)
    return stepped * lax.rsqrt(jnp.mean(stepped * stepped, axis=1, keepdims=True) + epsilon)


def three_terms(value):
    first = lax.reduce_precision(value, 8, 7)
    second = lax.reduce_precision(value - first, 8, 7)
    return first, second, value - first - second


def token_product(grads, inputs):
    return lax.dot_general(grads, inputs, (((0,), (0,)), ((), ())), preferred_element_type=jnp.float32)


def expert_tables(ids, weights, local, capacity):
    first = lax.axis_index("expert") * local
    experts = first + lax.broadcasted_iota(jnp.int32, (local, 1, 1), 0)
    hit = ids[..., None, :, :] == experts
    chosen = jnp.any(hit, axis=-2)
    token_weight = jnp.sum(jnp.where(hit, weights[..., None, :, :], 0.0), axis=-2)
    token = lax.broadcasted_iota(jnp.int32, (chosen.shape[-1],) * 2, 0)
    earlier = token < lax.broadcasted_iota(jnp.int32, token.shape, 1)
    position = jnp.dot(
        chosen.astype(jnp.bfloat16), earlier.astype(jnp.bfloat16), preferred_element_type=jnp.float32
    ).astype(jnp.int32)
    slot = jnp.where(chosen, position, -1)
    matched = slot[..., None, :] == lax.broadcasted_iota(jnp.int32, (capacity, 1), 0)
    slot_weight = jnp.sum(jnp.where(matched, token_weight[..., None, :], 0.0), axis=-1)
    return matched.astype(jnp.bfloat16), slot_weight


def slot_product(grads, gate_weight, up_weight):
    total = jnp.einsum("sh,ch->sc", grads[0], gate_weight, preferred_element_type=jnp.float32)
    total = total + jnp.einsum("sh,ch->sc", grads[1], up_weight, preferred_element_type=jnp.float32)
    return total.astype(jnp.bfloat16)


def general_weight_update(attn_input, query_grad, query_weight):
    gradient = lax.psum_scatter(
        token_product(query_grad, attn_input).astype(jnp.bfloat16), "dp", scatter_dimension=0, tiled=True
    ).astype(jnp.float32)
    return row_update(query_weight, gradient)


def general_expert_update(
    moe_cotangent, expert_ids, route_weights, gate_saved, up_saved, gate_weight, up_weight, down_weight
):
    groups = lax.axis_size("expert")
    local = gate_weight.shape[0]
    capacity = gate_saved.shape[0] * lax.axis_size("dp") // groups
    tokens, width = moe_cotangent.shape
    rows = lax.all_gather(moe_cotangent, "expert", axis=0, tiled=False)
    routing = jnp.stack([expert_ids.T.astype(jnp.float32), route_weights.T])
    routing = lax.all_gather(routing, "expert", axis=0, tiled=False)
    select, slot_weight = expert_tables(routing[:, 0].astype(jnp.int32), routing[:, 1], local, capacity)
    arrived = jnp.einsum("gect,gtd->egcd", select, rows, preferred_element_type=jnp.float32)
    arrived = (arrived * jnp.swapaxes(slot_weight, 0, 1)[..., None]).astype(jnp.bfloat16)
    total = 0.0
    for expert in range(local):
        flat = arrived[expert].reshape(groups * capacity, width)
        parts = jnp.einsum("sd,hd->sh", flat, down_weight[expert], preferred_element_type=jnp.float32)
        hidden = lax.psum_scatter(
            parts.astype(jnp.bfloat16), "dp", scatter_dimension=0, tiled=True
        ).astype(jnp.float32)
        grads = activation_grads(hidden, gate_saved[:, expert], up_saved[:, expert])
        grads = lax.all_gather(grads, "dp", axis=1, tiled=True)
        slot_input = slot_product(grads, gate_weight[expert], up_weight[expert])
        total = total + jnp.einsum(
            "gct,gcd->gtd",
            select[:, expert],
            slot_input.reshape(groups, capacity, width),
            preferred_element_type=jnp.float32,
        )
    return lax.psum_scatter(
        total.astype(jnp.bfloat16), "expert", scatter_dimension=0, tiled=False
    ).astype(jnp.float32)


def general(
    attn_input, query_grad, query_weight, moe_cotangent, expert_ids, route_weights,
    gate_saved, up_saved, gate_weight, up_weight, down_weight,
):
    moe_input_grad = general_expert_update(
        moe_cotangent, expert_ids, route_weights, gate_saved, up_saved, gate_weight, up_weight, down_weight
    )
    return general_weight_update(attn_input, query_grad, query_weight), moe_input_grad


def line_sources():
    own_end, own_middle, other_middle, other_end = line_places()
    middle = on_middle()
    return (
        jnp.where(middle, other_middle, own_middle),
        jnp.where(middle, own_end, other_middle),
        other_end,
    )


def shards(
    attn_input, query_grad, query_weight, moe_cotangent, expert_ids, route_weights,
    gate_saved, up_saved, gate_weight, up_weight, down_weight,
):
    if (lax.axis_size("expert"), lax.axis_size("dp")) != (8, 4):
        return general(
            attn_input, query_grad, query_weight, moe_cotangent, expert_ids, route_weights,
            gate_saved, up_saved, gate_weight, up_weight, down_weight,
        )
    z = lax.axis_index("dp")
    place = lax.axis_index("expert")
    chip, core = place // 2, place % 2
    own_end, own_middle, other_middle, other_end = line_places()
    middle = on_middle()
    local, width, hidden_units = gate_weight.shape
    tokens, top = expert_ids.shape
    per_dp = gate_saved.shape[0]
    capacity = per_dp // 2
    rows = query_weight.shape[0]
    half = rows // 2
    cut = rows * 3 // 4
    line = Line()

    routing = [expert_ids.astype(jnp.float32)] + list(three_terms(route_weights))
    tables = jnp.stack([value.T for value in routing]).astype(jnp.bfloat16)
    tables = jnp.stack([tables, swap(tables, 2, "routing_x")])
    own_tokens = after(moe_cotangent, tables)
    pieces = jnp.stack([own_tokens] + [swap(own_tokens, bits, "tokens_plane") for bits in (2, 4, 6)])
    tables = jnp.concatenate([tables, swap(tables, 4, "routing_y")])
    routed = tables
    tables = jnp.stack([tables, swap(tables, 1, "routing_core")], axis=1).astype(jnp.float32)

    def product(index, start, stop, *first):
        grads = lax.dynamic_slice_in_dim(query_grad, index * rows + start, stop - start, 1)
        return token_product(after(grads, *first) if first else grads, attn_input).astype(jnp.bfloat16)

    def add(a, b):
        return (a.astype(jnp.float32) + b.astype(jnp.float32)).astype(jnp.bfloat16)

    to_far_0 = product(other_end, 0, half, routed)
    far_0 = line.hop(to_far_0, ends_in, "rows_far_in_0")

    cotangents = (pieces, swap(pieces, 1, "tokens_core"))
    weights = tables[:, :, 1] + tables[:, :, 2] + tables[:, :, 3]
    select, slot_weight = expert_tables(tables[:, :, 0].astype(jnp.int32), weights, local, capacity)
    parts = []
    for expert in range(local):
        arrived = jnp.stack(
            [
                jnp.einsum(
                    "gct,gtd->gcd", select[:, i, expert], cotangents[i], preferred_element_type=jnp.float32
                )
                * slot_weight[:, i, expert, :, None]
                for i in range(2)
            ],
            axis=1,
        ).astype(jnp.bfloat16)
        part = jnp.einsum(
            "sd,hd->sh",
            arrived.reshape(4 * per_dp, width),
            down_weight[expert],
            preferred_element_type=jnp.float32,
        )
        parts.append(part.astype(jnp.bfloat16).reshape(4, per_dp, hidden_units))

    def block(index):
        return jnp.stack([pick(part, index ^ chip) for part in parts])

    def saved(array):
        blocks = jnp.swapaxes(array, 0, 1).reshape(local, 2, capacity, hidden_units)
        return jnp.where(core == 0, blocks, blocks[:, ::-1]).reshape(local, per_dp, hidden_units)

    far_0 = line.last[tuple(ends_in)] = after(far_0, *parts)
    to_end = product(own_end, 0, rows, far_0)
    sum_far = line.hop(block(other_end), ends_in, "sum_far_in")
    far_0 = line.hop(add(to_far_0, far_0), across, "rows_far_across_0")
    saved_pair = [saved(after(array, far_0)) for array in (gate_saved, up_saved)]
    to_far_1 = product(other_end, half, cut, sum_far)
    sum_middle = line.hop(block(other_middle), ends_in, "sum_middle_in")
    sum_far = line.hop(add(block(other_end), sum_far), across, "sum_far_across")
    far_0 = line.hop(add(to_end[:half], far_0), ends_out, "rows_far_out_0")
    to_middle = product(other_middle, 0, rows, sum_far)
    to_far_2 = product(other_end, cut, rows, sum_far)
    sum_near = line.hop(block(own_middle), ends_in, "sum_near_in", to_far_1)
    sum_middle = line.hop(add(block(other_middle), sum_middle), across, "sum_middle_across")
    sum_far = line.hop(add(block(own_end), sum_far), ends_out, "sum_far_out")
    far_1 = line.hop(to_far_1, ends_in, "rows_far_in_1")
    sum_far = after(sum_far, to_far_2, to_middle)
    hidden = block(z).astype(jnp.float32) + sum_far.astype(jnp.float32)
    hidden = hidden + sum_middle.astype(jnp.float32) + sum_near.astype(jnp.float32)
    grads = activation_grads(hidden, *saved_pair)

    sources = (z,) + line_sources()
    relatives = [source ^ chip for source in sources]

    def units(values, places):
        values = jnp.concatenate(values, axis=2)
        chosen = jnp.stack([pick(select, index) for index in places])
        total = 0.0
        for expert in range(local):
            slot_input = slot_product(values[:, expert], gate_weight[expert], up_weight[expert])
            total = total + jnp.einsum(
                "ugct,ugcd->ugtd",
                chosen[:, :, expert],
                slot_input.reshape(2, 2, capacity, width),
                preferred_element_type=jnp.float32,
            )
        return total

    grads = after(grads, far_1)
    out_1 = line.hop(grads, ends_out, "grads_out_1")
    cross_1 = line.hop(grads, across, "grads_across_1")
    inward = line.hop(grads, ends_in, "grads_in")
    to_near = product(own_middle, 0, rows, grads)
    out_2 = line.hop(cross_1, ends_out, "grads_out_2")
    cross_2 = line.hop(inward, across, "grads_across_2")
    far_2 = line.hop(to_far_2, ends_in, "rows_far_in_2")
    early = units((grads, jnp.where(middle, cross_1, out_1)), relatives[:2])
    out_3 = line.hop(cross_2, ends_out, "grads_out_3", early, to_near)
    far_1 = jnp.concatenate([add(to_far_1, far_1), add(to_far_2, far_2)])
    far_1 = line.hop(far_1, across, "rows_far_across_1")
    middle_sum = line.hop(to_middle, ends_in, "rows_middle_in")
    near = line.hop(to_near, ends_in, "rows_near_in")
    far_1 = line.hop(add(to_end[half:], far_1), ends_out, "rows_far_out_1")
    middle_sum = line.hop(add(to_middle, middle_sum), across, "rows_middle_across")
    late = units((jnp.where(middle, inward, out_2), jnp.where(middle, cross_2, out_3)), relatives[2:])
    totals = jnp.concatenate([early[:, 0], late[:, 0]])
    early = swap(after(early[:, 1].astype(jnp.bfloat16), out_3), 1, "returned_core_early")
    late = swap(late[:, 1].astype(jnp.bfloat16), 1, "returned_core_late")

    blocks = [add(totals[i], arrived) for i, arrived in enumerate((early[0], early[1], late[0], late[1]))]

    def returned(relative):
        value = blocks[3]
        for i in range(3):
            value = jnp.where(relatives[i] == relative, blocks[i], value)
        return value

    moe_input_grad = returned(0).astype(jnp.float32)
    for relative in (1, 2, 3):
        moe_input_grad = moe_input_grad + swap(returned(relative), 2 * relative, "returned_plane").astype(jnp.float32)

    own = after(jnp.where(middle, to_near, to_end), out_3)
    gradient = [
        own[cut].astype(jnp.float32) + sum(part.astype(jnp.float32) for part in (far, middle_sum[cut], near[cut]))
        for cut, far in ((slice(0, half), far_0), (slice(half, rows), far_1))
    ]
    query_weight_next = row_update(query_weight, jnp.concatenate(gradient, axis=0))
    return (query_weight_next, moe_input_grad)


def solution(mesh):
    placed = (
        P("dp", None),
        P("dp", "expert"),
        P(("expert", "dp"), None),
        P("expert", "dp"),
        P("expert", None),
        P("expert", None),
        P("dp", "expert", None),
        P("dp", "expert", None),
        P("expert", "dp", None),
        P("expert", "dp", None),
        P("expert", None, "dp"),
    )
    return jax.shard_map(
        shards,
        mesh=mesh,
        in_specs=placed,
        out_specs=(P(("expert", "dp"), None), P("expert", "dp")),
        check_vma=False,
    )
```

```python
import jax
import jax.numpy as jnp
from jax import lax
from jax.sharding import PartitionSpec as P

step_rate = 0.01
epsilon = 1e-06

ends_in = [(0, 1), (3, 2)]
across = [(1, 2), (2, 1)]
ends_out = [(1, 0), (2, 3)]


class Line:
    def __init__(self):
        self.last = {}

    def hop(self, value, pairs, name, *first):
        key = tuple(pairs)
        first += (self.last[key],) if key in self.last else ()
        value = after(value, *first) if first else value
        with jax.named_scope(name):
            self.last[key] = lax.ppermute(value, "dp", pairs)
        return self.last[key]


def swap(value, bits, name):
    with jax.named_scope(name):
        return lax.ppermute(value, "expert", [(i, i ^ bits) for i in range(8)])


def after(value, *others):
    return lax.optimization_barrier((value,) + others)[0]


def pick(stack, index):
    return lax.dynamic_index_in_dim(stack, index, 0, keepdims=False)


def line_places():
    low = lax.axis_index("dp") < 2
    return [jnp.where(low, a, b) for a, b in ((0, 3), (1, 2), (2, 1), (3, 0))]


def on_middle():
    z = lax.axis_index("dp")
    return (z == 1) | (z == 2)


def activation_grads(hidden, gate_vals, up_vals):
    gate_float = gate_vals.astype(jnp.float32)
    up_float = up_vals.astype(jnp.float32)
    sigmoid_vals = jax.nn.sigmoid(gate_float)
    gate_grad = hidden * up_float * sigmoid_vals * (1.0 + gate_float * (1.0 - sigmoid_vals))
    up_grad = hidden * gate_float * sigmoid_vals
    return jnp.stack([gate_grad, up_grad], axis=0).astype(jnp.bfloat16)


def row_update(query_weight, gradient):
    radial = jnp.mean(query_weight * gradient, axis=1, keepdims=True) / (
        jnp.mean(query_weight * query_weight, axis=1, keepdims=True) + epsilon
    )
    stepped = query_weight - step_rate * (gradient - radial * query_weight)
    return stepped * lax.rsqrt(jnp.mean(stepped * stepped, axis=1, keepdims=True) + epsilon)


def three_terms(value):
    first = lax.reduce_precision(value, 8, 7)
    second = lax.reduce_precision(value - first, 8, 7)
    return first, second, value - first - second


def token_product(grads, inputs):
    return lax.dot_general(grads, inputs, (((0,), (0,)), ((), ())), preferred_element_type=jnp.float32)


def expert_tables(ids, weights, local, capacity):
    first = lax.axis_index("expert") * local
    experts = first + lax.broadcasted_iota(jnp.int32, (local, 1, 1), 0)
    hit = ids[..., None, :, :] == experts
    chosen = jnp.any(hit, axis=-2)
    token_weight = jnp.sum(jnp.where(hit, weights[..., None, :, :], 0.0), axis=-2)
    token = lax.broadcasted_iota(jnp.int32, (chosen.shape[-1],) * 2, 0)
    earlier = token < lax.broadcasted_iota(jnp.int32, token.shape, 1)
    position = jnp.dot(
        chosen.astype(jnp.bfloat16), earlier.astype(jnp.bfloat16), preferred_element_type=jnp.float32
    ).astype(jnp.int32)
    slot = jnp.where(chosen, position, -1)
    matched = slot[..., None, :] == lax.broadcasted_iota(jnp.int32, (capacity, 1), 0)
    slot_weight = jnp.sum(jnp.where(matched, token_weight[..., None, :], 0.0), axis=-1)
    return matched.astype(jnp.bfloat16), slot_weight


def slot_product(grads, gate_weight, up_weight):
    total = jnp.einsum("sh,ch->sc", grads[0], gate_weight, preferred_element_type=jnp.float32)
    total = total + jnp.einsum("sh,ch->sc", grads[1], up_weight, preferred_element_type=jnp.float32)
    return total.astype(jnp.bfloat16)


def general_weight_update(attn_input, query_grad, query_weight):
    gradient = lax.psum_scatter(
        token_product(query_grad, attn_input).astype(jnp.bfloat16), "dp", scatter_dimension=0, tiled=True
    ).astype(jnp.float32)
    return row_update(query_weight, gradient)


def general_expert_update(
    moe_cotangent, expert_ids, route_weights, gate_saved, up_saved, gate_weight, up_weight, down_weight
):
    groups = lax.axis_size("expert")
    local = gate_weight.shape[0]
    capacity = gate_saved.shape[0] * lax.axis_size("dp") // groups
    tokens, width = moe_cotangent.shape
    rows = lax.all_gather(moe_cotangent, "expert", axis=0, tiled=False)
    routing = jnp.stack([expert_ids.T.astype(jnp.float32), route_weights.T])
    routing = lax.all_gather(routing, "expert", axis=0, tiled=False)
    select, slot_weight = expert_tables(routing[:, 0].astype(jnp.int32), routing[:, 1], local, capacity)
    arrived = jnp.einsum("gect,gtd->egcd", select, rows, preferred_element_type=jnp.float32)
    arrived = (arrived * jnp.swapaxes(slot_weight, 0, 1)[..., None]).astype(jnp.bfloat16)
    total = 0.0
    for expert in range(local):
        flat = arrived[expert].reshape(groups * capacity, width)
        parts = jnp.einsum("sd,hd->sh", flat, down_weight[expert], preferred_element_type=jnp.float32)
        hidden = lax.psum_scatter(
            parts.astype(jnp.bfloat16), "dp", scatter_dimension=0, tiled=True
        ).astype(jnp.float32)
        grads = activation_grads(hidden, gate_saved[:, expert], up_saved[:, expert])
        grads = lax.all_gather(grads, "dp", axis=1, tiled=True)
        slot_input = slot_product(grads, gate_weight[expert], up_weight[expert])
        total = total + jnp.einsum(
            "gct,gcd->gtd",
            select[:, expert],
            slot_input.reshape(groups, capacity, width),
            preferred_element_type=jnp.float32,
        )
    return lax.psum_scatter(
        total.astype(jnp.bfloat16), "expert", scatter_dimension=0, tiled=False
    ).astype(jnp.float32)


def general(
    attn_input, query_grad, query_weight, moe_cotangent, expert_ids, route_weights,
    gate_saved, up_saved, gate_weight, up_weight, down_weight,
):
    moe_input_grad = general_expert_update(
        moe_cotangent, expert_ids, route_weights, gate_saved, up_saved, gate_weight, up_weight, down_weight
    )
    return general_weight_update(attn_input, query_grad, query_weight), moe_input_grad


def line_sources():
    own_end, own_middle, other_middle, other_end = line_places()
    middle = on_middle()
    return (
        jnp.where(middle, other_middle, own_middle),
        jnp.where(middle, own_end, other_middle),
        other_end,
    )


def shards(
    attn_input, query_grad, query_weight, moe_cotangent, expert_ids, route_weights,
    gate_saved, up_saved, gate_weight, up_weight, down_weight,
):
    if (lax.axis_size("expert"), lax.axis_size("dp")) != (8, 4):
        return general(
            attn_input, query_grad, query_weight, moe_cotangent, expert_ids, route_weights,
            gate_saved, up_saved, gate_weight, up_weight, down_weight,
        )
    z = lax.axis_index("dp")
    place = lax.axis_index("expert")
    chip, core = place // 2, place % 2
    own_end, own_middle, other_middle, other_end = line_places()
    middle = on_middle()
    local, width, hidden_units = gate_weight.shape
    tokens, top = expert_ids.shape
    per_dp = gate_saved.shape[0]
    capacity = per_dp // 2
    rows = query_weight.shape[0]
    cut = rows * 3 // 8
    line = Line()

    routing = [expert_ids.astype(jnp.float32)] + list(three_terms(route_weights))
    tables = jnp.stack([value.T for value in routing]).astype(jnp.bfloat16)
    tables = jnp.stack([tables, swap(tables, 2, "routing_x")])
    own_tokens = after(moe_cotangent, tables)
    pieces = jnp.stack([own_tokens] + [swap(own_tokens, bits, "tokens_plane") for bits in (2, 4, 6)])
    tables = jnp.concatenate([tables, swap(tables, 4, "routing_y")])
    routed = tables
    tables = jnp.stack([tables, swap(tables, 1, "routing_core")], axis=1).astype(jnp.float32)

    def product(places, *first):
        grads = [
            lax.dynamic_slice_in_dim(query_grad, index * rows + start, stop - start, 1) for index, start, stop in places
        ]
        grads = jnp.concatenate(grads, axis=1)
        return token_product(after(grads, *first) if first else grads, attn_input).astype(jnp.bfloat16)

    def add(a, b):
        return (a.astype(jnp.float32) + b.astype(jnp.float32)).astype(jnp.bfloat16)

    to_far_0 = product([(other_end, 0, cut)], routed)
    far_0 = line.hop(to_far_0, ends_in, "rows_far_in_0")

    cotangents = (pieces, swap(pieces, 1, "tokens_core"))
    weights = tables[:, :, 1] + tables[:, :, 2] + tables[:, :, 3]
    select, slot_weight = expert_tables(tables[:, :, 0].astype(jnp.int32), weights, local, capacity)
    parts = []
    for expert in range(local):
        arrived = jnp.stack(
            [
                jnp.einsum(
                    "gct,gtd->gcd", select[:, i, expert], cotangents[i], preferred_element_type=jnp.float32
                )
                * slot_weight[:, i, expert, :, None]
                for i in range(2)
            ],
            axis=1,
        ).astype(jnp.bfloat16)
        part = jnp.einsum(
            "sd,hd->sh",
            arrived.reshape(4 * per_dp, width),
            down_weight[expert],
            preferred_element_type=jnp.float32,
        )
        parts.append(part.astype(jnp.bfloat16).reshape(4, per_dp, hidden_units))

    def block(index):
        return jnp.stack([pick(part, index ^ chip) for part in parts])

    def saved(array):
        blocks = jnp.swapaxes(array, 0, 1).reshape(local, 2, capacity, hidden_units)
        return jnp.where(core == 0, blocks, blocks[:, ::-1]).reshape(local, per_dp, hidden_units)

    line.last.clear()
    far_0 = after(far_0, *parts)
    to_end = product([(own_end, 0, rows)], far_0)
    sum_far = line.hop(block(other_end), ends_in, "sum_far_in")
    far_0 = line.hop(add(to_far_0, far_0), across, "rows_far_across_0")
    saved_pair = [saved(after(array, far_0)) for array in (gate_saved, up_saved)]
    to_far_1_middle_0 = product([(other_end, cut, rows), (other_middle, 0, cut)], sum_far)
    sum_middle = line.hop(block(other_middle), ends_in, "sum_middle_in")
    sum_far = line.hop(add(block(other_end), sum_far), across, "sum_far_across")
    far_0 = line.hop(add(to_end[:cut], far_0), ends_out, "rows_far_out_0")
    to_middle_1 = product([(other_middle, cut, rows)], sum_far)
    sum_near = line.hop(block(own_middle), ends_in, "sum_near_in")
    sum_middle = line.hop(add(block(other_middle), sum_middle), across, "sum_middle_across")
    sum_far = line.hop(add(block(own_end), sum_far), ends_out, "sum_far_out")
    hidden = block(z).astype(jnp.float32) + sum_far.astype(jnp.float32)
    hidden = hidden + sum_middle.astype(jnp.float32) + sum_near.astype(jnp.float32)
    grads = activation_grads(hidden, *saved_pair)

    sources = (z,) + line_sources()
    relatives = [source ^ chip for source in sources]

    def units(values, places):
        values = jnp.concatenate(values, axis=2)
        chosen = jnp.stack([pick(select, index) for index in places])
        total = 0.0
        for expert in range(local):
            slot_input = slot_product(values[:, expert], gate_weight[expert], up_weight[expert])
            total = total + jnp.einsum(
                "ugct,ugcd->ugtd",
                chosen[:, :, expert],
                slot_input.reshape(2, 2, capacity, width),
                preferred_element_type=jnp.float32,
            )
        return total

    out_1 = line.hop(grads, ends_out, "grads_out_1", to_far_1_middle_0, to_middle_1)
    cross_1 = line.hop(grads, across, "grads_across_1")
    inward = line.hop(grads, ends_in, "grads_in")
    to_near = product([(own_middle, 0, rows)], grads)
    out_2 = line.hop(cross_1, ends_out, "grads_out_2")
    cross_2 = line.hop(inward, across, "grads_across_2")
    far_1_middle_0_in = line.hop(to_far_1_middle_0, ends_in, "rows_far_1_middle_0_in")
    early = units((grads, jnp.where(middle, cross_1, out_1)), relatives[:2])
    out_3 = line.hop(cross_2, ends_out, "grads_out_3", early, to_near)
    far_1_middle_0 = line.hop(
        add(to_far_1_middle_0, far_1_middle_0_in), across, "rows_far_1_middle_0_across"
    )
    middle_1 = line.hop(to_middle_1, ends_in, "rows_middle_in_1")
    near = line.hop(to_near, ends_in, "rows_near_in")
    far_1 = line.hop(add(to_end[cut:], far_1_middle_0[: rows - cut]), ends_out, "rows_far_out_1")
    middle_1 = line.hop(add(to_middle_1, middle_1), across, "rows_middle_across_1")
    late = units((jnp.where(middle, inward, out_2), jnp.where(middle, cross_2, out_3)), relatives[2:])
    totals = jnp.concatenate([early[:, 0], late[:, 0]])
    early = swap(after(early[:, 1].astype(jnp.bfloat16), out_3), 1, "returned_core_early")
    late = swap(late[:, 1].astype(jnp.bfloat16), 1, "returned_core_late")

    returned = jnp.zeros((4, tokens, width), jnp.bfloat16)
    for i, arrived in enumerate((early[0], early[1], late[0], late[1])):
        returned = lax.dynamic_update_slice_in_dim(returned, add(totals[i], arrived)[None], relatives[i], 0)
    moe_input_grad = returned[0].astype(jnp.float32)
    for relative in (1, 2, 3):
        moe_input_grad = moe_input_grad + swap(returned[relative], 2 * relative, "returned_plane").astype(jnp.float32)

    gradient = [
        jnp.where(middle, at_middle, at_end).astype(jnp.float32) + sum(part.astype(jnp.float32) for part in arrived)
        for at_middle, at_end, arrived in (
            (to_near[:cut], to_end[:cut], (far_0, far_1_middle_0[rows - cut :], near[:cut])),
            (to_near[cut:], to_end[cut:], (far_1, middle_1, near[cut:])),
        )
    ]
    query_weight_next = row_update(query_weight, jnp.concatenate(gradient, axis=0))
    return (query_weight_next, moe_input_grad)


def solution(mesh):
    placed = (
        P("dp", None),
        P("dp", "expert"),
        P(("expert", "dp"), None),
        P("expert", "dp"),
        P("expert", None),
        P("expert", None),
        P("dp", "expert", None),
        P("dp", "expert", None),
        P("expert", "dp", None),
        P("expert", "dp", None),
        P("expert", None, "dp"),
    )
    return jax.shard_map(
        shards,
        mesh=mesh,
        in_specs=placed,
        out_specs=(P(("expert", "dp"), None), P("expert", "dp")),
        check_vma=False,
    )
```

```python
import jax
import jax.numpy as jnp
from jax import lax
from jax.sharding import PartitionSpec as P

step_rate = 0.01
epsilon = 1e-06

ends_in = [(0, 1), (3, 2)]
across = [(1, 2), (2, 1)]
ends_out = [(1, 0), (2, 3)]


class Line:
    def __init__(self):
        self.last = {}

    def hop(self, value, pairs, name, *first):
        key = tuple(pairs)
        first += (self.last[key],) if key in self.last else ()
        value = after(value, *first) if first else value
        with jax.named_scope(name):
            self.last[key] = lax.ppermute(value, "dp", pairs)
        return self.last[key]


def swap(value, bits, name):
    with jax.named_scope(name):
        return lax.ppermute(value, "expert", [(i, i ^ bits) for i in range(8)])


def after(value, *others):
    return lax.optimization_barrier((value,) + others)[0]


def pick(stack, index):
    return lax.dynamic_index_in_dim(stack, index, 0, keepdims=False)


def line_places():
    low = lax.axis_index("dp") < 2
    return [jnp.where(low, a, b) for a, b in ((0, 3), (1, 2), (2, 1), (3, 0))]


def on_middle():
    z = lax.axis_index("dp")
    return (z == 1) | (z == 2)


def activation_grads(hidden, gate_vals, up_vals):
    gate_float = gate_vals.astype(jnp.float32)
    up_float = up_vals.astype(jnp.float32)
    sigmoid_vals = jax.nn.sigmoid(gate_float)
    gate_grad = hidden * up_float * sigmoid_vals * (1.0 + gate_float * (1.0 - sigmoid_vals))
    up_grad = hidden * gate_float * sigmoid_vals
    return jnp.stack([gate_grad, up_grad], axis=0).astype(jnp.bfloat16)


def row_update(query_weight, gradient):
    radial = jnp.mean(query_weight * gradient, axis=1, keepdims=True) / (
        jnp.mean(query_weight * query_weight, axis=1, keepdims=True) + epsilon
    )
    stepped = query_weight - step_rate * (gradient - radial * query_weight)
    return stepped * lax.rsqrt(jnp.mean(stepped * stepped, axis=1, keepdims=True) + epsilon)


def three_terms(value):
    first = lax.reduce_precision(value, 8, 7)
    second = lax.reduce_precision(value - first, 8, 7)
    return first, second, value - first - second


def token_product(grads, inputs):
    return lax.dot_general(grads, inputs, (((0,), (0,)), ((), ())), preferred_element_type=jnp.float32)


def expert_tables(ids, weights, local, capacity):
    first = lax.axis_index("expert") * local
    experts = first + lax.broadcasted_iota(jnp.int32, (local, 1, 1), 0)
    hit = ids[..., None, :, :] == experts
    chosen = jnp.any(hit, axis=-2)
    token_weight = jnp.sum(jnp.where(hit, weights[..., None, :, :], 0.0), axis=-2)
    token = lax.broadcasted_iota(jnp.int32, (chosen.shape[-1],) * 2, 0)
    earlier = token < lax.broadcasted_iota(jnp.int32, token.shape, 1)
    position = jnp.dot(
        chosen.astype(jnp.bfloat16), earlier.astype(jnp.bfloat16), preferred_element_type=jnp.float32
    ).astype(jnp.int32)
    slot = jnp.where(chosen, position, -1)
    matched = slot[..., None, :] == lax.broadcasted_iota(jnp.int32, (capacity, 1), 0)
    slot_weight = jnp.sum(jnp.where(matched, token_weight[..., None, :], 0.0), axis=-1)
    return matched.astype(jnp.bfloat16), slot_weight


def slot_product(grads, gate_weight, up_weight):
    total = jnp.einsum("sh,ch->sc", grads[0], gate_weight, preferred_element_type=jnp.float32)
    total = total + jnp.einsum("sh,ch->sc", grads[1], up_weight, preferred_element_type=jnp.float32)
    return total.astype(jnp.bfloat16)


def general_weight_update(attn_input, query_grad, query_weight):
    gradient = lax.psum_scatter(
        token_product(query_grad, attn_input).astype(jnp.bfloat16), "dp", scatter_dimension=0, tiled=True
    ).astype(jnp.float32)
    return row_update(query_weight, gradient)


def general_expert_update(
    moe_cotangent, expert_ids, route_weights, gate_saved, up_saved, gate_weight, up_weight, down_weight
):
    groups = lax.axis_size("expert")
    local = gate_weight.shape[0]
    capacity = gate_saved.shape[0] * lax.axis_size("dp") // groups
    tokens, width = moe_cotangent.shape
    rows = lax.all_gather(moe_cotangent, "expert", axis=0, tiled=False)
    routing = jnp.stack([expert_ids.T.astype(jnp.float32), route_weights.T])
    routing = lax.all_gather(routing, "expert", axis=0, tiled=False)
    select, slot_weight = expert_tables(routing[:, 0].astype(jnp.int32), routing[:, 1], local, capacity)
    arrived = jnp.einsum("gect,gtd->egcd", select, rows, preferred_element_type=jnp.float32)
    arrived = (arrived * jnp.swapaxes(slot_weight, 0, 1)[..., None]).astype(jnp.bfloat16)
    total = 0.0
    for expert in range(local):
        flat = arrived[expert].reshape(groups * capacity, width)
        parts = jnp.einsum("sd,hd->sh", flat, down_weight[expert], preferred_element_type=jnp.float32)
        hidden = lax.psum_scatter(
            parts.astype(jnp.bfloat16), "dp", scatter_dimension=0, tiled=True
        ).astype(jnp.float32)
        grads = activation_grads(hidden, gate_saved[:, expert], up_saved[:, expert])
        grads = lax.all_gather(grads, "dp", axis=1, tiled=True)
        slot_input = slot_product(grads, gate_weight[expert], up_weight[expert])
        total = total + jnp.einsum(
            "gct,gcd->gtd",
            select[:, expert],
            slot_input.reshape(groups, capacity, width),
            preferred_element_type=jnp.float32,
        )
    return lax.psum_scatter(
        total.astype(jnp.bfloat16), "expert", scatter_dimension=0, tiled=False
    ).astype(jnp.float32)


def general(
    attn_input, query_grad, query_weight, moe_cotangent, expert_ids, route_weights,
    gate_saved, up_saved, gate_weight, up_weight, down_weight,
):
    moe_input_grad = general_expert_update(
        moe_cotangent, expert_ids, route_weights, gate_saved, up_saved, gate_weight, up_weight, down_weight
    )
    return general_weight_update(attn_input, query_grad, query_weight), moe_input_grad


def line_sources():
    own_end, own_middle, other_middle, other_end = line_places()
    middle = on_middle()
    return (
        jnp.where(middle, other_middle, own_middle),
        jnp.where(middle, own_end, other_middle),
        other_end,
    )


def shards(
    attn_input, query_grad, query_weight, moe_cotangent, expert_ids, route_weights,
    gate_saved, up_saved, gate_weight, up_weight, down_weight,
):
    if (lax.axis_size("expert"), lax.axis_size("dp")) != (8, 4):
        return general(
            attn_input, query_grad, query_weight, moe_cotangent, expert_ids, route_weights,
            gate_saved, up_saved, gate_weight, up_weight, down_weight,
        )
    z = lax.axis_index("dp")
    place = lax.axis_index("expert")
    chip, core = place // 2, place % 2
    own_end, own_middle, other_middle, other_end = line_places()
    middle = on_middle()
    local, width, hidden_units = gate_weight.shape
    tokens, top = expert_ids.shape
    per_dp = gate_saved.shape[0]
    capacity = per_dp // 2
    rows = query_weight.shape[0]
    half = rows // 2
    line = Line()

    routing = [expert_ids.astype(jnp.float32)] + list(three_terms(route_weights))
    tables = jnp.stack([value.T for value in routing]).astype(jnp.bfloat16)
    tables = jnp.stack([tables, swap(tables, 2, "routing_x")])
    own_tokens = after(moe_cotangent, tables)
    pieces = jnp.stack([own_tokens] + [swap(own_tokens, bits, "tokens_plane") for bits in (2, 4, 6)])
    tables = jnp.concatenate([tables, swap(tables, 4, "routing_y")])
    routed = tables
    tables = jnp.stack([tables, swap(tables, 1, "routing_core")], axis=1).astype(jnp.float32)

    def product(places, *first):
        grads = [lax.dynamic_slice_in_dim(query_grad, index * rows + at * half, half, 1) for index, at in places]
        grads = jnp.concatenate(grads, axis=1)
        return token_product(after(grads, *first) if first else grads, attn_input).astype(jnp.bfloat16)

    def add(a, b):
        return (a.astype(jnp.float32) + b.astype(jnp.float32)).astype(jnp.bfloat16)

    to_far_0 = product([(other_end, 0)], routed)
    far_0 = line.hop(to_far_0, ends_in, "rows_far_in_0")

    cotangents = (pieces, swap(pieces, 1, "tokens_core"))
    weights = tables[:, :, 1] + tables[:, :, 2] + tables[:, :, 3]
    select, slot_weight = expert_tables(tables[:, :, 0].astype(jnp.int32), weights, local, capacity)
    parts = []
    for expert in range(local):
        arrived = jnp.stack(
            [
                jnp.einsum(
                    "gct,gtd->gcd", select[:, i, expert], cotangents[i], preferred_element_type=jnp.float32
                )
                * slot_weight[:, i, expert, :, None]
                for i in range(2)
            ],
            axis=1,
        ).astype(jnp.bfloat16)
        part = jnp.einsum(
            "sd,hd->sh",
            arrived.reshape(4 * per_dp, width),
            down_weight[expert],
            preferred_element_type=jnp.float32,
        )
        parts.append(part.astype(jnp.bfloat16).reshape(4, per_dp, hidden_units))

    def block(index):
        return jnp.stack([pick(part, index ^ chip) for part in parts])

    def saved(array):
        blocks = jnp.swapaxes(array, 0, 1).reshape(local, 2, capacity, hidden_units)
        return jnp.where(core == 0, blocks, blocks[:, ::-1]).reshape(local, per_dp, hidden_units)

    far_0 = line.last[tuple(ends_in)] = after(far_0, *parts)
    to_end = product([(own_end, 0), (own_end, 1)], far_0)
    sum_far = line.hop(block(other_end), ends_in, "sum_far_in")
    far_0 = line.hop(add(to_far_0, far_0), across, "rows_far_across_0")
    saved_pair = [saved(after(array, far_0)) for array in (gate_saved, up_saved)]
    to_far_1_middle_0 = product([(other_end, 1), (other_middle, 0)], sum_far)
    sum_middle = line.hop(block(other_middle), ends_in, "sum_middle_in")
    sum_far = line.hop(add(block(other_end), sum_far), across, "sum_far_across")
    far_0 = line.hop(add(to_end[:half], far_0), ends_out, "rows_far_out_0")
    to_middle_1_near_0 = product([(other_middle, 1), (own_middle, 0)], sum_far)
    sum_near = line.hop(block(own_middle), ends_in, "sum_near_in")
    sum_middle = line.hop(add(block(other_middle), sum_middle), across, "sum_middle_across")
    sum_far = line.hop(add(block(own_end), sum_far), ends_out, "sum_far_out")
    to_near_1 = product([(own_middle, 1)], sum_near)
    hidden = block(z).astype(jnp.float32) + sum_far.astype(jnp.float32)
    hidden = hidden + sum_middle.astype(jnp.float32) + sum_near.astype(jnp.float32)
    grads = activation_grads(hidden, *saved_pair)

    sources = (z,) + line_sources()
    relatives = [source ^ chip for source in sources]

    def units(values, places):
        values = jnp.concatenate(values, axis=2)
        chosen = jnp.stack([pick(select, index) for index in places])
        total = 0.0
        for expert in range(local):
            slot_input = slot_product(values[:, expert], gate_weight[expert], up_weight[expert])
            total = total + jnp.einsum(
                "ugct,ugcd->ugtd",
                chosen[:, :, expert],
                slot_input.reshape(2, 2, capacity, width),
                preferred_element_type=jnp.float32,
            )
        return total

    out_1 = line.hop(grads, ends_out, "grads_out_1", to_far_1_middle_0, to_middle_1_near_0)
    cross_1 = line.hop(grads, across, "grads_across_1")
    inward = line.hop(grads, ends_in, "grads_in")
    out_2 = line.hop(cross_1, ends_out, "grads_out_2")
    cross_2 = line.hop(inward, across, "grads_across_2")
    far_1_middle_0_in = line.hop(to_far_1_middle_0, ends_in, "rows_far_1_middle_0_in")
    early = units((grads, jnp.where(middle, cross_1, out_1)), relatives[:2])
    out_3 = line.hop(cross_2, ends_out, "grads_out_3", early)
    far_1_middle_0 = line.hop(
        add(to_far_1_middle_0, far_1_middle_0_in), across, "rows_far_1_middle_0_across"
    )
    middle_1_near_0 = line.hop(to_middle_1_near_0, ends_in, "rows_middle_1_near_0_in")
    far_1 = line.hop(add(to_end[half:], far_1_middle_0[:half]), ends_out, "rows_far_out_1")
    middle_1 = line.hop(
        add(to_middle_1_near_0[:half], middle_1_near_0[:half]), across, "rows_middle_across_1"
    )
    near_1 = line.hop(to_near_1, ends_in, "rows_near_in_1")
    late = units((jnp.where(middle, inward, out_2), jnp.where(middle, cross_2, out_3)), relatives[2:])
    totals = jnp.concatenate([early[:, 0], late[:, 0]])
    early = swap(after(early[:, 1].astype(jnp.bfloat16), out_3), 1, "returned_core_early")
    late = swap(late[:, 1].astype(jnp.bfloat16), 1, "returned_core_late")

    returned = jnp.zeros((4, tokens, width), jnp.bfloat16)
    for i, arrived in enumerate((early[0], early[1], late[0], late[1])):
        returned = lax.dynamic_update_slice_in_dim(returned, add(totals[i], arrived)[None], relatives[i], 0)
    moe_input_grad = returned[0].astype(jnp.float32)
    for relative in (1, 2, 3):
        moe_input_grad = moe_input_grad + swap(returned[relative], 2 * relative, "returned_plane").astype(jnp.float32)

    gradient = [
        jnp.where(middle, at_middle, at_end).astype(jnp.float32) + sum(part.astype(jnp.float32) for part in arrived)
        for at_middle, at_end, arrived in (
            (to_middle_1_near_0[half:], to_end[:half], (far_0, far_1_middle_0[half:], middle_1_near_0[half:])),
            (to_near_1, to_end[half:], (far_1, middle_1, near_1)),
        )
    ]
    query_weight_next = row_update(query_weight, jnp.concatenate(gradient, axis=0))
    return (query_weight_next, moe_input_grad)


def solution(mesh):
    placed = (
        P("dp", None),
        P("dp", "expert"),
        P(("expert", "dp"), None),
        P("expert", "dp"),
        P("expert", None),
        P("expert", None),
        P("dp", "expert", None),
        P("dp", "expert", None),
        P("expert", "dp", None),
        P("expert", "dp", None),
        P("expert", None, "dp"),
    )
    return jax.shard_map(
        shards,
        mesh=mesh,
        in_specs=placed,
        out_specs=(P(("expert", "dp"), None), P("expert", "dp")),
        check_vma=False,
    )
```

```python
import jax
import jax.numpy as jnp
from jax import lax
from jax.sharding import PartitionSpec as P

step_rate = 0.01
epsilon = 1e-06

ends_in = [(0, 1), (3, 2)]
across = [(1, 2), (2, 1)]
ends_out = [(1, 0), (2, 3)]


class Line:
    def __init__(self):
        self.last = {}

    def hop(self, value, pairs, name, *first):
        key = tuple(pairs)
        first += (self.last[key],) if key in self.last else ()
        value = after(value, *first) if first else value
        with jax.named_scope(name):
            self.last[key] = lax.ppermute(value, "dp", pairs)
        return self.last[key]


def swap(value, bits, name):
    with jax.named_scope(name):
        return lax.ppermute(value, "expert", [(i, i ^ bits) for i in range(8)])


def after(value, *others):
    return lax.optimization_barrier((value,) + others)[0]


def pick(stack, index):
    return lax.dynamic_index_in_dim(stack, index, 0, keepdims=False)


def line_places():
    low = lax.axis_index("dp") < 2
    return [jnp.where(low, a, b) for a, b in ((0, 3), (1, 2), (2, 1), (3, 0))]


def on_middle():
    z = lax.axis_index("dp")
    return (z == 1) | (z == 2)


def activation_grads(hidden, gate_vals, up_vals):
    gate_float = gate_vals.astype(jnp.float32)
    up_float = up_vals.astype(jnp.float32)
    sigmoid_vals = jax.nn.sigmoid(gate_float)
    gate_grad = hidden * up_float * sigmoid_vals * (1.0 + gate_float * (1.0 - sigmoid_vals))
    up_grad = hidden * gate_float * sigmoid_vals
    return jnp.stack([gate_grad, up_grad], axis=0).astype(jnp.bfloat16)


def row_update(query_weight, gradient):
    radial = jnp.mean(query_weight * gradient, axis=1, keepdims=True) / (
        jnp.mean(query_weight * query_weight, axis=1, keepdims=True) + epsilon
    )
    stepped = query_weight - step_rate * (gradient - radial * query_weight)
    return stepped * lax.rsqrt(jnp.mean(stepped * stepped, axis=1, keepdims=True) + epsilon)


def three_terms(value):
    first = lax.reduce_precision(value, 8, 7)
    second = lax.reduce_precision(value - first, 8, 7)
    return first, second, value - first - second


def token_product(grads, inputs):
    return lax.dot_general(grads, inputs, (((0,), (0,)), ((), ())), preferred_element_type=jnp.float32)


def expert_tables(ids, weights, local, capacity):
    first = lax.axis_index("expert") * local
    experts = first + lax.broadcasted_iota(jnp.int32, (local, 1, 1), 0)
    hit = ids[..., None, :, :] == experts
    chosen = jnp.any(hit, axis=-2)
    token_weight = jnp.sum(jnp.where(hit, weights[..., None, :, :], 0.0), axis=-2)
    token = lax.broadcasted_iota(jnp.int32, (chosen.shape[-1],) * 2, 0)
    earlier = token < lax.broadcasted_iota(jnp.int32, token.shape, 1)
    position = jnp.dot(
        chosen.astype(jnp.bfloat16), earlier.astype(jnp.bfloat16), preferred_element_type=jnp.float32
    ).astype(jnp.int32)
    slot = jnp.where(chosen, position, -1)
    matched = slot[..., None, :] == lax.broadcasted_iota(jnp.int32, (capacity, 1), 0)
    slot_weight = jnp.sum(jnp.where(matched, token_weight[..., None, :], 0.0), axis=-1)
    return matched.astype(jnp.bfloat16), slot_weight


def slot_product(grads, gate_weight, up_weight):
    total = jnp.einsum("sh,ch->sc", grads[0], gate_weight, preferred_element_type=jnp.float32)
    total = total + jnp.einsum("sh,ch->sc", grads[1], up_weight, preferred_element_type=jnp.float32)
    return total.astype(jnp.bfloat16)


def general_weight_update(attn_input, query_grad, query_weight):
    gradient = lax.psum_scatter(
        token_product(query_grad, attn_input).astype(jnp.bfloat16), "dp", scatter_dimension=0, tiled=True
    ).astype(jnp.float32)
    return row_update(query_weight, gradient)


def general_expert_update(
    moe_cotangent, expert_ids, route_weights, gate_saved, up_saved, gate_weight, up_weight, down_weight
):
    groups = lax.axis_size("expert")
    local = gate_weight.shape[0]
    capacity = gate_saved.shape[0] * lax.axis_size("dp") // groups
    tokens, width = moe_cotangent.shape
    rows = lax.all_gather(moe_cotangent, "expert", axis=0, tiled=False)
    routing = jnp.stack([expert_ids.T.astype(jnp.float32), route_weights.T])
    routing = lax.all_gather(routing, "expert", axis=0, tiled=False)
    select, slot_weight = expert_tables(routing[:, 0].astype(jnp.int32), routing[:, 1], local, capacity)
    arrived = jnp.einsum("gect,gtd->egcd", select, rows, preferred_element_type=jnp.float32)
    arrived = (arrived * jnp.swapaxes(slot_weight, 0, 1)[..., None]).astype(jnp.bfloat16)
    total = 0.0
    for expert in range(local):
        flat = arrived[expert].reshape(groups * capacity, width)
        parts = jnp.einsum("sd,hd->sh", flat, down_weight[expert], preferred_element_type=jnp.float32)
        hidden = lax.psum_scatter(
            parts.astype(jnp.bfloat16), "dp", scatter_dimension=0, tiled=True
        ).astype(jnp.float32)
        grads = activation_grads(hidden, gate_saved[:, expert], up_saved[:, expert])
        grads = lax.all_gather(grads, "dp", axis=1, tiled=True)
        slot_input = slot_product(grads, gate_weight[expert], up_weight[expert])
        total = total + jnp.einsum(
            "gct,gcd->gtd",
            select[:, expert],
            slot_input.reshape(groups, capacity, width),
            preferred_element_type=jnp.float32,
        )
    return lax.psum_scatter(
        total.astype(jnp.bfloat16), "expert", scatter_dimension=0, tiled=False
    ).astype(jnp.float32)


def general(
    attn_input, query_grad, query_weight, moe_cotangent, expert_ids, route_weights,
    gate_saved, up_saved, gate_weight, up_weight, down_weight,
):
    moe_input_grad = general_expert_update(
        moe_cotangent, expert_ids, route_weights, gate_saved, up_saved, gate_weight, up_weight, down_weight
    )
    return general_weight_update(attn_input, query_grad, query_weight), moe_input_grad


def line_sources():
    own_end, own_middle, other_middle, other_end = line_places()
    middle = on_middle()
    return (
        jnp.where(middle, other_middle, own_middle),
        jnp.where(middle, own_end, other_middle),
        other_end,
    )


def shards(
    attn_input, query_grad, query_weight, moe_cotangent, expert_ids, route_weights,
    gate_saved, up_saved, gate_weight, up_weight, down_weight,
):
    if (lax.axis_size("expert"), lax.axis_size("dp")) != (8, 4):
        return general(
            attn_input, query_grad, query_weight, moe_cotangent, expert_ids, route_weights,
            gate_saved, up_saved, gate_weight, up_weight, down_weight,
        )
    z = lax.axis_index("dp")
    place = lax.axis_index("expert")
    chip, core = place // 2, place % 2
    own_end, own_middle, other_middle, other_end = line_places()
    middle = on_middle()
    local, width, hidden_units = gate_weight.shape
    tokens, top = expert_ids.shape
    per_dp = gate_saved.shape[0]
    capacity = per_dp // 2
    rows = query_weight.shape[0]
    half = rows // 2
    line = Line()

    pieces = jnp.stack([moe_cotangent] + [swap(moe_cotangent, bits, "tokens_plane") for bits in (2, 4, 6)])
    routing = [expert_ids.astype(jnp.float32)] + list(three_terms(route_weights))
    tables = jnp.stack([value.T for value in routing]).astype(jnp.bfloat16)
    tables = jnp.stack([tables, swap(tables, 2, "routing_x")])
    routed = tables
    tables = jnp.concatenate([tables, swap(tables, 4, "routing_y")])
    tables = jnp.stack([tables, swap(tables, 1, "routing_core")], axis=1).astype(jnp.float32)

    def product(places, *first):
        grads = [lax.dynamic_slice_in_dim(query_grad, index * rows + at * half, half, 1) for index, at in places]
        grads = jnp.concatenate(grads, axis=1)
        return token_product(after(grads, *first) if first else grads, attn_input).astype(jnp.bfloat16)

    def add(a, b):
        return (a.astype(jnp.float32) + b.astype(jnp.float32)).astype(jnp.bfloat16)

    to_far_0 = product([(other_end, 0)], routed)
    far_0 = line.hop(to_far_0, ends_in, "rows_far_in_0")

    cotangents = (pieces, swap(pieces, 1, "tokens_core"))
    weights = tables[:, :, 1] + tables[:, :, 2] + tables[:, :, 3]
    select, slot_weight = expert_tables(tables[:, :, 0].astype(jnp.int32), weights, local, capacity)
    parts = []
    for expert in range(local):
        arrived = jnp.stack(
            [
                jnp.einsum(
                    "gct,gtd->gcd", select[:, i, expert], cotangents[i], preferred_element_type=jnp.float32
                )
                * slot_weight[:, i, expert, :, None]
                for i in range(2)
            ],
            axis=1,
        ).astype(jnp.bfloat16)
        part = jnp.einsum(
            "sd,hd->sh",
            arrived.reshape(4 * per_dp, width),
            down_weight[expert],
            preferred_element_type=jnp.float32,
        )
        parts.append(part.astype(jnp.bfloat16).reshape(4, per_dp, hidden_units))

    def block(index):
        return jnp.stack([pick(part, index ^ chip) for part in parts])

    def saved(array):
        blocks = jnp.swapaxes(array, 0, 1).reshape(local, 2, capacity, hidden_units)
        return jnp.where(core == 0, blocks, blocks[:, ::-1]).reshape(local, per_dp, hidden_units)

    to_end = product([(own_end, 0), (own_end, 1)], far_0)
    sum_far = line.hop(block(other_end), ends_in, "sum_far_in")
    far_0 = line.hop(add(to_far_0, far_0), across, "rows_far_across_0")
    saved_pair = [saved(after(array, far_0)) for array in (gate_saved, up_saved)]
    to_far_1_middle_0 = product([(other_end, 1), (other_middle, 0)], sum_far)
    sum_middle = line.hop(block(other_middle), ends_in, "sum_middle_in")
    sum_far = line.hop(add(block(other_end), sum_far), across, "sum_far_across")
    far_0 = line.hop(add(to_end[:half], far_0), ends_out, "rows_far_out_0")
    to_middle_1_near_0 = product([(other_middle, 1), (own_middle, 0)], sum_far)
    sum_near = line.hop(block(own_middle), ends_in, "sum_near_in")
    sum_middle = line.hop(add(block(other_middle), sum_middle), across, "sum_middle_across")
    sum_far = line.hop(add(block(own_end), sum_far), ends_out, "sum_far_out")
    to_near_1 = product([(own_middle, 1)], sum_near)
    hidden = block(z).astype(jnp.float32) + sum_far.astype(jnp.float32)
    hidden = hidden + sum_middle.astype(jnp.float32) + sum_near.astype(jnp.float32)
    grads = activation_grads(hidden, *saved_pair)

    sources = (z,) + line_sources()
    relatives = [source ^ chip for source in sources]

    def units(values, places):
        values = jnp.concatenate(values, axis=2)
        chosen = jnp.stack([pick(select, index) for index in places])
        total = 0.0
        for expert in range(local):
            slot_input = slot_product(values[:, expert], gate_weight[expert], up_weight[expert])
            total = total + jnp.einsum(
                "ugct,ugcd->ugtd",
                chosen[:, :, expert],
                slot_input.reshape(2, 2, capacity, width),
                preferred_element_type=jnp.float32,
            )
        return total

    out_1 = line.hop(grads, ends_out, "grads_out_1", to_far_1_middle_0, to_middle_1_near_0)
    cross_1 = line.hop(grads, across, "grads_across_1")
    inward = line.hop(grads, ends_in, "grads_in")
    out_2 = line.hop(cross_1, ends_out, "grads_out_2")
    cross_2 = line.hop(inward, across, "grads_across_2")
    far_1_middle_0_in = line.hop(to_far_1_middle_0, ends_in, "rows_far_1_middle_0_in")
    early = units((grads, jnp.where(middle, cross_1, out_1)), relatives[:2])
    out_3 = line.hop(cross_2, ends_out, "grads_out_3", early)
    far_1_middle_0 = line.hop(
        add(to_far_1_middle_0, far_1_middle_0_in), across, "rows_far_1_middle_0_across"
    )
    middle_1_near_0 = line.hop(to_middle_1_near_0, ends_in, "rows_middle_1_near_0_in")
    far_1 = line.hop(add(to_end[half:], far_1_middle_0[:half]), ends_out, "rows_far_out_1")
    middle_1 = line.hop(
        add(to_middle_1_near_0[:half], middle_1_near_0[:half]), across, "rows_middle_across_1"
    )
    near_1 = line.hop(to_near_1, ends_in, "rows_near_in_1")
    late = units((jnp.where(middle, inward, out_2), jnp.where(middle, cross_2, out_3)), relatives[2:])
    totals = jnp.concatenate([early[:, 0], late[:, 0]])
    early = swap(after(early[:, 1].astype(jnp.bfloat16), out_3), 1, "returned_core_early")
    late = swap(late[:, 1].astype(jnp.bfloat16), 1, "returned_core_late")

    blocks = [add(totals[i], arrived) for i, arrived in enumerate((early[0], early[1], late[0], late[1]))]

    def returned(relative):
        value = blocks[3]
        for i in range(3):
            value = jnp.where(relatives[i] == relative, blocks[i], value)
        return value

    moe_input_grad = returned(0).astype(jnp.float32)
    for relative in (1, 2, 3):
        moe_input_grad = moe_input_grad + swap(returned(relative), 2 * relative, "returned_plane").astype(jnp.float32)

    gradient = [
        jnp.where(middle, at_middle, at_end).astype(jnp.float32) + sum(part.astype(jnp.float32) for part in arrived)
        for at_middle, at_end, arrived in (
            (to_middle_1_near_0[half:], to_end[:half], (far_0, far_1_middle_0[half:], middle_1_near_0[half:])),
            (to_near_1, to_end[half:], (far_1, middle_1, near_1)),
        )
    ]
    query_weight_next = row_update(query_weight, jnp.concatenate(gradient, axis=0))
    return (query_weight_next, moe_input_grad)


def solution(mesh):
    placed = (
        P("dp", None),
        P("dp", "expert"),
        P(("expert", "dp"), None),
        P("expert", "dp"),
        P("expert", None),
        P("expert", None),
        P("dp", "expert", None),
        P("dp", "expert", None),
        P("expert", "dp", None),
        P("expert", "dp", None),
        P("expert", None, "dp"),
    )
    return jax.shard_map(
        shards,
        mesh=mesh,
        in_specs=placed,
        out_specs=(P(("expert", "dp"), None), P("expert", "dp")),
        check_vma=False,
    )
```
